32 devices in a mesh: groups: 2 (over x), dom: 16 (over z, y, core).
Axes of the slice: x: 2, y: 2, z: 4, core: 2. Of those that a mesh axis runs over, the one named last changes fastest.
Arguments:
- features: bfloat16 [65536, 256], P(('groups', 'dom')), parts along dimension 0, may hold values from -6 to 6
- cotangent: bfloat16 [65536, 256], P(('groups', 'dom')), parts along dimension 0, may hold values from -6 to 6
- w_fine: bfloat16 [4, 256, 256], replicated, may hold values from -0.375 to 0.375
- w_coarse: bfloat16 [4, 256, 256], replicated, may hold values from -0.375 to 0.375
- bias: float32 [2, 256], replicated, may hold values from -3 to 3
- fine_src: int32 [131072], P('dom'), may hold values from 0 to 2559
- fine_dst: int32 [131072], P('dom'), may hold values from 0 to 127
- send_left: int32 [4096], P('dom'), may hold values from 0 to 2047
- send_right: int32 [4096], P('dom'), may hold values from 0 to 2047
- pool_map: int32 [32768], P('dom'), may hold values from 0 to 511, as said below
- coarse_src: int32 [32768], P('dom'), may hold values from 0 to 1023
- coarse_dst: int32 [32768], P('dom'), may hold values from 0 to 127
- coarse_send: int32 [256, 32], P('dom'), may hold values from 0 to 511
Outputs:
- grad_input: float32 [65536, 256], P(('groups', 'dom')), parts along dimension 0
- grad_fine: float32 [8, 256, 256], P('groups'), parts along dimension 0
- grad_coarse: float32 [8, 256, 256], P('groups'), parts along dimension 0
- grad_bias: float32 [4, 256], P('groups'), parts along dimension 0
The draws below stay inside these ranges and needn't reach their ends.
There are 2 independent parts, one for each index of `groups`. The reference program is written for one: setup_inputs(seed, part) draws one part's arguments, and reference() takes and returns one part's arrays. A program takes and returns all parts, laid end to end along the dimension named above; an argument that names none is the same for every part. Nothing has to cross between parts.
Inputs may be any that keep to these rules, and one draw needn't show every extreme that they name: `fine_src`: rows below 2048 are the partition's own nodes, then 256 rows from the lower neighbour, then 256 from the upper one. `pool_map`: every coarse index of 0 to 511 is the image of at least one fine node of each partition. `coarse_src`: rows below 512 are the partition's own coarse nodes, then 32 rows from each partition in order.
All inputs are finite; a program needn't handle non-finite values.
Results may differ from the reference program's by a relative error of at most 0.012.
The reference program's roundings to bfloat16 on the way count: a program that leaves them out, or rounds other values in their place, can miss the bound.
Values may be sent and summed in bfloat16 or wider, within the bound.
No kernel may reach another device: no remote copies, remote signals or barrier semaphores. Data moves between devices by JAX's collectives and lax.ppermute only.
A program may use at most 128 MiB of HBM per device.

```python
from functools import partial
import jax
import jax.numpy as jnp
from jax import lax

LATENT = 256
TILE = 128
EDGE_TILE = 512
NODES_DEV = 2048
COARSE_DEV = 512
HALO = 256
CSEND = 32
E_DEV = 8192
CE_DEV = 2048
NODES = 32768
GRAD_DIV = 128
N_DOM = 16


def draw_pool_map(key, part):
    parts = NODES // NODES_DEV

    def one_partition(sub):
        first, second = jax.random.split(sub)
        extra = jax.random.randint(first, (NODES_DEV - COARSE_DEV,), 0, COARSE_DEV).astype(jnp.int32)
        full = jnp.concatenate([jnp.arange(COARSE_DEV, dtype=jnp.int32), extra])
        return jax.random.permutation(second, full)
    keys = jax.random.split(jax.random.fold_in(key, 17), parts)
    return jax.vmap(one_partition)(keys).reshape(-1).astype(jnp.int32)


def plant(entries, stream_key, least, top_value):
    dims = entries.shape
    index_at = [jax.random.randint(jax.random.fold_in(stream_key, axis), (), 0, dims[axis]) for axis in range(len(dims))]
    entries = entries.at[tuple(index_at)].set(least)
    longest = dims.index(max(dims))
    index_at[longest] = (index_at[longest] + 1) % dims[longest]
    return entries.at[tuple(index_at)].set(top_value)


def levels(stream_key, dims, shards, smallest, top_value):
    def one(position, shards_of):
        steps = jax.random.uniform(jax.random.fold_in(jax.random.fold_in(stream_key, 6), position), (shards_of,), jnp.float32, smallest / len(shards), top_value / len(shards))
        return jnp.repeat(jnp.exp(steps), dims[position] // shards_of).reshape((-1,) + (1,) * (len(dims) - position - 1))

    loudness = one(*shards[0])
    for cut in shards[1:]:
        loudness = loudness * one(*cut)
    return loudness


def normal_values(rng, extent, deviation, reach, shards=(), kind=jnp.bfloat16):
    result = jax.random.normal(rng, extent, jnp.float32) * deviation
    if len(shards) > 0:
        result = levels(rng, extent, shards, -0.22, 0.18) * result
    return jnp.clip(result, min=-reach, max=reach).astype(kind)


def setup_inputs(seed: int = 0, part: int = 0) -> dict:
    arg_keys = jax.random.split(jax.random.key(seed), 14)
    part_splits = jax.random.split(jax.random.fold_in(arg_keys[13], part), 14)
    return {
        "features": normal_values(part_splits[0], (NODES, LATENT), 1.0, 6.0, ((0, 16),)),
        "cotangent": normal_values(part_splits[1], (NODES, LATENT), 1.0, 6.0, ((0, 16),)),
        "w_fine": normal_values(arg_keys[2], (4, LATENT, LATENT), LATENT ** -0.5, 0.375),
        "w_coarse": normal_values(arg_keys[3], (4, LATENT, LATENT), LATENT ** -0.5, 0.375),
        "bias": normal_values(arg_keys[4], (2, LATENT), 0.5, 3.0, (), jnp.float32),
        "fine_src": plant(jax.random.randint(arg_keys[5], (N_DOM * E_DEV,), 0, NODES_DEV + 2 * HALO), jax.random.fold_in(arg_keys[5], 1), 0, (NODES_DEV + 2 * HALO) - 1).astype(jnp.int32),
        "fine_dst": plant(jax.random.randint(arg_keys[6], (N_DOM * E_DEV,), 0, TILE), jax.random.fold_in(arg_keys[6], 1), 0, TILE - 1).astype(jnp.int32),
        "send_left": plant(jax.random.randint(arg_keys[7], (N_DOM * HALO,), 0, NODES_DEV), jax.random.fold_in(arg_keys[7], 1), 0, NODES_DEV - 1).astype(jnp.int32),
        "send_right": plant(jax.random.randint(arg_keys[8], (N_DOM * HALO,), 0, NODES_DEV), jax.random.fold_in(arg_keys[8], 1), 0, NODES_DEV - 1).astype(jnp.int32),
        "pool_map": draw_pool_map(jax.random.fold_in(arg_keys[13], 71), part),
        "coarse_src": plant(jax.random.randint(arg_keys[10], (N_DOM * CE_DEV,), 0, 2 * COARSE_DEV), jax.random.fold_in(arg_keys[10], 1), 0, (2 * COARSE_DEV) - 1).astype(jnp.int32),
        "coarse_dst": plant(jax.random.randint(arg_keys[11], (N_DOM * CE_DEV,), 0, TILE), jax.random.fold_in(arg_keys[11], 1), 0, TILE - 1).astype(jnp.int32),
        "coarse_send": plant(jax.random.randint(arg_keys[12], (N_DOM * N_DOM, CSEND), 0, COARSE_DEV), jax.random.fold_in(arg_keys[12], 1), 0, COARSE_DEV - 1).astype(jnp.int32),
    }


def silu_grad(value):
    sig = jax.nn.sigmoid(value)
    return sig * (1.0 + value * (1.0 - sig))

def tile_onehot(dst):
    tiles = dst.reshape(-1, EDGE_TILE)
    return (tiles[:, :, None] == jnp.arange(TILE, dtype=jnp.int32)[None, None, :]).astype(jnp.bfloat16)

def project(hidden, weights):
    send_proj = jnp.dot(hidden, weights[0], preferred_element_type=jnp.float32).astype(jnp.bfloat16)
    recv_proj = jnp.dot(hidden, weights[1], preferred_element_type=jnp.float32).astype(jnp.bfloat16)
    return (send_proj, recv_proj)

def edge_update(hidden, extended, recv_proj, onehot, src, weights, edge_bias):
    tiles = onehot.shape[0]
    latent = hidden.shape[1]
    gathered = extended[src].astype(jnp.float32)
    recv_tiles = recv_proj.reshape(tiles, TILE, latent).astype(jnp.float32)
    at_edges = jnp.einsum('tej,tjl->tel', onehot.astype(jnp.float32), recv_tiles).reshape(-1, latent)
    zvals = gathered + at_edges + edge_bias[None, :]
    message = jax.nn.silu(zvals).astype(jnp.bfloat16)
    summed = jnp.einsum('tej,tel->tjl', onehot.astype(jnp.float32), message.astype(jnp.float32).reshape(tiles, EDGE_TILE, latent))
    aggregate = summed.reshape(-1, latent).astype(jnp.bfloat16)
    update = jnp.dot(hidden, weights[3], preferred_element_type=jnp.float32) + jnp.dot(aggregate, weights[2], preferred_element_type=jnp.float32)
    newer = (hidden.astype(jnp.float32) + jax.nn.silu(update)).astype(jnp.bfloat16)
    return (newer, zvals, aggregate, update)

def edge_back(rows_ext, grad_new, hidden, zvals, aggregate, update, onehot, src, weights):
    tiles = onehot.shape[0]
    latent = hidden.shape[1]
    grad_u = (grad_new * silu_grad(update)).astype(jnp.bfloat16)
    grad_w3 = jnp.dot(hidden.T, grad_u, preferred_element_type=jnp.float32)
    grad_w2 = jnp.dot(aggregate.T, grad_u, preferred_element_type=jnp.float32)
    grad_h = grad_new + jnp.dot(grad_u, weights[3].T, preferred_element_type=jnp.float32)
    grad_agg = jnp.dot(grad_u, weights[2].T, preferred_element_type=jnp.float32).astype(jnp.bfloat16)
    hot32 = onehot.astype(jnp.float32)
    grad_msg = jnp.einsum('tej,tjl->tel', hot32, grad_agg.astype(jnp.float32).reshape(tiles, TILE, latent)).reshape(-1, latent)
    grad_z = (grad_msg * silu_grad(zvals)).astype(jnp.bfloat16)
    grad_b = lax.optimization_barrier(jnp.sum(grad_z.astype(jnp.float32), axis=0))
    grad_q = jnp.einsum('tej,tel->tjl', hot32, grad_z.astype(jnp.float32).reshape(tiles, EDGE_TILE, latent)).reshape(-1, latent).astype(jnp.bfloat16)
    grad_ext = jax.ops.segment_sum(grad_z.astype(jnp.float32), src, num_segments=rows_ext).astype(jnp.bfloat16)
    return (grad_h, grad_ext, grad_q, grad_w3, grad_w2, grad_b)

def front_back(grad_h, hidden, grad_p, grad_q, weights):
    grad_h = grad_h + jnp.dot(grad_p, weights[0].T, preferred_element_type=jnp.float32) + jnp.dot(grad_q, weights[1].T, preferred_element_type=jnp.float32)
    grad_w0 = jnp.dot(hidden.T, grad_p, preferred_element_type=jnp.float32)
    grad_w1 = jnp.dot(hidden.T, grad_q, preferred_element_type=jnp.float32)
    return (grad_h, grad_w0, grad_w1)

def take_rows(table, index):
    return table[index]

def add_rows(local_part, arrivals, index):
    latent = local_part.shape[-1]
    total = jnp.zeros(local_part.shape, jnp.float32).at[index.reshape(-1)].add(arrivals.reshape(-1, latent).astype(jnp.float32))
    return (total + local_part.astype(jnp.float32)).astype(jnp.bfloat16)

def pool_tables(mapping):
    onehot = (mapping[None, :] == jnp.arange(COARSE_DEV, dtype=jnp.int32)[:, None]).astype(jnp.bfloat16)
    counts = lax.optimization_barrier(jnp.sum(onehot.astype(jnp.float32), axis=1))
    return (onehot, counts)

def pool_rows(onehot, counts, hidden):
    return (jnp.dot(onehot, hidden, preferred_element_type=jnp.float32) / counts[:, None]).astype(jnp.bfloat16)

def reference(features, cotangent, w_fine, w_coarse, bias, fine_src, fine_dst, send_left, send_right, pool_map, coarse_src, coarse_dst, coarse_send):
    parts = N_DOM
    latent = LATENT
    inputs = features.reshape(parts, NODES_DEV, latent)
    cot = cotangent.reshape(parts, NODES_DEV, latent)
    fsrc = fine_src.reshape(parts, E_DEV)
    csrc = coarse_src.reshape(parts, CE_DEV)
    fine_hot = jax.vmap(tile_onehot)(fine_dst.reshape(parts, E_DEV))
    coarse_hot = jax.vmap(tile_onehot)(coarse_dst.reshape(parts, CE_DEV))
    lefts = send_left.reshape(parts, HALO)
    rights = send_right.reshape(parts, HALO)
    csend = coarse_send.reshape(parts, parts, CSEND)
    fine_ext_rows = NODES_DEV + 2 * HALO
    coarse_ext_rows = COARSE_DEV + parts * CSEND
    send_f, recv_f = jax.vmap(project, (0, None))(inputs, w_fine)
    to_right = jax.vmap(take_rows)(send_f, rights)
    to_left = jax.vmap(take_rows)(send_f, lefts)
    zero = jnp.zeros((1, HALO, latent), jnp.bfloat16)
    from_left = jnp.concatenate([zero, to_right[:-1]], axis=0)
    from_right = jnp.concatenate([to_left[1:], zero], axis=0)
    fine_ext = jnp.concatenate([send_f, from_left, from_right], axis=1)
    level_f = jax.vmap(edge_update, (0, 0, 0, 0, 0, None, None))
    h_one, z_one, agg_one, u_one = level_f(inputs, fine_ext, recv_f, fine_hot, fsrc, w_fine, bias[0])
    pool_hot, counts = jax.vmap(pool_tables)(pool_map.reshape(parts, NODES_DEV))
    pooled = jax.vmap(pool_rows)(pool_hot, counts, h_one)
    send_c, recv_c = jax.vmap(project, (0, None))(pooled, w_coarse)
    outgoing = jax.vmap(take_rows)(send_c, csend)
    incoming = outgoing.transpose(1, 0, 2, 3).reshape(parts, parts * CSEND, latent)
    coarse_ext = jnp.concatenate([send_c, incoming], axis=1)
    level_c = jax.vmap(edge_update, (0, 0, 0, 0, 0, None, None))
    h_c, z_c, agg_c, u_c = level_c(pooled, coarse_ext, recv_c, coarse_hot, csrc, w_coarse, bias[1])
    grad_hc = jax.vmap(lambda hot, g: jnp.dot(hot, g, preferred_element_type=jnp.float32))(pool_hot, cot)
    back_c = jax.vmap(partial(edge_back, coarse_ext_rows), (0, 0, 0, 0, 0, 0, 0, None))
    grad_c, gext_c, gq_c, gw3_c, gw2_c, gb_c = back_c(grad_hc, pooled, z_c, agg_c, u_c, coarse_hot, csrc, w_coarse)
    returned = gext_c[:, COARSE_DEV:].reshape(parts, parts, CSEND, latent).transpose(1, 0, 2, 3)
    gp_c = jax.vmap(add_rows)(gext_c[:, :COARSE_DEV], returned, csend)
    grad_c, gw0_c, gw1_c = jax.vmap(front_back, (0, 0, 0, 0, None))(grad_c, pooled, gp_c, gq_c, w_coarse)
    scaled = (grad_c / counts[:, :, None]).astype(jnp.bfloat16)
    grad_h1 = cot.astype(jnp.float32) + jax.vmap(lambda hot, g: jnp.dot(hot.T, g, preferred_element_type=jnp.float32))(pool_hot, scaled)
    back_f = jax.vmap(partial(edge_back, fine_ext_rows), (0, 0, 0, 0, 0, 0, 0, None))
    grad_f, gext_f, gq_f, gw3_f, gw2_f, gb_f = back_f(grad_h1, inputs, z_one, agg_one, u_one, fine_hot, fsrc, w_fine)
    got_left = gext_f[:, NODES_DEV:NODES_DEV + HALO]
    got_right = gext_f[:, NODES_DEV + HALO:]
    for_right = jnp.concatenate([got_left[1:], zero], axis=0)
    for_left = jnp.concatenate([zero, got_right[:-1]], axis=0)
    gp_f = jax.vmap(add_rows)(gext_f[:, :NODES_DEV], jnp.concatenate([for_right, for_left], axis=1), jnp.concatenate([rights, lefts], axis=1))
    grad_f, gw0_f, gw1_f = jax.vmap(front_back, (0, 0, 0, 0, None))(grad_f, inputs, gp_f, gq_f, w_fine)
    divisor = float(GRAD_DIV)
    grad_fine = jnp.stack([lax.optimization_barrier(jnp.sum(gw0_f, 0)), lax.optimization_barrier(jnp.sum(gw1_f, 0)), lax.optimization_barrier(jnp.sum(gw2_f, 0)), lax.optimization_barrier(jnp.sum(gw3_f, 0))]) / divisor
    grad_coarse = jnp.stack([lax.optimization_barrier(jnp.sum(gw0_c, 0)), lax.optimization_barrier(jnp.sum(gw1_c, 0)), lax.optimization_barrier(jnp.sum(gw2_c, 0)), lax.optimization_barrier(jnp.sum(gw3_c, 0))]) / divisor
    grad_bias = jnp.stack([lax.optimization_barrier(jnp.sum(gb_f, 0)), lax.optimization_barrier(jnp.sum(gb_c, 0))]) / divisor
    return (grad_f.reshape(NODES, latent), grad_fine, grad_coarse, grad_bias)
```

```python
import functools

import jax
import jax.numpy as jnp
from jax import lax
from jax.experimental import pallas as pl
from jax.experimental.pallas import tpu as pltpu
from jax.sharding import PartitionSpec as P

bf = jnp.bfloat16
f32 = jnp.float32
TILE = 128
LANES = 128


def mm(a, b):
    return jnp.dot(a, b, preferred_element_type=f32)


def mm_tn(a, b):
    return lax.dot_general(a, b, (((0,), (0,)), ((), ())), preferred_element_type=f32)


def mm_nt(a, b):
    return lax.dot_general(a, b, (((1,), (1,)), ((), ())), preferred_element_type=f32)


def as_bf(x):
    return x.astype(f32).astype(bf)


def row_form(ref, first, count):
    return jnp.concatenate([ref[pl.ds(first + j, 1), :] for j in range(count)], axis=1)


def hot_rows(row, rows):
    cols = row.shape[1]
    if rows <= 256:
        io = as_bf(lax.broadcasted_iota(jnp.int32, (rows, cols), 0))
        return jnp.where(io == as_bf(row), bf(1), bf(0))
    low = as_bf(row & 255)
    high = as_bf(lax.shift_right_arithmetic(row, 8))
    io = as_bf(lax.broadcasted_iota(jnp.int32, (256, cols), 0))
    base = jnp.where(io == low, bf(1), bf(0))
    return jnp.concatenate(
        [jnp.where(high == bf(k), base, bf(0)) for k in range(rows // 256)], axis=0
    )


def silu_parts(v):
    sig = jax.nn.sigmoid(v)
    return v * sig, sig * (1.0 + v * (1.0 - sig))


def call(kernel, outs, args, grid=(), specs=None, out_specs=None, scratch=(), cost=(0, 0)):
    def whole(a):
        return pl.BlockSpec(a.shape, lambda *_: (0,) * len(a.shape))

    in_specs = [whole(a) for a in args]
    o_specs = [whole(o) for o in outs]
    for k, s in (specs or {}).items():
        in_specs[k] = s
    for k, s in (out_specs or {}).items():
        o_specs[k] = s
    return pl.pallas_call(
        kernel,
        grid=grid or (1,),
        in_specs=in_specs,
        out_specs=o_specs,
        out_shape=outs,
        scratch_shapes=list(scratch),
        compiler_params=pltpu.CompilerParams(vmem_limit_bytes=56 << 20),
        cost_estimate=pl.CostEstimate(
            flops=int(cost[0]), bytes_accessed=int(cost[1]), transcendentals=0
        ),
    )(*args)


def sds(shape, dtype):
    return jax.ShapeDtypeStruct(shape, dtype)


def halo_kernel(h_ref, right_ref, left_ref, to_right_ref, to_left_ref):
    h = h_ref[...]
    n = right_ref.shape[0]
    to_right_ref[...] = mm_tn(hot_rows(row_form(right_ref, 0, n), h.shape[0]), h).astype(bf)
    to_left_ref[...] = mm_tn(hot_rows(row_form(left_ref, 0, n), h.shape[0]), h).astype(bf)


def own_kernel(per, h_ref, w_ref, b_ref, src_ref, dst_ref, z_ref, p_ref, q_ref):
    t = pl.program_id(0)

    @pl.when(t == 0)
    def _():
        h = h_ref[...]
        p_ref[...] = mm(h, w_ref[0]).astype(bf)
        q_ref[...] = mm(h, w_ref[1]).astype(bf)

    src = row_form(src_ref, t * per, per)
    dst = row_form(dst_ref, t * per, per)
    qt = q_ref[pl.ds(pl.multiple_of(t * TILE, TILE), TILE), :]
    z_ref[...] = (
        mm_tn(hot_rows(src, p_ref.shape[0]), p_ref[...])
        + mm_tn(hot_rows(dst, TILE), qt)
        + b_ref[0:1, :]
    )


def fine_kernel(
    per, tiles, z_ref, left_ref, right_ref, h_ref, w_ref, src_ref, dst_ref, pool_ref, send_ref,
    d_ref, agg_ref, dsu_ref, pooled_ref, out_ref, count_ref, halo_p,
):
    t = pl.program_id(0)
    nodes = h_ref.shape[0]
    halo = left_ref.shape[0]

    @pl.when(t == 0)
    def _():
        halo_p[0:halo, :] = mm(left_ref[...], w_ref[0]).astype(bf)
        halo_p[halo : 2 * halo, :] = mm(right_ref[...], w_ref[0]).astype(bf)

    src = row_form(src_ref, t * per, per) - nodes
    dst = row_form(dst_ref, t * per, per)
    z = z_ref[...] + mm_tn(hot_rows(src, 2 * halo), halo_p[...])
    m, d = silu_parts(z)
    d_ref[...] = d.astype(bf)
    rows = pl.ds(pl.multiple_of(t * TILE, TILE), TILE)
    agg_ref[rows, :] = mm(hot_rows(dst, TILE), m.astype(bf)).astype(bf)

    @pl.when(t == tiles - 1)
    def _():
        h = h_ref[...]
        u = mm(h, w_ref[3]) + mm(agg_ref[...], w_ref[2])
        su, dsu = silu_parts(u)
        dsu_ref[...] = dsu.astype(bf)
        h1 = (h.astype(f32) + su).astype(bf)
        coarse = pooled_ref.shape[0]
        hot = hot_rows(row_form(pool_ref, 0, pool_ref.shape[0]), coarse)
        count = mm(hot, jnp.ones((nodes, LANES), bf))
        count_ref[...] = count
        pooled = (mm(hot, h1) / jnp.concatenate([count, count], axis=1)).astype(bf)
        pooled_ref[...] = pooled
        sends = hot_rows(row_form(send_ref, 0, send_ref.shape[0]), coarse)
        out_ref[...] = mm_tn(sends, pooled).astype(bf)


def coarse_own_kernel(
    per, pooled_ref, w_ref, b_ref, src_ref, dst_ref, pool_ref, cot_ref, z_ref, ghc_ref, u_ref
):
    pooled = pooled_ref[...]
    coarse = pooled.shape[0]
    proj = mm(pooled, w_ref[0]).astype(bf)
    recv = mm(pooled, w_ref[1]).astype(bf)
    u_ref[...] = mm(pooled, w_ref[3])
    edges = per * LANES
    for t in range(coarse // TILE):
        src = row_form(src_ref, t * per, per)
        dst = row_form(dst_ref, t * per, per)
        z_ref[t * edges : (t + 1) * edges, :] = (
            mm_tn(hot_rows(src, coarse), proj)
            + mm_tn(hot_rows(dst, TILE), recv[t * TILE : (t + 1) * TILE, :])
            + b_ref[1:2, :]
        )
    hot = hot_rows(row_form(pool_ref, 0, pool_ref.shape[0]), coarse)
    ghc_ref[...] = mm(hot, cot_ref[...])


def coarse_kernel(
    per, z_ref, in_ref, ghc_ref, u_ref, w_ref, src_ref, dst_ref,
    own_ref, back_ref, dz_ref, du_ref, agg_ref, deriv,
):
    coarse = ghc_ref.shape[0]
    edges = per * LANES
    tiles = coarse // TILE
    proj = mm(in_ref[...], w_ref[0]).astype(bf)
    for t in range(tiles):
        src = row_form(src_ref, t * per, per) - coarse
        dst = row_form(dst_ref, t * per, per)
        z = z_ref[t * edges : (t + 1) * edges, :] + mm_tn(hot_rows(src, proj.shape[0]), proj)
        m, d = silu_parts(z)
        deriv[t * edges : (t + 1) * edges, :] = d
        agg_ref[t * TILE : (t + 1) * TILE, :] = mm(hot_rows(dst, TILE), m.astype(bf)).astype(bf)
    u = u_ref[...] + mm(agg_ref[...], w_ref[2])
    _, dsu = silu_parts(u)
    du = (ghc_ref[...] * dsu).astype(bf)
    du_ref[...] = du
    dagg = mm_nt(du, w_ref[2]).astype(bf)
    total = None
    for t in range(tiles):
        src = row_form(src_ref, t * per, per)
        dst = row_form(dst_ref, t * per, per)
        gm = mm_tn(hot_rows(dst, TILE), dagg[t * TILE : (t + 1) * TILE, :])
        dz = (gm * deriv[t * edges : (t + 1) * edges, :]).astype(bf)
        dz_ref[t * edges : (t + 1) * edges, :] = dz
        part = mm(hot_rows(src, coarse + proj.shape[0]), dz)
        total = part if total is None else total + part
    own_ref[...] = total[:coarse].astype(bf)
    back_ref[...] = total[coarse:].astype(bf)


def coarse_grad_kernel(
    per, pooled_ref, in_ref, ghc_ref, w_ref, dst_ref, own_ref, back_ref, dz_ref, du_ref, agg_ref,
    gw_ref, gb_ref, part_ref,
):
    pooled = pooled_ref[...]
    coarse, width = pooled.shape
    edges = per * LANES
    dqs = []
    gb = jnp.zeros((1, width), f32)
    for t in range(coarse // TILE):
        dst = row_form(dst_ref, t * per, per)
        dq = mm(hot_rows(dst, TILE), dz_ref[t * edges : (t + 1) * edges, :])
        gb = gb + jnp.sum(dq, axis=0, keepdims=True)
        dqs.append(dq.astype(bf))
    dq = jnp.concatenate(dqs, axis=0)
    du = du_ref[...]
    gb_ref[...] = jnp.broadcast_to(gb, gb_ref.shape)
    gw_ref[0:width, :] = (mm_tn(pooled, own_ref[...]) + mm_tn(in_ref[...], back_ref[...])).astype(bf)
    gw_ref[width : 2 * width, :] = mm_tn(pooled, dq).astype(bf)
    gw_ref[2 * width : 3 * width, :] = mm_tn(agg_ref[...], du).astype(bf)
    gw_ref[3 * width : 4 * width, :] = mm_tn(pooled, du).astype(bf)
    part_ref[...] = ghc_ref[...] + mm_nt(du, w_ref[3]) + mm_nt(dq, w_ref[1])


def node_back_kernel(
    own_ref, ret_ref, send_ref, part_ref, wc_ref, count_ref, pool_ref, cot_ref, dsu_ref, w_ref,
    g_ref, du_ref, dagg_ref,
):
    coarse = own_ref.shape[0]
    sends = hot_rows(row_form(send_ref, 0, send_ref.shape[0]), coarse)
    dp = (own_ref[...].astype(f32) + mm(sends, ret_ref[...])).astype(bf)
    dc = part_ref[...] + mm_nt(dp, wc_ref[0])
    count = count_ref[...]
    dcs = (dc / jnp.concatenate([count, count], axis=1)).astype(bf)
    hot = hot_rows(row_form(pool_ref, 0, pool_ref.shape[0]), coarse)
    g = cot_ref[...].astype(f32) + mm_tn(hot, dcs)
    g_ref[...] = g
    du = (g * dsu_ref[...].astype(f32)).astype(bf)
    du_ref[...] = du
    dagg_ref[...] = mm_nt(du, w_ref[2]).astype(bf)


def edge_back_kernel(
    per, tiles, d_ref, dagg_ref, h_ref, left_ref, right_ref, src_ref, dst_ref,
    own_ref, gl_ref, gr_ref, dq_ref, gw_ref, gb_ref, acc,
):
    t = pl.program_id(0)
    nodes = h_ref.shape[0]
    halo = left_ref.shape[0]

    @pl.when(t == 0)
    def _():
        acc[...] = jnp.zeros_like(acc)
        gb_ref[...] = jnp.zeros_like(gb_ref)

    src = row_form(src_ref, t * per, per)
    dst = row_form(dst_ref, t * per, per)
    hot = hot_rows(dst, TILE)
    rows = pl.ds(pl.multiple_of(t * TILE, TILE), TILE)
    gm = mm_tn(hot, dagg_ref[rows, :])
    dz = (gm * d_ref[...].astype(f32)).astype(bf)
    dq = mm(hot, dz)
    gb_ref[...] += jnp.sum(dq, axis=0, keepdims=True)
    dq_ref[rows, :] = dq.astype(bf)
    acc[...] += mm(hot_rows(src, acc.shape[0]), dz)

    @pl.when(t == tiles - 1)
    def _():
        own = acc[0:nodes, :].astype(bf)
        gl = acc[nodes : nodes + halo, :].astype(bf)
        gr = acc[nodes + halo : nodes + 2 * halo, :].astype(bf)
        own_ref[...] = own
        gl_ref[...] = gl
        gr_ref[...] = gr
        gw_ref[...] = (
            mm_tn(h_ref[...], own) + mm_tn(left_ref[...], gl) + mm_tn(right_ref[...], gr)
        ).astype(bf)


def fine_grad_kernel(h_ref, dq_ref, du_ref, agg_ref, g_ref, w_ref, gw_ref, part_ref):
    h = h_ref[...]
    width = h.shape[1]
    dq = dq_ref[...]
    du = du_ref[...]
    gw_ref[0:width, :] = mm_tn(h, dq).astype(bf)
    gw_ref[width : 2 * width, :] = mm_tn(agg_ref[...], du).astype(bf)
    gw_ref[2 * width : 3 * width, :] = mm_tn(h, du).astype(bf)
    part_ref[...] = g_ref[...] + mm_nt(du, w_ref[3]) + mm_nt(dq, w_ref[1])


def input_kernel(own_ref, from_right_ref, from_left_ref, right_ref, left_ref, part_ref, w_ref, o_ref):
    nodes = own_ref.shape[0]
    n = right_ref.shape[0]
    add = mm(hot_rows(row_form(right_ref, 0, n), nodes), from_right_ref[...]) + mm(
        hot_rows(row_form(left_ref, 0, n), nodes), from_left_ref[...]
    )
    dp = (own_ref[...].astype(f32) + add).astype(bf)
    o_ref[...] = part_ref[...] + mm_nt(dp, w_ref[0])


def shifted(block, axis, distance):
    devices = range(lax.axis_size(axis))
    route = [(i - distance, i) for i in devices if i - distance in devices]
    return lax.ppermute(block, axis, route)


def exchange(block, parts):
    rows, width = block.shape
    got = lax.all_to_all(
        block.reshape(parts, rows // parts, width), "dom", split_axis=0, concat_axis=0, tiled=True
    )
    return got


def reduced(block, parts):
    rows, width = block.shape
    mine = jnp.sum(exchange(block, parts).astype(f32), axis=0).astype(bf)
    spread = jnp.broadcast_to(mine[None], (parts,) + mine.shape)
    full = lax.all_to_all(spread, "dom", split_axis=0, concat_axis=0, tiled=True)
    return full.reshape(rows, width)


def shards(
    features, cotangent, w_fine, w_coarse, bias, fine_src, fine_dst, send_left, send_right,
    pool_map, coarse_src, coarse_dst, coarse_send,
):
    nodes, width = features.shape
    parts = lax.axis_size("dom")
    coarse = nodes // 4
    tiles = nodes // TILE
    halo = send_left.shape[0]
    per = fine_src.shape[0] // tiles // LANES
    edges = per * LANES
    fsrc, fdst = fine_src.reshape(-1, LANES), fine_dst.reshape(-1, LANES)
    csrc, cdst = coarse_src.reshape(-1, LANES), coarse_dst.reshape(-1, LANES)
    right, left = send_right.reshape(-1, LANES), send_left.reshape(-1, LANES)
    pool = pool_map.reshape(-1, LANES)
    csend = coarse_send.reshape(-1, LANES)
    crows = coarse_send.shape[0] * coarse_send.shape[1]
    part = functools.partial

    to_right, to_left = call(
        halo_kernel, [sds((halo, width), bf)] * 2, [features, right, left]
    )
    h_left = shifted(to_right, "dom", 1)
    h_right = shifted(to_left, "dom", -1)
    edge_tile = pl.BlockSpec((edges, width), lambda t: (t, 0))
    (z_own,) = call(
        part(own_kernel, per),
        [sds((tiles * edges, width), f32)],
        [features, w_fine, bias, fsrc, fdst],
        grid=(tiles,),
        out_specs={0: edge_tile},
        scratch=[pltpu.VMEM((nodes, width), bf)] * 2,
        cost=(9e9, 10e6),
    )
    d_edge, agg, dsu, pooled, outgoing, count = call(
        part(fine_kernel, per, tiles),
        [
            sds((tiles * edges, width), bf),
            sds((nodes, width), bf),
            sds((nodes, width), bf),
            sds((coarse, width), bf),
            sds((crows, width), bf),
            sds((coarse, LANES), f32),
        ],
        [z_own, h_left, h_right, features, w_fine, fsrc, fdst, pool, csend],
        grid=(tiles,),
        specs={0: edge_tile},
        out_specs={0: edge_tile},
        scratch=[pltpu.VMEM((2 * halo, width), bf)],
    )
    incoming = exchange(outgoing, parts).reshape(crows, width)
    cedges = coarse_src.shape[0]
    zc, ghc, uc = call(
        part(coarse_own_kernel, per),
        [sds((cedges, width), f32), sds((coarse, width), f32), sds((coarse, width), f32)],
        [pooled, w_coarse, bias, csrc, cdst, pool, cotangent],
        cost=(4e9, 10e6),
    )
    own_c, back_c, dz_c, du_c, agg_c = call(
        part(coarse_kernel, per),
        [
            sds((coarse, width), bf),
            sds((crows, width), bf),
            sds((cedges, width), bf),
            sds((coarse, width), bf),
            sds((coarse, width), bf),
        ],
        [zc, incoming, ghc, uc, w_coarse, csrc, cdst],
        scratch=[pltpu.VMEM((cedges, width), f32)],
    )
    returned = exchange(back_c, parts).reshape(crows, width)
    gw_c, gb_c, part_c = call(
        part(coarse_grad_kernel, per),
        [sds((4 * width, width), bf), sds((8, width), f32), sds((coarse, width), f32)],
        [pooled, incoming, ghc, w_coarse, cdst, own_c, back_c, dz_c, du_c, agg_c],
        cost=(4e9, 10e6),
    )
    g, du, dagg = call(
        node_back_kernel,
        [sds((nodes, width), f32), sds((nodes, width), bf), sds((nodes, width), bf)],
        [own_c, returned, csend, part_c, w_coarse, count, pool, cotangent, dsu, w_fine],
    )
    own_f, gl, gr, dq, gw0, gb_f = call(
        part(edge_back_kernel, per, tiles),
        [
            sds((nodes, width), bf),
            sds((halo, width), bf),
            sds((halo, width), bf),
            sds((nodes, width), bf),
            sds((width, width), bf),
            sds((8, width), f32),
        ],
        [d_edge, dagg, features, h_left, h_right, fsrc, fdst],
        grid=(tiles,),
        specs={0: edge_tile},
        scratch=[pltpu.VMEM((nodes + 2 * halo, width), f32)],
    )
    from_right = shifted(gl, "dom", -1)
    from_left = shifted(gr, "dom", 1)
    gw_rest, part_f = call(
        fine_grad_kernel,
        [sds((3 * width, width), bf), sds((nodes, width), f32)],
        [features, dq, du, agg, g, w_fine],
    )
    (grad_input,) = call(
        input_kernel,
        [sds((nodes, width), f32)],
        [own_f, from_right, from_left, right, left, part_f, w_fine],
    )
    scale = 1.0 / float(nodes * parts // 256)
    total = reduced(jnp.concatenate([gw_c, gw0, gw_rest], axis=0), parts).astype(f32) * scale
    total = total.reshape(8, width, width)
    gb = jnp.stack([gb_f[0], gb_c[0]])
    spread = jnp.broadcast_to(gb[None], (parts,) + gb.shape)
    gbs = lax.all_to_all(spread, "dom", split_axis=0, concat_axis=0, tiled=True)
    grad_bias = jnp.sum(gbs, axis=0) * scale
    return (grad_input, total[4:], total[:4], grad_bias)


def solution(mesh):
    return jax.shard_map(
        shards,
        mesh=mesh,
        in_specs=(
            P(("groups", "dom"), None),
            P(("groups", "dom"), None),
            P(),
            P(),
            P(),
            P("dom"),
            P("dom"),
            P("dom"),
            P("dom"),
            P("dom"),
            P("dom"),
            P("dom"),
            P("dom", None),
        ),
        out_specs=(
            P(("groups", "dom"), None),
            P("groups", None, None),
            P("groups", None, None),
            P("groups", None),
        ),
        check_vma=False,
    )
```

```python
import functools

import jax
import jax.numpy as jnp
from jax import lax
from jax.experimental import pallas as pl
from jax.experimental.pallas import tpu as pltpu
from jax.sharding import PartitionSpec as P

bf = jnp.bfloat16
f32 = jnp.float32
TILE = 128
LANES = 128


def mm(a, b):
    return jnp.dot(a, b, preferred_element_type=f32)


def mm_tn(a, b):
    return lax.dot_general(a, b, (((0,), (0,)), ((), ())), preferred_element_type=f32)


def mm_nt(a, b):
    return lax.dot_general(a, b, (((1,), (1,)), ((), ())), preferred_element_type=f32)


def as_bf(x):
    return x.astype(f32).astype(bf)


def row_form(ref, first, count):
    return jnp.concatenate([ref[pl.ds(first + j, 1), :] for j in range(count)], axis=1)


def hot_rows(row, rows):
    cols = row.shape[1]
    if rows <= 256:
        io = as_bf(lax.broadcasted_iota(jnp.int32, (rows, cols), 0))
        return jnp.where(io == as_bf(row), bf(1), bf(0))
    low = as_bf(row & 255)
    high = as_bf(lax.shift_right_arithmetic(row, 8))
    io = as_bf(lax.broadcasted_iota(jnp.int32, (256, cols), 0))
    base = jnp.where(io == low, bf(1), bf(0))
    return jnp.concatenate(
        [jnp.where(high == bf(k), base, bf(0)) for k in range(rows // 256)], axis=0
    )


def silu_parts(v):
    sig = 0.5 * jnp.tanh(0.5 * v) + 0.5
    silu = v * sig
    return silu, sig + silu * (1.0 - sig)


def to_pairs(ref, first, rows):
    n = rows.shape[0]
    for j in range(2):
        ref[pl.ds(2 * first + j, n, stride=2), :] = rows[:, j * LANES : (j + 1) * LANES]


def from_pairs(ref, first, n):
    return jnp.concatenate([ref[pl.ds(2 * first + j, n, stride=2), :] for j in range(2)], axis=1)


def pair(index):
    return pl.ds(pl.multiple_of(index * 2, 2), 2)


def call(kernel, outs, args, grid=(), specs=None, out_specs=None, scratch=(), cost=(0, 0)):
    def whole(a):
        return pl.BlockSpec(a.shape, lambda *_: (0,) * len(a.shape))

    in_specs = [whole(a) for a in args]
    o_specs = [whole(o) for o in outs]
    for k, s in (specs or {}).items():
        in_specs[k] = s
    for k, s in (out_specs or {}).items():
        o_specs[k] = s
    return pl.pallas_call(
        kernel,
        grid=grid or (1,),
        in_specs=in_specs,
        out_specs=o_specs,
        out_shape=outs,
        scratch_shapes=list(scratch),
        compiler_params=pltpu.CompilerParams(vmem_limit_bytes=56 << 20),
        cost_estimate=pl.CostEstimate(
            flops=int(cost[0]), bytes_accessed=int(cost[1]), transcendentals=0
        ),
    )(*args)


def sds(shape, dtype):
    return jax.ShapeDtypeStruct(shape, dtype)


def halo_kernel(h_ref, right_ref, left_ref, to_right_ref, to_left_ref):
    h = h_ref[...]
    n = right_ref.shape[0]
    to_right_ref[...] = mm_tn(hot_rows(row_form(right_ref, 0, n), h.shape[0]), h).astype(bf)
    to_left_ref[...] = mm_tn(hot_rows(row_form(left_ref, 0, n), h.shape[0]), h).astype(bf)


def project_kernel(h_ref, w_ref, p_ref, q_ref):
    h = h_ref[...]
    p_ref[...] = mm(h, w_ref[0]).astype(bf)
    q_ref[...] = mm(h, w_ref[1]).astype(bf)


def fine_kernel(
    per, tiles, src_ref, p_ref, q_ref, left_ref, right_ref, h_ref, w_ref, b_ref, dst_ref, pool_ref,
    send_ref, d_ref, agg_ref, dsu_ref, pooled_ref, out_ref, count_ref, table, taken,
):
    t = pl.program_id(0)
    nodes = h_ref.shape[0]
    halo = left_ref.shape[0]
    edges = per * LANES

    @pl.when(t == 0)
    def _():
        to_pairs(table, 0, p_ref[...].astype(f32))
        to_pairs(table, nodes, as_bf(mm(left_ref[...], w_ref[0])).astype(f32))
        to_pairs(table, nodes + halo, as_bf(mm(right_ref[...], w_ref[0])).astype(f32))

    for e in range(edges):
        taken[2 * e : 2 * e + 2, :] = table[pair(src_ref[t * edges + e]), :]
    rows = pl.ds(pl.multiple_of(t * TILE, TILE), TILE)
    hot = hot_rows(row_form(dst_ref, t * per, per), TILE)
    z = from_pairs(taken, 0, edges) + mm_tn(hot, q_ref[rows, :]) + b_ref[0:1, :]
    m, d = silu_parts(z)
    d_ref[...] = d.astype(bf)
    agg_ref[rows, :] = mm(hot, m.astype(bf)).astype(bf)

    @pl.when(t == tiles - 1)
    def _():
        h = h_ref[...]
        u = mm(h, w_ref[3]) + mm(agg_ref[...], w_ref[2])
        su, dsu = silu_parts(u)
        dsu_ref[...] = dsu.astype(bf)
        h1 = (h.astype(f32) + su).astype(bf)
        coarse = pooled_ref.shape[0]
        hot = hot_rows(row_form(pool_ref, 0, pool_ref.shape[0]), coarse)
        count = mm(hot, jnp.ones((nodes, LANES), bf))
        count_ref[...] = count
        pooled = (mm(hot, h1) / jnp.concatenate([count, count], axis=1)).astype(bf)
        pooled_ref[...] = pooled
        sends = hot_rows(row_form(send_ref, 0, send_ref.shape[0]), coarse)
        out_ref[...] = mm_tn(sends, pooled).astype(bf)


def coarse_own_kernel(
    per, pooled_ref, w_ref, b_ref, src_ref, dst_ref, pool_ref, cot_ref, z_ref, ghc_ref, u_ref
):
    pooled = pooled_ref[...]
    coarse = pooled.shape[0]
    proj = mm(pooled, w_ref[0]).astype(bf)
    recv = mm(pooled, w_ref[1]).astype(bf)
    u_ref[...] = mm(pooled, w_ref[3])
    edges = per * LANES
    for t in range(coarse // TILE):
        src = row_form(src_ref, t * per, per)
        dst = row_form(dst_ref, t * per, per)
        z_ref[t * edges : (t + 1) * edges, :] = (
            mm_tn(hot_rows(src, coarse), proj)
            + mm_tn(hot_rows(dst, TILE), recv[t * TILE : (t + 1) * TILE, :])
            + b_ref[1:2, :]
        )
    hot = hot_rows(row_form(pool_ref, 0, pool_ref.shape[0]), coarse)
    ghc_ref[...] = mm(hot, cot_ref[...])


def coarse_kernel(
    per, z_ref, in_ref, ghc_ref, u_ref, w_ref, src_ref, dst_ref,
    own_ref, back_ref, dz_ref, du_ref, agg_ref, deriv,
):
    coarse = ghc_ref.shape[0]
    edges = per * LANES
    tiles = coarse // TILE
    proj = mm(in_ref[...], w_ref[0]).astype(bf)
    for t in range(tiles):
        src = row_form(src_ref, t * per, per) - coarse
        dst = row_form(dst_ref, t * per, per)
        z = z_ref[t * edges : (t + 1) * edges, :] + mm_tn(hot_rows(src, proj.shape[0]), proj)
        m, d = silu_parts(z)
        deriv[t * edges : (t + 1) * edges, :] = d
        agg_ref[t * TILE : (t + 1) * TILE, :] = mm(hot_rows(dst, TILE), m.astype(bf)).astype(bf)
    u = u_ref[...] + mm(agg_ref[...], w_ref[2])
    _, dsu = silu_parts(u)
    du = (ghc_ref[...] * dsu).astype(bf)
    du_ref[...] = du
    dagg = mm_nt(du, w_ref[2]).astype(bf)
    total = None
    for t in range(tiles):
        src = row_form(src_ref, t * per, per)
        dst = row_form(dst_ref, t * per, per)
        gm = mm_tn(hot_rows(dst, TILE), dagg[t * TILE : (t + 1) * TILE, :])
        dz = (gm * deriv[t * edges : (t + 1) * edges, :]).astype(bf)
        dz_ref[t * edges : (t + 1) * edges, :] = dz
        part = mm(hot_rows(src, coarse + proj.shape[0]), dz)
        total = part if total is None else total + part
    own_ref[...] = total[:coarse].astype(bf)
    back_ref[...] = total[coarse:].astype(bf)


def coarse_grad_kernel(
    per, pooled_ref, in_ref, ghc_ref, w_ref, dst_ref, own_ref, back_ref, dz_ref, du_ref, agg_ref,
    gw_ref, gb_ref, part_ref,
):
    pooled = pooled_ref[...]
    coarse, width = pooled.shape
    edges = per * LANES
    dqs = []
    gb = jnp.zeros((1, width), f32)
    for t in range(coarse // TILE):
        dst = row_form(dst_ref, t * per, per)
        dq = mm(hot_rows(dst, TILE), dz_ref[t * edges : (t + 1) * edges, :])
        gb = gb + jnp.sum(dq, axis=0, keepdims=True)
        dqs.append(dq.astype(bf))
    dq = jnp.concatenate(dqs, axis=0)
    du = du_ref[...]
    gb_ref[...] = jnp.broadcast_to(gb, gb_ref.shape)
    gw_ref[0:width, :] = (mm_tn(pooled, own_ref[...]) + mm_tn(in_ref[...], back_ref[...])).astype(bf)
    gw_ref[width : 2 * width, :] = mm_tn(pooled, dq).astype(bf)
    gw_ref[2 * width : 3 * width, :] = mm_tn(agg_ref[...], du).astype(bf)
    gw_ref[3 * width : 4 * width, :] = mm_tn(pooled, du).astype(bf)
    part_ref[...] = ghc_ref[...] + mm_nt(du, w_ref[3]) + mm_nt(dq, w_ref[1])


def node_back_kernel(
    own_ref, ret_ref, send_ref, part_ref, wc_ref, count_ref, pool_ref, cot_ref, dsu_ref, w_ref,
    h_ref, agg_ref, g_ref, du_ref, dagg_ref, gw_ref,
):
    coarse = own_ref.shape[0]
    width = h_ref.shape[1]
    sends = hot_rows(row_form(send_ref, 0, send_ref.shape[0]), coarse)
    dp = (own_ref[...].astype(f32) + mm(sends, ret_ref[...])).astype(bf)
    dc = part_ref[...] + mm_nt(dp, wc_ref[0])
    count = count_ref[...]
    dcs = (dc / jnp.concatenate([count, count], axis=1)).astype(bf)
    hot = hot_rows(row_form(pool_ref, 0, pool_ref.shape[0]), coarse)
    g = cot_ref[...].astype(f32) + mm_tn(hot, dcs)
    g_ref[...] = g
    du = (g * dsu_ref[...].astype(f32)).astype(bf)
    du_ref[...] = du
    dagg_ref[...] = mm_nt(du, w_ref[2]).astype(bf)
    gw_ref[0:width, :] = mm_tn(agg_ref[...], du).astype(bf)
    gw_ref[width : 2 * width, :] = mm_tn(h_ref[...], du).astype(bf)


def edge_back_kernel(
    per, tiles, src_ref, d_ref, dagg_ref, h_ref, left_ref, right_ref, dst_ref, gbc_ref,
    own_ref, gl_ref, gr_ref, dq_ref, gw_ref, gb, dzs, *accs,
):
    t = pl.program_id(0)
    nodes, width = h_ref.shape
    halo = left_ref.shape[0]
    edges = per * LANES

    @pl.when(t == 0)
    def _():
        gb[...] = jnp.zeros_like(gb)
        for acc in accs:
            acc[...] = jnp.zeros_like(acc)

    hot = hot_rows(row_form(dst_ref, t * per, per), TILE)
    rows = pl.ds(pl.multiple_of(t * TILE, TILE), TILE)
    gm = mm_tn(hot, dagg_ref[rows, :])
    dz = (gm * d_ref[...].astype(f32)).astype(bf)
    dq = mm(hot, dz)
    gb[...] += jnp.sum(dq, axis=0, keepdims=True)
    dq_ref[rows, :] = dq.astype(bf)
    to_pairs(dzs, 0, dz.astype(f32))
    for e in range(edges):
        acc = accs[e % len(accs)]
        at = pair(src_ref[t * edges + e])
        acc[at, :] = acc[at, :] + dzs[2 * e : 2 * e + 2, :]

    @pl.when(t == tiles - 1)
    def _():
        def summed(first, n):
            total = from_pairs(accs[0], first, n)
            for acc in accs[1:]:
                total = total + from_pairs(acc, first, n)
            return total.astype(bf)

        own = summed(0, nodes)
        gl = summed(nodes, halo)
        gr = summed(nodes + halo, halo)
        own_ref[...] = own
        gl_ref[...] = gl
        gr_ref[...] = gr
        gw_ref[0:width, :] = (
            mm_tn(h_ref[...], own) + mm_tn(left_ref[...], gl) + mm_tn(right_ref[...], gr)
        ).astype(bf)
        gw_ref[width : width + 16, :] = jnp.broadcast_to(gb[0:1, :], (16, width)).astype(bf)
        gw_ref[width + 16 : 2 * width + 16, :] = mm_tn(h_ref[...], dq_ref[...]).astype(bf)
        gw_ref[2 * width + 16 :, :] = jnp.broadcast_to(gbc_ref[0:1, :], (16, width)).astype(bf)


def part_kernel(dq_ref, du_ref, g_ref, w_ref, part_ref):
    part_ref[...] = (
        g_ref[...] + mm_nt(du_ref[...], w_ref[3]) + mm_nt(dq_ref[...], w_ref[1])
    )


def input_kernel(own_ref, from_right_ref, from_left_ref, right_ref, left_ref, part_ref, w_ref, o_ref):
    nodes = own_ref.shape[0]
    n = right_ref.shape[0]
    add = mm(hot_rows(row_form(right_ref, 0, n), nodes), from_right_ref[...]) + mm(
        hot_rows(row_form(left_ref, 0, n), nodes), from_left_ref[...]
    )
    dp = (own_ref[...].astype(f32) + add).astype(bf)
    o_ref[...] = part_ref[...] + mm_nt(dp, w_ref[0])


def finish_kernel(scale, core_ref, a_ref, ax_ref, b_ref, bx_ref, gf_ref, gc_ref, gb_ref):
    width = a_ref.shape[1]

    def write(a0, a1, b0, b1):
        def put(ref, k, src, at):
            ref[k * width : (k + 1) * width, :] = (
                src[at * width : (at + 1) * width, :].astype(f32) * scale
            )

        for k in range(3):
            put(gc_ref, k, a0, k)
        put(gc_ref, 3, a1, 0)
        put(gf_ref, 2, a1, 1)
        put(gf_ref, 3, a1, 2)
        put(gf_ref, 0, b0, 0)
        put(gf_ref, 1, b1, 0)
        gb_ref[0:1, :] = b0[width : width + 1, :].astype(f32) * scale
        gb_ref[1:2, :] = b1[width : width + 1, :].astype(f32) * scale

    core = core_ref[0]

    @pl.when(core == 0)
    def _():
        write(a_ref, ax_ref, b_ref, bx_ref)

    @pl.when(core != 0)
    def _():
        write(ax_ref, a_ref, bx_ref, b_ref)


def shifted(block, axis, distance):
    devices = range(lax.axis_size(axis))
    route = [(i - distance, i) for i in devices if i - distance in devices]
    return lax.ppermute(block, axis, route)


def swapped(block, parts, bit):
    return lax.ppermute(block, "dom", [(i, i ^ bit) for i in range(parts)])


def exchange(block, parts):
    rows, width = block.shape
    got = lax.all_to_all(
        block.reshape(parts, rows // parts, width), "dom", split_axis=0, concat_axis=0, tiled=True
    )
    return got


def halves(block, core):
    two = block.reshape((2, block.shape[0] // 2) + block.shape[1:])
    mine = lax.dynamic_index_in_dim(two, core, 0, keepdims=False)
    other = lax.dynamic_index_in_dim(two, 1 - core, 0, keepdims=False)
    return mine, other


def add(a, b):
    return (a.astype(f32) + b.astype(f32)).astype(bf)


def shards(
    features, cotangent, w_fine, w_coarse, bias, fine_src, fine_dst, send_left, send_right,
    pool_map, coarse_src, coarse_dst, coarse_send,
):
    nodes, width = features.shape
    parts = lax.axis_size("dom")
    coarse = nodes // 4
    tiles = nodes // TILE
    halo = send_left.shape[0]
    per = fine_src.shape[0] // tiles // LANES
    edges = per * LANES
    fsrc, fdst = fine_src.reshape(-1, LANES), fine_dst.reshape(-1, LANES)
    csrc, cdst = coarse_src.reshape(-1, LANES), coarse_dst.reshape(-1, LANES)
    right, left = send_right.reshape(-1, LANES), send_left.reshape(-1, LANES)
    pool = pool_map.reshape(-1, LANES)
    csend = coarse_send.reshape(-1, LANES)
    crows = coarse_send.shape[0] * coarse_send.shape[1]
    part = functools.partial

    to_right, to_left = call(
        halo_kernel, [sds((halo, width), bf)] * 2, [features, right, left]
    )
    h_left = shifted(to_right, "dom", 1)
    h_right = shifted(to_left, "dom", -1)
    edge_tile = pl.BlockSpec((edges, width), lambda t: (t, 0))
    proj, recv = call(
        project_kernel,
        [sds((nodes, width), bf)] * 2,
        [features, w_fine],
        cost=(3e9, 10e6),
    )
    smem = pl.BlockSpec(memory_space=pltpu.SMEM)
    ext_pairs = 2 * (nodes + 2 * halo)
    d_edge, agg, dsu, pooled, outgoing, count = call(
        part(fine_kernel, per, tiles),
        [
            sds((tiles * edges, width), bf),
            sds((nodes, width), bf),
            sds((nodes, width), bf),
            sds((coarse, width), bf),
            sds((crows, width), bf),
            sds((coarse, LANES), f32),
        ],
        [fine_src, proj, recv, h_left, h_right, features, w_fine, bias, fdst, pool, csend],
        grid=(tiles,),
        specs={0: smem},
        out_specs={0: edge_tile},
        scratch=[pltpu.VMEM((ext_pairs, LANES), f32), pltpu.VMEM((2 * edges, LANES), f32)],
    )
    incoming = exchange(outgoing, parts).reshape(crows, width)
    cedges = coarse_src.shape[0]
    zc, ghc, uc = call(
        part(coarse_own_kernel, per),
        [sds((cedges, width), f32), sds((coarse, width), f32), sds((coarse, width), f32)],
        [pooled, w_coarse, bias, csrc, cdst, pool, cotangent],
        cost=(4e9, 10e6),
    )
    own_c, back_c, dz_c, du_c, agg_c = call(
        part(coarse_kernel, per),
        [
            sds((coarse, width), bf),
            sds((crows, width), bf),
            sds((cedges, width), bf),
            sds((coarse, width), bf),
            sds((coarse, width), bf),
        ],
        [zc, incoming, ghc, uc, w_coarse, csrc, cdst],
        scratch=[pltpu.VMEM((cedges, width), f32)],
    )
    returned = exchange(back_c, parts).reshape(crows, width)
    gw_c, gb_c, part_c = call(
        part(coarse_grad_kernel, per),
        [sds((4 * width, width), bf), sds((8, width), f32), sds((coarse, width), f32)],
        [pooled, incoming, ghc, w_coarse, cdst, own_c, back_c, dz_c, du_c, agg_c],
        cost=(4e9, 10e6),
    )
    g, du, dagg, gw_n = call(
        node_back_kernel,
        [
            sds((nodes, width), f32),
            sds((nodes, width), bf),
            sds((nodes, width), bf),
            sds((2 * width, width), bf),
        ],
        [
            own_c, returned, csend, part_c, w_coarse, count, pool, cotangent, dsu, w_fine,
            features, agg,
        ],
    )
    core = lax.axis_index("dom") % 2
    same_core = [list(range(c, parts, 2)) for c in range(2)]
    chips = parts // 2
    mine, other = halves(jnp.concatenate([gw_c, gw_n], axis=0), core)
    early = add(mine, swapped(other, parts, 1))
    early, dagg = lax.optimization_barrier((early, dagg))
    early = lax.all_to_all(
        early.reshape(chips, -1, width), "dom", 0, 0, axis_index_groups=same_core, tiled=True
    )
    own_f, gl, gr, dq, gw_e = call(
        part(edge_back_kernel, per, tiles),
        [
            sds((nodes, width), bf),
            sds((halo, width), bf),
            sds((halo, width), bf),
            sds((nodes, width), bf),
            sds((2 * (width + 16), width), bf),
        ],
        [fine_src, d_edge, dagg, features, h_left, h_right, fdst, gb_c],
        grid=(tiles,),
        specs={0: smem, 1: edge_tile},
        scratch=[pltpu.VMEM((8, width), f32), pltpu.VMEM((2 * edges, LANES), f32)]
        + [pltpu.VMEM((ext_pairs, LANES), f32)] * 8,
        cost=(30e9, 10e6),
    )
    mine, other = halves(gw_e, core)
    late = add(mine, swapped(other, parts, 1))
    early = jnp.sum(early.astype(f32), axis=0).astype(bf)
    early = lax.all_to_all(
        jnp.broadcast_to(early[None], (chips,) + early.shape),
        "dom", 0, 0, axis_index_groups=same_core, tiled=True,
    ).reshape(-1, width)
    bit = 2
    while bit < parts:
        late = add(late, swapped(late, parts, bit))
        bit *= 2
    from_right = shifted(gl, "dom", -1)
    from_left = shifted(gr, "dom", 1)
    (part_f,) = call(
        part_kernel, [sds((nodes, width), f32)], [dq, du, g, w_fine], cost=(4e9, 10e6)
    )
    (grad_input,) = call(
        input_kernel,
        [sds((nodes, width), f32)],
        [own_f, from_right, from_left, right, left, part_f, w_fine],
        cost=(4e9, 10e6),
    )
    scale = 1.0 / float(nodes * parts // 256)
    grad_fine, grad_coarse, grad_bias = call(
        part(finish_kernel, scale),
        [sds((4 * width, width), f32), sds((4 * width, width), f32), sds((2, width), f32)],
        [
            core.astype(jnp.int32).reshape(1), early, swapped(early, parts, 1),
            late, swapped(late, parts, 1),
        ],
        specs={0: smem},
    )
    shape = (4, width, width)
    return (grad_input, grad_fine.reshape(shape), grad_coarse.reshape(shape), grad_bias)


def solution(mesh):
    return jax.shard_map(
        shards,
        mesh=mesh,
        in_specs=(
            P(("groups", "dom"), None),
            P(("groups", "dom"), None),
            P(),
            P(),
            P(),
            P("dom"),
            P("dom"),
            P("dom"),
            P("dom"),
            P("dom"),
            P("dom"),
            P("dom"),
            P("dom", None),
        ),
        out_specs=(
            P(("groups", "dom"), None),
            P("groups", None, None),
            P("groups", None, None),
            P("groups", None),
        ),
        check_vma=False,
    )
```

```python
import functools

import jax
import jax.numpy as jnp
from jax import lax
from jax.experimental import pallas as pl
from jax.experimental.pallas import tpu as pltpu
from jax.sharding import PartitionSpec as P

bf = jnp.bfloat16
f32 = jnp.float32
TILE = 128
LANES = 128


def mm(a, b):
    return jnp.dot(a, b, preferred_element_type=f32)


def mm_tn(a, b):
    return lax.dot_general(a, b, (((0,), (0,)), ((), ())), preferred_element_type=f32)


def mm_nt(a, b):
    return lax.dot_general(a, b, (((1,), (1,)), ((), ())), preferred_element_type=f32)


def as_bf(x):
    return x.astype(f32).astype(bf)


def row_form(ref, first, count):
    return jnp.concatenate([ref[pl.ds(first + j, 1), :] for j in range(count)], axis=1)


def hot_rows(row, rows):
    cols = row.shape[1]
    if rows <= 256:
        io = as_bf(lax.broadcasted_iota(jnp.int32, (rows, cols), 0))
        return jnp.where(io == as_bf(row), bf(1), bf(0))
    low = as_bf(row & 255)
    high = as_bf(lax.shift_right_arithmetic(row, 8))
    io = as_bf(lax.broadcasted_iota(jnp.int32, (256, cols), 0))
    base = jnp.where(io == low, bf(1), bf(0))
    return jnp.concatenate(
        [jnp.where(high == bf(k), base, bf(0)) for k in range(rows // 256)], axis=0
    )


def silu_parts(v):
    sig = 0.5 * jnp.tanh(0.5 * v) + 0.5
    silu = v * sig
    return silu, sig + silu * (1.0 - sig)


def to_pairs(ref, first, rows):
    n = rows.shape[0]
    for j in range(2):
        ref[pl.ds(2 * first + j, n, stride=2), :] = rows[:, j * LANES : (j + 1) * LANES]


def from_pairs(ref, first, n):
    return jnp.concatenate([ref[pl.ds(2 * first + j, n, stride=2), :] for j in range(2)], axis=1)


def pair(index):
    return pl.ds(pl.multiple_of(index * 2, 2), 2)


def call(kernel, outs, args, grid=(), specs=None, out_specs=None, scratch=(), cost=(0, 0)):
    def whole(a):
        return pl.BlockSpec(a.shape, lambda *_: (0,) * len(a.shape))

    in_specs = [whole(a) for a in args]
    o_specs = [whole(o) for o in outs]
    for k, s in (specs or {}).items():
        in_specs[k] = s
    for k, s in (out_specs or {}).items():
        o_specs[k] = s
    return pl.pallas_call(
        kernel,
        grid=grid or (1,),
        in_specs=in_specs,
        out_specs=o_specs,
        out_shape=outs,
        scratch_shapes=list(scratch),
        compiler_params=pltpu.CompilerParams(vmem_limit_bytes=56 << 20),
        cost_estimate=pl.CostEstimate(
            flops=int(cost[0]), bytes_accessed=int(cost[1]), transcendentals=0
        ),
    )(*args)


def sds(shape, dtype):
    return jax.ShapeDtypeStruct(shape, dtype)


def halo_kernel(h_ref, right_ref, left_ref, to_right_ref, to_left_ref):
    h = h_ref[...]
    n = right_ref.shape[0]
    to_right_ref[...] = mm_tn(hot_rows(row_form(right_ref, 0, n), h.shape[0]), h).astype(bf)
    to_left_ref[...] = mm_tn(hot_rows(row_form(left_ref, 0, n), h.shape[0]), h).astype(bf)


def fine_kernel(
    per, tiles, src_ref, left_ref, right_ref, h_ref, w_ref, b_ref, dst_ref, pool_ref, send_ref,
    d_ref, he_ref, agg_ref, dsu_ref, pooled_ref, out_ref, count_ref, recv, table, taken,
):
    t = pl.program_id(0)
    nodes = h_ref.shape[0]
    halo = left_ref.shape[0]
    edges = per * LANES

    @pl.when(t == 0)
    def _():
        recv[...] = mm(h_ref[...], w_ref[1]).astype(bf)
        to_pairs(table, 0, h_ref[...].astype(f32))
        to_pairs(table, nodes, left_ref[...].astype(f32))
        to_pairs(table, nodes + halo, right_ref[...].astype(f32))

    for e in range(edges):
        taken[2 * e : 2 * e + 2, :] = table[pair(src_ref[t * edges + e]), :]
    rows = pl.ds(pl.multiple_of(t * TILE, TILE), TILE)
    hot = hot_rows(row_form(dst_ref, t * per, per), TILE)
    he = from_pairs(taken, 0, edges).astype(bf)
    he_ref[...] = he
    sent = as_bf(mm(he, w_ref[0])).astype(f32)
    z = sent + mm_tn(hot, recv[rows, :]) + b_ref[0:1, :]
    m, d = silu_parts(z)
    d_ref[...] = d.astype(bf)
    agg_ref[rows, :] = mm(hot, m.astype(bf)).astype(bf)

    @pl.when(t == tiles - 1)
    def _():
        h = h_ref[...]
        u = mm(h, w_ref[3]) + mm(agg_ref[...], w_ref[2])
        su, dsu = silu_parts(u)
        dsu_ref[...] = dsu.astype(bf)
        h1 = (h.astype(f32) + su).astype(bf)
        coarse = pooled_ref.shape[0]
        hot = hot_rows(row_form(pool_ref, 0, pool_ref.shape[0]), coarse)
        count = mm(hot, jnp.ones((nodes, LANES), bf))
        count_ref[...] = count
        pooled = (mm(hot, h1) / jnp.concatenate([count, count], axis=1)).astype(bf)
        pooled_ref[...] = pooled
        sends = hot_rows(row_form(send_ref, 0, send_ref.shape[0]), coarse)
        out_ref[...] = mm_tn(sends, pooled).astype(bf)


def coarse_own_kernel(
    per, pooled_ref, w_ref, b_ref, src_ref, dst_ref, pool_ref, cot_ref, z_ref, ghc_ref, u_ref
):
    pooled = pooled_ref[...]
    coarse = pooled.shape[0]
    proj = mm(pooled, w_ref[0]).astype(bf)
    recv = mm(pooled, w_ref[1]).astype(bf)
    u_ref[...] = mm(pooled, w_ref[3])
    edges = per * LANES
    for t in range(coarse // TILE):
        src = row_form(src_ref, t * per, per)
        dst = row_form(dst_ref, t * per, per)
        z_ref[t * edges : (t + 1) * edges, :] = (
            mm_tn(hot_rows(src, coarse), proj)
            + mm_tn(hot_rows(dst, TILE), recv[t * TILE : (t + 1) * TILE, :])
            + b_ref[1:2, :]
        )
    hot = hot_rows(row_form(pool_ref, 0, pool_ref.shape[0]), coarse)
    ghc_ref[...] = mm(hot, cot_ref[...])


def coarse_kernel(
    per, z_ref, in_ref, ghc_ref, u_ref, w_ref, src_ref, dst_ref,
    own_ref, back_ref, dz_ref, du_ref, agg_ref, deriv,
):
    coarse = ghc_ref.shape[0]
    edges = per * LANES
    tiles = coarse // TILE
    proj = mm(in_ref[...], w_ref[0]).astype(bf)
    for t in range(tiles):
        src = row_form(src_ref, t * per, per) - coarse
        dst = row_form(dst_ref, t * per, per)
        z = z_ref[t * edges : (t + 1) * edges, :] + mm_tn(hot_rows(src, proj.shape[0]), proj)
        m, d = silu_parts(z)
        deriv[t * edges : (t + 1) * edges, :] = d
        agg_ref[t * TILE : (t + 1) * TILE, :] = mm(hot_rows(dst, TILE), m.astype(bf)).astype(bf)
    u = u_ref[...] + mm(agg_ref[...], w_ref[2])
    _, dsu = silu_parts(u)
    du = (ghc_ref[...] * dsu).astype(bf)
    du_ref[...] = du
    dagg = mm_nt(du, w_ref[2]).astype(bf)
    total = None
    for t in range(tiles):
        src = row_form(src_ref, t * per, per)
        dst = row_form(dst_ref, t * per, per)
        gm = mm_tn(hot_rows(dst, TILE), dagg[t * TILE : (t + 1) * TILE, :])
        dz = (gm * deriv[t * edges : (t + 1) * edges, :]).astype(bf)
        dz_ref[t * edges : (t + 1) * edges, :] = dz
        part = mm(hot_rows(src, coarse + proj.shape[0]), dz)
        total = part if total is None else total + part
    own_ref[...] = total[:coarse].astype(bf)
    back_ref[...] = total[coarse:].astype(bf)


def coarse_grad_kernel(
    per, pooled_ref, in_ref, ghc_ref, w_ref, dst_ref, own_ref, back_ref, dz_ref, du_ref, agg_ref,
    gw_ref, gb_ref, part_ref,
):
    pooled = pooled_ref[...]
    coarse, width = pooled.shape
    edges = per * LANES
    dqs = []
    gb = jnp.zeros((1, width), f32)
    for t in range(coarse // TILE):
        dst = row_form(dst_ref, t * per, per)
        dq = mm(hot_rows(dst, TILE), dz_ref[t * edges : (t + 1) * edges, :])
        gb = gb + jnp.sum(dq, axis=0, keepdims=True)
        dqs.append(dq.astype(bf))
    dq = jnp.concatenate(dqs, axis=0)
    du = du_ref[...]
    gb_ref[...] = jnp.broadcast_to(gb, gb_ref.shape)
    gw_ref[0:width, :] = (mm_tn(pooled, own_ref[...]) + mm_tn(in_ref[...], back_ref[...])).astype(bf)
    gw_ref[width : 2 * width, :] = mm_tn(pooled, dq).astype(bf)
    gw_ref[2 * width : 3 * width, :] = mm_tn(agg_ref[...], du).astype(bf)
    gw_ref[3 * width : 4 * width, :] = mm_tn(pooled, du).astype(bf)
    part_ref[...] = ghc_ref[...] + mm_nt(du, w_ref[3]) + mm_nt(dq, w_ref[1])


def by_core(core_ref, mine_ref, other_ref, half0, half1):
    core = core_ref[0]

    def write(ref, half):
        at = 0
        for piece in half:
            ref[at : at + piece.shape[0], :] = piece
            at += piece.shape[0]

    @pl.when(core == 0)
    def _():
        write(mine_ref, half0)
        write(other_ref, half1)

    @pl.when(core != 0)
    def _():
        write(mine_ref, half1)
        write(other_ref, half0)


def node_back_kernel(
    core_ref, own_ref, ret_ref, send_ref, part_ref, wc_ref, count_ref, pool_ref, cot_ref, dsu_ref,
    w_ref, h_ref, agg_ref, gwc_ref, g_ref, du_ref, dagg_ref, mine_ref, other_ref,
):
    coarse = own_ref.shape[0]
    width = h_ref.shape[1]
    sends = hot_rows(row_form(send_ref, 0, send_ref.shape[0]), coarse)
    dp = (own_ref[...].astype(f32) + mm(sends, ret_ref[...])).astype(bf)
    dc = part_ref[...] + mm_nt(dp, wc_ref[0])
    count = count_ref[...]
    dcs = (dc / jnp.concatenate([count, count], axis=1)).astype(bf)
    hot = hot_rows(row_form(pool_ref, 0, pool_ref.shape[0]), coarse)
    g = cot_ref[...].astype(f32) + mm_tn(hot, dcs)
    g_ref[...] = g
    du = (g * dsu_ref[...].astype(f32)).astype(bf)
    du_ref[...] = du
    dagg_ref[...] = mm_nt(du, w_ref[2]).astype(bf)
    gw2 = mm_tn(agg_ref[...], du).astype(bf)
    gw3 = mm_tn(h_ref[...], du).astype(bf)
    by_core(
        core_ref, mine_ref, other_ref,
        [gwc_ref[0 : 3 * width, :]], [gwc_ref[3 * width : 4 * width, :], gw2, gw3],
    )


def edge_back_kernel(
    per, tiles, core_ref, d_ref, he_ref, dagg_ref, h_ref, dst_ref, gbc_ref,
    dz_ref, dq_ref, mine_ref, other_ref, gb, gw0,
):
    t = pl.program_id(0)
    nodes, width = h_ref.shape

    @pl.when(t == 0)
    def _():
        gb[...] = jnp.zeros_like(gb)
        gw0[...] = jnp.zeros_like(gw0)

    hot = hot_rows(row_form(dst_ref, t * per, per), TILE)
    rows = pl.ds(pl.multiple_of(t * TILE, TILE), TILE)
    gm = mm_tn(hot, dagg_ref[rows, :])
    dz = (gm * d_ref[...].astype(f32)).astype(bf)
    dz_ref[...] = dz
    dq = mm(hot, dz)
    gb[...] += jnp.sum(dq, axis=0, keepdims=True)
    dq_ref[rows, :] = dq.astype(bf)
    gw0[...] += mm_tn(he_ref[...], dz)

    @pl.when(t == tiles - 1)
    def _():
        gbf = jnp.broadcast_to(gb[0:1, :], (16, width)).astype(bf)
        gbc = jnp.broadcast_to(gbc_ref[0:1, :], (16, width)).astype(bf)
        gw1 = mm_tn(h_ref[...], dq_ref[...]).astype(bf)
        by_core(core_ref, mine_ref, other_ref, [gw0[...].astype(bf), gbf], [gw1, gbc])


def scatter_kernel(per, tiles, src_ref, dz_ref, own_ref, gl_ref, gr_ref, dzs, *accs):
    t = pl.program_id(0)
    nodes = own_ref.shape[0]
    halo = gl_ref.shape[0]
    edges = per * LANES

    @pl.when(t == 0)
    def _():
        for acc in accs:
            acc[...] = jnp.zeros_like(acc)

    to_pairs(dzs, 0, dz_ref[...].astype(f32))
    for e in range(edges):
        acc = accs[e % len(accs)]
        at = pair(src_ref[t * edges + e])
        acc[at, :] = acc[at, :] + dzs[2 * e : 2 * e + 2, :]

    @pl.when(t == tiles - 1)
    def _():
        def summed(first, n):
            total = from_pairs(accs[0], first, n)
            for acc in accs[1:]:
                total = total + from_pairs(acc, first, n)
            return total.astype(bf)

        own_ref[...] = summed(0, nodes)
        gl_ref[...] = summed(nodes, halo)
        gr_ref[...] = summed(nodes + halo, halo)


def part_kernel(dq_ref, du_ref, g_ref, w_ref, part_ref):
    part_ref[...] = (
        g_ref[...] + mm_nt(du_ref[...], w_ref[3]) + mm_nt(dq_ref[...], w_ref[1])
    )


def input_kernel(own_ref, from_right_ref, from_left_ref, right_ref, left_ref, part_ref, w_ref, o_ref):
    nodes = own_ref.shape[0]
    n = right_ref.shape[0]
    add = mm(hot_rows(row_form(right_ref, 0, n), nodes), from_right_ref[...]) + mm(
        hot_rows(row_form(left_ref, 0, n), nodes), from_left_ref[...]
    )
    dp = (own_ref[...].astype(f32) + add).astype(bf)
    o_ref[...] = part_ref[...] + mm_nt(dp, w_ref[0])


def finish_kernel(scale, core_ref, a_ref, ax_ref, b_ref, bx_ref, gf_ref, gc_ref, gb_ref):
    width = a_ref.shape[1]

    def write(a0, a1, b0, b1):
        def put(ref, k, src, at):
            ref[k * width : (k + 1) * width, :] = (
                src[at * width : (at + 1) * width, :].astype(f32) * scale
            )

        for k in range(3):
            put(gc_ref, k, a0, k)
        put(gc_ref, 3, a1, 0)
        put(gf_ref, 2, a1, 1)
        put(gf_ref, 3, a1, 2)
        put(gf_ref, 0, b0, 0)
        put(gf_ref, 1, b1, 0)
        gb_ref[0:1, :] = b0[width : width + 1, :].astype(f32) * scale
        gb_ref[1:2, :] = b1[width : width + 1, :].astype(f32) * scale

    core = core_ref[0]

    @pl.when(core == 0)
    def _():
        write(a_ref, ax_ref, b_ref, bx_ref)

    @pl.when(core != 0)
    def _():
        write(ax_ref, a_ref, bx_ref, b_ref)


def shifted(block, axis, distance):
    devices = range(lax.axis_size(axis))
    route = [(i - distance, i) for i in devices if i - distance in devices]
    return lax.ppermute(block, axis, route)


def swapped(block, parts, bit):
    return lax.ppermute(block, "dom", [(i, i ^ bit) for i in range(parts)])


def exchange(block, parts):
    rows, width = block.shape
    got = lax.all_to_all(
        block.reshape(parts, rows // parts, width), "dom", split_axis=0, concat_axis=0, tiled=True
    )
    return got


def add(a, b):
    return (a.astype(f32) + b.astype(f32)).astype(bf)


def shards(
    features, cotangent, w_fine, w_coarse, bias, fine_src, fine_dst, send_left, send_right,
    pool_map, coarse_src, coarse_dst, coarse_send,
):
    nodes, width = features.shape
    parts = lax.axis_size("dom")
    coarse = nodes // 4
    tiles = nodes // TILE
    halo = send_left.shape[0]
    per = fine_src.shape[0] // tiles // LANES
    edges = per * LANES
    fsrc, fdst = fine_src.reshape(-1, LANES), fine_dst.reshape(-1, LANES)
    csrc, cdst = coarse_src.reshape(-1, LANES), coarse_dst.reshape(-1, LANES)
    right, left = send_right.reshape(-1, LANES), send_left.reshape(-1, LANES)
    pool = pool_map.reshape(-1, LANES)
    csend = coarse_send.reshape(-1, LANES)
    crows = coarse_send.shape[0] * coarse_send.shape[1]
    part = functools.partial

    to_right, to_left = call(
        halo_kernel, [sds((halo, width), bf)] * 2, [features, right, left]
    )
    h_left = shifted(to_right, "dom", 1)
    h_right = shifted(to_left, "dom", -1)
    edge_tile = pl.BlockSpec((edges, width), lambda t: (t, 0))
    smem = pl.BlockSpec(memory_space=pltpu.SMEM)
    ext_pairs = 2 * (nodes + 2 * halo)
    d_edge, he, agg, dsu, pooled, outgoing, count = call(
        part(fine_kernel, per, tiles),
        [
            sds((tiles * edges, width), bf),
            sds((tiles * edges, width), bf),
            sds((nodes, width), bf),
            sds((nodes, width), bf),
            sds((coarse, width), bf),
            sds((crows, width), bf),
            sds((coarse, LANES), f32),
        ],
        [fine_src, h_left, h_right, features, w_fine, bias, fdst, pool, csend],
        grid=(tiles,),
        specs={0: smem},
        out_specs={0: edge_tile, 1: edge_tile},
        scratch=[
            pltpu.VMEM((nodes, width), bf),
            pltpu.VMEM((ext_pairs, LANES), f32),
            pltpu.VMEM((2 * edges, LANES), f32),
        ],
    )
    incoming = exchange(outgoing, parts).reshape(crows, width)
    cedges = coarse_src.shape[0]
    zc, ghc, uc = call(
        part(coarse_own_kernel, per),
        [sds((cedges, width), f32), sds((coarse, width), f32), sds((coarse, width), f32)],
        [pooled, w_coarse, bias, csrc, cdst, pool, cotangent],
        cost=(4e9, 10e6),
    )
    own_c, back_c, dz_c, du_c, agg_c = call(
        part(coarse_kernel, per),
        [
            sds((coarse, width), bf),
            sds((crows, width), bf),
            sds((cedges, width), bf),
            sds((coarse, width), bf),
            sds((coarse, width), bf),
        ],
        [zc, incoming, ghc, uc, w_coarse, csrc, cdst],
        scratch=[pltpu.VMEM((cedges, width), f32)],
    )
    returned = exchange(back_c, parts).reshape(crows, width)
    gw_c, gb_c, part_c = call(
        part(coarse_grad_kernel, per),
        [sds((4 * width, width), bf), sds((8, width), f32), sds((coarse, width), f32)],
        [pooled, incoming, ghc, w_coarse, cdst, own_c, back_c, dz_c, du_c, agg_c],
        cost=(4e9, 10e6),
    )
    core = (lax.axis_index("dom") % 2).astype(jnp.int32).reshape(1)
    same_core = [list(range(c, parts, 2)) for c in range(2)]
    chips = parts // 2
    g, du, dagg, mine, other = call(
        node_back_kernel,
        [
            sds((nodes, width), f32),
            sds((nodes, width), bf),
            sds((nodes, width), bf),
            sds((3 * width, width), bf),
            sds((3 * width, width), bf),
        ],
        [
            core, own_c, returned, csend, part_c, w_coarse, count, pool, cotangent, dsu, w_fine,
            features, agg, gw_c,
        ],
        specs={0: smem},
    )
    early = add(mine, swapped(other, parts, 1))
    early, dagg = lax.optimization_barrier((early, dagg))
    early = lax.all_to_all(
        early.reshape(chips, -1, width), "dom", 0, 0, axis_index_groups=same_core, tiled=True
    )
    dz, dq, mine, other = call(
        part(edge_back_kernel, per, tiles),
        [
            sds((tiles * edges, width), bf),
            sds((nodes, width), bf),
            sds((width + 16, width), bf),
            sds((width + 16, width), bf),
        ],
        [core, d_edge, he, dagg, features, fdst, gb_c],
        grid=(tiles,),
        specs={0: smem, 1: edge_tile, 2: edge_tile},
        out_specs={0: edge_tile},
        scratch=[pltpu.VMEM((8, width), f32), pltpu.VMEM((width, width), f32)],
        cost=(15e9, 10e6),
    )
    early, dz, dq, mine, other = lax.optimization_barrier((early, dz, dq, mine, other))
    late = add(mine, swapped(other, parts, 1))
    early = jnp.sum(early.astype(f32), axis=0).astype(bf)
    early = lax.all_to_all(
        jnp.broadcast_to(early[None], (chips,) + early.shape),
        "dom", 0, 0, axis_index_groups=same_core, tiled=True,
    ).reshape(-1, width)
    own_f, gl, gr = call(
        part(scatter_kernel, per, tiles),
        [sds((nodes, width), bf), sds((halo, width), bf), sds((halo, width), bf)],
        [fine_src, dz],
        grid=(tiles,),
        specs={0: smem, 1: edge_tile},
        scratch=[pltpu.VMEM((2 * edges, LANES), f32)]
        + [pltpu.VMEM((ext_pairs, LANES), f32)] * 8,
        cost=(15e9, 10e6),
    )
    bit = 2
    while bit < parts:
        late = add(late, swapped(late, parts, bit))
        bit *= 2
    from_right = shifted(gl, "dom", -1)
    from_left = shifted(gr, "dom", 1)
    (part_f,) = call(
        part_kernel, [sds((nodes, width), f32)], [dq, du, g, w_fine], cost=(4e9, 10e6)
    )
    (grad_input,) = call(
        input_kernel,
        [sds((nodes, width), f32)],
        [own_f, from_right, from_left, right, left, part_f, w_fine],
        cost=(4e9, 10e6),
    )
    scale = 1.0 / float(nodes * parts // 256)
    grad_fine, grad_coarse, grad_bias = call(
        part(finish_kernel, scale),
        [sds((4 * width, width), f32), sds((4 * width, width), f32), sds((2, width), f32)],
        [
            core, early, swapped(early, parts, 1), late, swapped(late, parts, 1),
        ],
        specs={0: smem},
    )
    shape = (4, width, width)
    return (grad_input, grad_fine.reshape(shape), grad_coarse.reshape(shape), grad_bias)


def solution(mesh):
    return jax.shard_map(
        shards,
        mesh=mesh,
        in_specs=(
            P(("groups", "dom"), None),
            P(("groups", "dom"), None),
            P(),
            P(),
            P(),
            P("dom"),
            P("dom"),
            P("dom"),
            P("dom"),
            P("dom"),
            P("dom"),
            P("dom"),
            P("dom", None),
        ),
        out_specs=(
            P(("groups", "dom"), None),
            P("groups", None, None),
            P("groups", None, None),
            P("groups", None),
        ),
        check_vma=False,
    )
```

```python
import functools

import jax
import jax.numpy as jnp
from jax import lax
from jax.experimental import pallas as pl
from jax.experimental.pallas import tpu as pltpu
from jax.sharding import PartitionSpec as P

bf = jnp.bfloat16
f32 = jnp.float32
TILE = 128
LANES = 128


def mm(a, b):
    return jnp.dot(a, b, preferred_element_type=f32)


def mm_tn(a, b):
    return lax.dot_general(a, b, (((0,), (0,)), ((), ())), preferred_element_type=f32)


def mm_nt(a, b):
    return lax.dot_general(a, b, (((1,), (1,)), ((), ())), preferred_element_type=f32)


def as_bf(x):
    return x.astype(f32).astype(bf)


def row_form(ref, first, count):
    return jnp.concatenate([ref[pl.ds(first + j, 1), :] for j in range(count)], axis=1)


def hot_rows(row, rows):
    cols = row.shape[1]
    if rows <= 256:
        io = as_bf(lax.broadcasted_iota(jnp.int32, (rows, cols), 0))
        return jnp.where(io == as_bf(row), bf(1), bf(0))
    low = as_bf(row & 255)
    high = as_bf(lax.shift_right_arithmetic(row, 8))
    io = as_bf(lax.broadcasted_iota(jnp.int32, (256, cols), 0))
    base = jnp.where(io == low, bf(1), bf(0))
    return jnp.concatenate(
        [jnp.where(high == bf(k), base, bf(0)) for k in range(rows // 256)], axis=0
    )


def tile_loop(group, body):
    if group == 1:
        body(0)
    else:

        def step(k, carry):
            body(k)
            return carry

        lax.fori_loop(0, group, step, 0)


def tile_rows(index, size):
    return pl.ds(pl.multiple_of(index * size, size), size)


def silu_parts(v):
    sig = 0.5 * jnp.tanh(0.5 * v) + 0.5
    silu = v * sig
    return silu, sig + silu * (1.0 - sig)


def to_pairs(ref, first, rows):
    n = rows.shape[0]
    for j in range(2):
        ref[pl.ds(2 * first + j, n, stride=2), :] = rows[:, j * LANES : (j + 1) * LANES]


def from_pairs(ref, first, n):
    return jnp.concatenate([ref[pl.ds(2 * first + j, n, stride=2), :] for j in range(2)], axis=1)


def pair(index):
    return pl.ds(pl.multiple_of(index * 2, 2), 2)


def call(kernel, outs, args, grid=(), specs=None, out_specs=None, scratch=(), cost=(0, 0)):
    def whole(a):
        return pl.BlockSpec(a.shape, lambda *_: (0,) * len(a.shape))

    in_specs = [whole(a) for a in args]
    o_specs = [whole(o) for o in outs]
    for k, s in (specs or {}).items():
        in_specs[k] = s
    for k, s in (out_specs or {}).items():
        o_specs[k] = s
    return pl.pallas_call(
        kernel,
        grid=grid or (1,),
        in_specs=in_specs,
        out_specs=o_specs,
        out_shape=outs,
        scratch_shapes=list(scratch),
        compiler_params=pltpu.CompilerParams(vmem_limit_bytes=56 << 20),
        cost_estimate=pl.CostEstimate(
            flops=int(cost[0]), bytes_accessed=int(cost[1]), transcendentals=0
        ),
    )(*args)


def sds(shape, dtype):
    return jax.ShapeDtypeStruct(shape, dtype)


def halo_kernel(h_ref, right_ref, left_ref, to_right_ref, to_left_ref):
    h = h_ref[...]
    n = right_ref.shape[0]
    to_right_ref[...] = mm_tn(hot_rows(row_form(right_ref, 0, n), h.shape[0]), h).astype(bf)
    to_left_ref[...] = mm_tn(hot_rows(row_form(left_ref, 0, n), h.shape[0]), h).astype(bf)


def fine_kernel(
    per, group, src_ref, left_ref, right_ref, h_ref, w_ref, b_ref, dst_ref, pool_ref, send_ref,
    d_ref, he_ref, agg_ref, dsu_ref, pooled_ref, out_ref, count_ref, recv, table, taken,
):
    step = pl.program_id(0)
    nodes = h_ref.shape[0]
    halo = left_ref.shape[0]
    edges = per * LANES

    @pl.when(step == 0)
    def _():
        recv[...] = mm(h_ref[...], w_ref[1]).astype(bf)
        to_pairs(table, 0, h_ref[...].astype(f32))
        to_pairs(table, nodes, left_ref[...].astype(f32))
        to_pairs(table, nodes + halo, right_ref[...].astype(f32))

    def tile(k):
        t = step * group + k
        for e in range(edges):
            taken[2 * e : 2 * e + 2, :] = table[pair(src_ref[t * edges + e]), :]
        rows = tile_rows(t, TILE)
        hot = hot_rows(row_form(dst_ref, t * per, per), TILE)
        he = from_pairs(taken, 0, edges).astype(bf)
        he_ref[tile_rows(k, edges), :] = he
        sent = as_bf(mm(he, w_ref[0])).astype(f32)
        z = sent + mm_tn(hot, recv[rows, :]) + b_ref[0:1, :]
        m, d = silu_parts(z)
        d_ref[tile_rows(k, edges), :] = d.astype(bf)
        agg_ref[rows, :] = mm(hot, m.astype(bf)).astype(bf)

    tile_loop(group, tile)

    @pl.when(step == pl.num_programs(0) - 1)
    def _():
        h = h_ref[...]
        u = mm(h, w_ref[3]) + mm(agg_ref[...], w_ref[2])
        su, dsu = silu_parts(u)
        dsu_ref[...] = dsu.astype(bf)
        h1 = (h.astype(f32) + su).astype(bf)
        coarse = pooled_ref.shape[0]
        hot = hot_rows(row_form(pool_ref, 0, pool_ref.shape[0]), coarse)
        count = mm(hot, jnp.ones((nodes, LANES), bf))
        count_ref[...] = count
        pooled = (mm(hot, h1) / jnp.concatenate([count, count], axis=1)).astype(bf)
        pooled_ref[...] = pooled
        sends = hot_rows(row_form(send_ref, 0, send_ref.shape[0]), coarse)
        out_ref[...] = mm_tn(sends, pooled).astype(bf)


def coarse_own_kernel(
    per, pooled_ref, w_ref, b_ref, src_ref, dst_ref, pool_ref, cot_ref, z_ref, ghc_ref, u_ref
):
    pooled = pooled_ref[...]
    coarse = pooled.shape[0]
    proj = mm(pooled, w_ref[0]).astype(bf)
    recv = mm(pooled, w_ref[1]).astype(bf)
    u_ref[...] = mm(pooled, w_ref[3])
    edges = per * LANES
    for t in range(coarse // TILE):
        src = row_form(src_ref, t * per, per)
        dst = row_form(dst_ref, t * per, per)
        z_ref[t * edges : (t + 1) * edges, :] = (
            mm_tn(hot_rows(src, coarse), proj)
            + mm_tn(hot_rows(dst, TILE), recv[t * TILE : (t + 1) * TILE, :])
            + b_ref[1:2, :]
        )
    hot = hot_rows(row_form(pool_ref, 0, pool_ref.shape[0]), coarse)
    ghc_ref[...] = mm(hot, cot_ref[...])


def coarse_kernel(
    per, z_ref, in_ref, ghc_ref, u_ref, w_ref, src_ref, dst_ref,
    own_ref, back_ref, dz_ref, du_ref, agg_ref, deriv,
):
    coarse = ghc_ref.shape[0]
    edges = per * LANES
    tiles = coarse // TILE
    proj = mm(in_ref[...], w_ref[0]).astype(bf)
    for t in range(tiles):
        src = row_form(src_ref, t * per, per) - coarse
        dst = row_form(dst_ref, t * per, per)
        z = z_ref[t * edges : (t + 1) * edges, :] + mm_tn(hot_rows(src, proj.shape[0]), proj)
        m, d = silu_parts(z)
        deriv[t * edges : (t + 1) * edges, :] = d
        agg_ref[t * TILE : (t + 1) * TILE, :] = mm(hot_rows(dst, TILE), m.astype(bf)).astype(bf)
    u = u_ref[...] + mm(agg_ref[...], w_ref[2])
    _, dsu = silu_parts(u)
    du = (ghc_ref[...] * dsu).astype(bf)
    du_ref[...] = du
    dagg = mm_nt(du, w_ref[2]).astype(bf)
    total = None
    for t in range(tiles):
        src = row_form(src_ref, t * per, per)
        dst = row_form(dst_ref, t * per, per)
        gm = mm_tn(hot_rows(dst, TILE), dagg[t * TILE : (t + 1) * TILE, :])
        dz = (gm * deriv[t * edges : (t + 1) * edges, :]).astype(bf)
        dz_ref[t * edges : (t + 1) * edges, :] = dz
        part = mm(hot_rows(src, coarse + proj.shape[0]), dz)
        total = part if total is None else total + part
    own_ref[...] = total[:coarse].astype(bf)
    back_ref[...] = total[coarse:].astype(bf)


def by_core(core_ref, mine_ref, other_ref, half0, half1):
    core = core_ref[0]

    def write(ref, half):
        at = 0
        for piece in half:
            ref[at : at + piece.shape[0], :] = piece
            at += piece.shape[0]

    @pl.when(core == 0)
    def _():
        write(mine_ref, half0)
        write(other_ref, half1)

    @pl.when(core != 0)
    def _():
        write(mine_ref, half1)
        write(other_ref, half0)


def coarse_grad_kernel(
    per, pooled_ref, in_ref, ghc_ref, w_ref, dst_ref, own_ref, back_ref, dz_ref, du_ref, agg_ref,
    gw_ref, gb_ref, part_ref,
):
    pooled = pooled_ref[...]
    coarse, width = pooled.shape
    edges = per * LANES
    dqs = []
    gb = jnp.zeros((1, width), f32)
    for t in range(coarse // TILE):
        dst = row_form(dst_ref, t * per, per)
        dq = mm(hot_rows(dst, TILE), dz_ref[t * edges : (t + 1) * edges, :])
        gb = gb + jnp.sum(dq, axis=0, keepdims=True)
        dqs.append(dq.astype(bf))
    dq = jnp.concatenate(dqs, axis=0)
    du = du_ref[...]
    gb_ref[...] = jnp.broadcast_to(gb, gb_ref.shape)
    gw_ref[0:width, :] = (mm_tn(pooled, own_ref[...]) + mm_tn(in_ref[...], back_ref[...])).astype(bf)
    gw_ref[width : 2 * width, :] = mm_tn(pooled, dq).astype(bf)
    gw_ref[2 * width : 3 * width, :] = mm_tn(agg_ref[...], du).astype(bf)
    gw_ref[3 * width : 4 * width, :] = mm_tn(pooled, du).astype(bf)
    part_ref[...] = ghc_ref[...] + mm_nt(du, w_ref[3]) + mm_nt(dq, w_ref[1])


def node_back_kernel(
    own_ref, ret_ref, send_ref, part_ref, wc_ref, count_ref, pool_ref, cot_ref, dsu_ref, w_ref,
    g_ref, du_ref, dagg_ref,
):
    coarse = own_ref.shape[0]
    sends = hot_rows(row_form(send_ref, 0, send_ref.shape[0]), coarse)
    dp = (own_ref[...].astype(f32) + mm(sends, ret_ref[...])).astype(bf)
    dc = part_ref[...] + mm_nt(dp, wc_ref[0])
    count = count_ref[...]
    dcs = (dc / jnp.concatenate([count, count], axis=1)).astype(bf)
    hot = hot_rows(row_form(pool_ref, 0, pool_ref.shape[0]), coarse)
    g = cot_ref[...].astype(f32) + mm_tn(hot, dcs)
    g_ref[...] = g
    du = (g * dsu_ref[...].astype(f32)).astype(bf)
    du_ref[...] = du
    dagg_ref[...] = mm_nt(du, w_ref[2]).astype(bf)


def edge_back_kernel(
    per, group, core_ref, d_ref, he_ref, dagg_ref, h_ref, dst_ref, gwc_ref, gbc_ref, agg_ref, du_ref,
    dz_ref, dq_ref, mine_ref, other_ref, gb, gw0,
):
    step = pl.program_id(0)
    width = h_ref.shape[1]
    edges = per * LANES

    @pl.when(step == 0)
    def _():
        gb[...] = jnp.zeros_like(gb)
        gw0[...] = jnp.zeros_like(gw0)

    def tile(k):
        t = step * group + k
        hot = hot_rows(row_form(dst_ref, t * per, per), TILE)
        rows = tile_rows(t, TILE)
        here = tile_rows(k, edges)
        gm = mm_tn(hot, dagg_ref[rows, :])
        dz = (gm * d_ref[here, :].astype(f32)).astype(bf)
        dz_ref[here, :] = dz
        dq = mm(hot, dz)
        gb[...] += jnp.sum(dq, axis=0, keepdims=True)
        dq_ref[rows, :] = dq.astype(bf)

    tile_loop(group, tile)
    gw0[...] += mm_tn(he_ref[...], dz_ref[...])

    @pl.when(step == pl.num_programs(0) - 1)
    def _():
        gbf = jnp.broadcast_to(gb[0:1, :], (16, width)).astype(bf)
        gbc = jnp.broadcast_to(gbc_ref[0:1, :], (16, width)).astype(bf)
        h = h_ref[...]
        gw1 = mm_tn(h, dq_ref[...]).astype(bf)
        gw2 = mm_tn(agg_ref[...], du_ref[...]).astype(bf)
        gw3 = mm_tn(h, du_ref[...]).astype(bf)
        half0 = [gwc_ref[0 : 2 * width, :], gw0[...].astype(bf), gw1] + [gbf] * 4
        half1 = [gwc_ref[2 * width : 4 * width, :], gw2, gw3] + [gbc] * 4
        by_core(core_ref, mine_ref, other_ref, half0, half1)


def scatter_kernel(per, group, src_ref, dz_ref, own_ref, gl_ref, gr_ref, dzs, *accs):
    step = pl.program_id(0)
    nodes = own_ref.shape[0]
    halo = gl_ref.shape[0]
    edges = per * LANES

    @pl.when(step == 0)
    def _():
        for acc in accs:
            acc[...] = jnp.zeros_like(acc)

    def tile(k):
        t = step * group + k
        to_pairs(dzs, 0, dz_ref[tile_rows(k, edges), :].astype(f32))
        for e in range(edges):
            acc = accs[e % len(accs)]
            at = pair(src_ref[t * edges + e])
            acc[at, :] = acc[at, :] + dzs[2 * e : 2 * e + 2, :]

    tile_loop(group, tile)

    @pl.when(step == pl.num_programs(0) - 1)
    def _():
        def summed(first, n):
            total = from_pairs(accs[0], first, n)
            for acc in accs[1:]:
                total = total + from_pairs(acc, first, n)
            return total.astype(bf)

        own_ref[...] = summed(0, nodes)
        gl_ref[...] = summed(nodes, halo)
        gr_ref[...] = summed(nodes + halo, halo)


def part_kernel(dq_ref, du_ref, g_ref, w_ref, part_ref):
    part_ref[...] = (
        g_ref[...] + mm_nt(du_ref[...], w_ref[3]) + mm_nt(dq_ref[...], w_ref[1])
    )


def input_kernel(own_ref, from_right_ref, from_left_ref, right_ref, left_ref, part_ref, w_ref, o_ref):
    nodes = own_ref.shape[0]
    n = right_ref.shape[0]
    add = mm(hot_rows(row_form(right_ref, 0, n), nodes), from_right_ref[...]) + mm(
        hot_rows(row_form(left_ref, 0, n), nodes), from_left_ref[...]
    )
    dp = (own_ref[...].astype(f32) + add).astype(bf)
    o_ref[...] = part_ref[...] + mm_nt(dp, w_ref[0])


def finish_kernel(scale, core_ref, a_ref, ax_ref, gf_ref, gc_ref, gb_ref):
    two = gf_ref.shape[0] // 2

    def write(half, src):
        rows = slice(half * two, (half + 1) * two)
        gc_ref[rows, :] = src[0:two, :].astype(f32) * scale
        gf_ref[rows, :] = src[two : 2 * two, :].astype(f32) * scale
        gb_ref[half : half + 1, :] = src[2 * two : 2 * two + 16, :].astype(f32)[0:1] * scale

    core = core_ref[0]

    @pl.when(core == 0)
    def _():
        write(0, a_ref)
        write(1, ax_ref)

    @pl.when(core != 0)
    def _():
        write(1, a_ref)
        write(0, ax_ref)


def shifted(block, axis, distance):
    devices = range(lax.axis_size(axis))
    route = [(i - distance, i) for i in devices if i - distance in devices]
    return lax.ppermute(block, axis, route)


def swapped(block, parts, bit):
    return lax.ppermute(block, "dom", [(i, i ^ bit) for i in range(parts)])


def exchange(block, parts):
    rows, width = block.shape
    got = lax.all_to_all(
        block.reshape(parts, rows // parts, width), "dom", split_axis=0, concat_axis=0, tiled=True
    )
    return got


def add(a, b):
    return (a.astype(f32) + b.astype(f32)).astype(bf)


def over_chips(blocks, groups):
    return lax.all_to_all(blocks, "dom", 0, 0, axis_index_groups=groups, tiled=True)


def shards(
    features, cotangent, w_fine, w_coarse, bias, fine_src, fine_dst, send_left, send_right,
    pool_map, coarse_src, coarse_dst, coarse_send,
):
    nodes, width = features.shape
    parts = lax.axis_size("dom")
    coarse = nodes // 4
    tiles = nodes // TILE
    halo = send_left.shape[0]
    per = fine_src.shape[0] // tiles // LANES
    edges = per * LANES
    fsrc, fdst = fine_src.reshape(-1, LANES), fine_dst.reshape(-1, LANES)
    csrc, cdst = coarse_src.reshape(-1, LANES), coarse_dst.reshape(-1, LANES)
    right, left = send_right.reshape(-1, LANES), send_left.reshape(-1, LANES)
    pool = pool_map.reshape(-1, LANES)
    csend = coarse_send.reshape(-1, LANES)
    crows = coarse_send.shape[0] * coarse_send.shape[1]
    part = functools.partial
    core = (lax.axis_index("dom") % 2).astype(jnp.int32).reshape(1)
    same_core = [list(range(c, parts, 2)) for c in range(2)]
    chips = parts // 2
    group = 4
    steps = tiles // group

    to_right, to_left = call(
        halo_kernel, [sds((halo, width), bf)] * 2, [features, right, left]
    )
    h_left = shifted(to_right, "dom", 1)
    h_right = shifted(to_left, "dom", -1)
    edge_tile = pl.BlockSpec((group * edges, width), lambda t: (t, 0))
    smem = pl.BlockSpec(memory_space=pltpu.SMEM)
    ext_pairs = 2 * (nodes + 2 * halo)
    d_edge, he, agg, dsu, pooled, outgoing, count = call(
        part(fine_kernel, per, group),
        [
            sds((tiles * edges, width), bf),
            sds((tiles * edges, width), bf),
            sds((nodes, width), bf),
            sds((nodes, width), bf),
            sds((coarse, width), bf),
            sds((crows, width), bf),
            sds((coarse, LANES), f32),
        ],
        [fine_src, h_left, h_right, features, w_fine, bias, fdst, pool, csend],
        grid=(steps,),
        specs={0: smem},
        out_specs={0: edge_tile, 1: edge_tile},
        scratch=[
            pltpu.VMEM((nodes, width), bf),
            pltpu.VMEM((ext_pairs, LANES), f32),
            pltpu.VMEM((2 * edges, LANES), f32),
        ],
    )
    incoming = exchange(outgoing, parts).reshape(crows, width)
    cedges = coarse_src.shape[0]
    zc, ghc, uc = call(
        part(coarse_own_kernel, per),
        [sds((cedges, width), f32), sds((coarse, width), f32), sds((coarse, width), f32)],
        [pooled, w_coarse, bias, csrc, cdst, pool, cotangent],
        cost=(4e9, 10e6),
    )
    own_c, back_c, dz_c, du_c, agg_c = call(
        part(coarse_kernel, per),
        [
            sds((coarse, width), bf),
            sds((crows, width), bf),
            sds((cedges, width), bf),
            sds((coarse, width), bf),
            sds((coarse, width), bf),
        ],
        [zc, incoming, ghc, uc, w_coarse, csrc, cdst],
        scratch=[pltpu.VMEM((cedges, width), f32)],
    )
    returned = exchange(back_c, parts).reshape(crows, width)
    gw_c, gb_c, part_c = call(
        part(coarse_grad_kernel, per),
        [sds((4 * width, width), bf), sds((8, width), f32), sds((coarse, width), f32)],
        [pooled, incoming, ghc, w_coarse, cdst, own_c, back_c, dz_c, du_c, agg_c],
        cost=(4e9, 10e6),
    )
    g, du, dagg = call(
        node_back_kernel,
        [sds((nodes, width), f32), sds((nodes, width), bf), sds((nodes, width), bf)],
        [own_c, returned, csend, part_c, w_coarse, count, pool, cotangent, dsu, w_fine],
        cost=(6e9, 10e6),
    )
    half_rows = 4 * width + 64
    dz, dq, mine, other = call(
        part(edge_back_kernel, per, group),
        [
            sds((tiles * edges, width), bf),
            sds((nodes, width), bf),
            sds((half_rows, width), bf),
            sds((half_rows, width), bf),
        ],
        [core, d_edge, he, dagg, features, fdst, gw_c, gb_c, agg, du],
        grid=(steps,),
        specs={0: smem, 1: edge_tile, 2: edge_tile},
        out_specs={0: edge_tile},
        scratch=[pltpu.VMEM((8, width), f32), pltpu.VMEM((width, width), f32)],
        cost=(15e9, 10e6),
    )
    sums = add(mine, swapped(other, parts, 1)).reshape(chips, -1, width)
    sums, dz = lax.optimization_barrier((sums, dz))
    sums = over_chips(sums, same_core)
    own_f, gl, gr = call(
        part(scatter_kernel, per, group),
        [sds((nodes, width), bf), sds((halo, width), bf), sds((halo, width), bf)],
        [fine_src, dz],
        grid=(steps,),
        specs={0: smem, 1: edge_tile},
        scratch=[pltpu.VMEM((2 * edges, LANES), f32)]
        + [pltpu.VMEM((ext_pairs, LANES), f32)] * 8,
        cost=(15e9, 10e6),
    )
    sums, own_f, gl, gr = lax.optimization_barrier((sums, own_f, gl, gr))
    sums = jnp.sum(sums.astype(f32), axis=0).astype(bf)
    sums = over_chips(jnp.broadcast_to(sums[None], (chips,) + sums.shape), same_core)
    from_right = shifted(gl, "dom", -1)
    from_left = shifted(gr, "dom", 1)
    (part_f,) = call(
        part_kernel, [sds((nodes, width), f32)], [dq, du, g, w_fine], cost=(4e9, 10e6)
    )
    (grad_input,) = call(
        input_kernel,
        [sds((nodes, width), f32)],
        [own_f, from_right, from_left, right, left, part_f, w_fine],
        cost=(4e9, 10e6),
    )
    sums, grad_input = lax.optimization_barrier((sums, grad_input))
    sums = sums.reshape(half_rows, width)
    scale = 1.0 / float(nodes * parts // 256)
    grad_fine, grad_coarse, grad_bias = call(
        part(finish_kernel, scale),
        [sds((4 * width, width), f32), sds((4 * width, width), f32), sds((2, width), f32)],
        [core, sums, swapped(sums, parts, 1)],
        specs={0: smem},
    )
    shape = (4, width, width)
    return (grad_input, grad_fine.reshape(shape), grad_coarse.reshape(shape), grad_bias)


def solution(mesh):
    return jax.shard_map(
        shards,
        mesh=mesh,
        in_specs=(
            P(("groups", "dom"), None),
            P(("groups", "dom"), None),
            P(),
            P(),
            P(),
            P("dom"),
            P("dom"),
            P("dom"),
            P("dom"),
            P("dom"),
            P("dom"),
            P("dom"),
            P("dom", None),
        ),
        out_specs=(
            P(("groups", "dom"), None),
            P("groups", None, None),
            P("groups", None, None),
            P("groups", None),
        ),
        check_vma=False,
    )
```

```python
import functools

import jax
import jax.numpy as jnp
from jax import lax
from jax.experimental import pallas as pl
from jax.experimental.pallas import tpu as pltpu
from jax.sharding import PartitionSpec as P

bf = jnp.bfloat16
f32 = jnp.float32
TILE = 128
LANES = 128
FINE_UNROLL = 4
EDGE_UNROLL = 4


def mm(a, b):
    return jnp.dot(a, b, preferred_element_type=f32)


def mm_tn(a, b):
    return lax.dot_general(a, b, (((0,), (0,)), ((), ())), preferred_element_type=f32)


def mm_nt(a, b):
    return lax.dot_general(a, b, (((1,), (1,)), ((), ())), preferred_element_type=f32)


def as_bf(x):
    return x.astype(f32).astype(bf)


def row_form(ref, first, count):
    return jnp.concatenate([ref[pl.ds(first + j, 1), :] for j in range(count)], axis=1)


def hot_rows(row, rows):
    cols = row.shape[1]
    if rows <= 256:
        io = as_bf(lax.broadcasted_iota(jnp.int32, (rows, cols), 0))
        return jnp.where(io == as_bf(row), bf(1), bf(0))
    low = as_bf(row & 255)
    high = as_bf(lax.shift_right_arithmetic(row, 8))
    io = as_bf(lax.broadcasted_iota(jnp.int32, (256, cols), 0))
    base = jnp.where(io == low, bf(1), bf(0))
    return jnp.concatenate(
        [jnp.where(high == bf(k), base, bf(0)) for k in range(rows // 256)], axis=0
    )


def tile_loop(group, unroll, body):
    if group == unroll:
        for k in range(group):
            body(k, k)
    else:

        def step(j, carry):
            for k in range(unroll):
                body(j * unroll + k, k)
            return carry

        lax.fori_loop(0, group // unroll, step, 0)


def tile_rows(index, size):
    return pl.ds(pl.multiple_of(index * size, size), size)


def silu_parts(v):
    sig = 0.5 * jnp.tanh(0.5 * v) + 0.5
    silu = v * sig
    return silu, sig + silu * (1.0 - sig)


def to_pairs(ref, first, rows):
    n = rows.shape[0]
    for j in range(2):
        ref[pl.ds(2 * first + j, n, stride=2), :] = rows[:, j * LANES : (j + 1) * LANES]


def from_pairs(ref, first, n):
    return jnp.concatenate([ref[pl.ds(2 * first + j, n, stride=2), :] for j in range(2)], axis=1)


def pair(index):
    return pl.ds(pl.multiple_of(index * 2, 2), 2)


def call(kernel, outs, args, grid=(), specs=None, out_specs=None, scratch=(), cost=(0, 0)):
    def whole(a):
        return pl.BlockSpec(a.shape, lambda *_: (0,) * len(a.shape))

    in_specs = [whole(a) for a in args]
    o_specs = [whole(o) for o in outs]
    for k, s in (specs or {}).items():
        in_specs[k] = s
    for k, s in (out_specs or {}).items():
        o_specs[k] = s
    return pl.pallas_call(
        kernel,
        grid=grid or (1,),
        in_specs=in_specs,
        out_specs=o_specs,
        out_shape=outs,
        scratch_shapes=list(scratch),
        compiler_params=pltpu.CompilerParams(vmem_limit_bytes=24 << 20),
        cost_estimate=pl.CostEstimate(
            flops=int(cost[0]), bytes_accessed=int(cost[1]), transcendentals=0
        ),
    )(*args)


def sds(shape, dtype):
    return jax.ShapeDtypeStruct(shape, dtype)


def halo_kernel(h_ref, right_ref, left_ref, to_right_ref, to_left_ref):
    h = h_ref[...]
    n = right_ref.shape[0]
    to_right_ref[...] = mm_tn(hot_rows(row_form(right_ref, 0, n), h.shape[0]), h).astype(bf)
    to_left_ref[...] = mm_tn(hot_rows(row_form(left_ref, 0, n), h.shape[0]), h).astype(bf)


def fine_kernel(
    per, group, src_ref, left_ref, right_ref, h_ref, w_ref, b_ref, dst_ref, pool_ref, send_ref,
    d_ref, he_ref, agg_ref, dsu_ref, pooled_ref, out_ref, count_ref, recv, table, taken,
):
    step = pl.program_id(0)
    nodes = h_ref.shape[0]
    halo = left_ref.shape[0]
    edges = per * LANES

    @pl.when(step == 0)
    def _():
        recv[...] = mm(h_ref[...], w_ref[1]).astype(bf)
        to_pairs(table, 0, h_ref[...].astype(f32))
        to_pairs(table, nodes, left_ref[...].astype(f32))
        to_pairs(table, nodes + halo, right_ref[...].astype(f32))

    def tile(k, slot):
        t = step * group + k
        for e in range(edges):
            at = 2 * (slot * edges + e)
            taken[at : at + 2, :] = table[pair(src_ref[t * edges + e]), :]
        rows = tile_rows(t, TILE)
        hot = hot_rows(row_form(dst_ref, t * per, per), TILE)
        he = from_pairs(taken, slot * edges, edges).astype(bf)
        he_ref[tile_rows(k, edges), :] = he
        sent = as_bf(mm(he, w_ref[0])).astype(f32)
        z = sent + mm_tn(hot, recv[rows, :]) + b_ref[0:1, :]
        m, d = silu_parts(z)
        d_ref[tile_rows(k, edges), :] = d.astype(bf)
        agg_ref[rows, :] = mm(hot, m.astype(bf)).astype(bf)

    tile_loop(group, FINE_UNROLL, tile)

    @pl.when(step == pl.num_programs(0) - 1)
    def _():
        h = h_ref[...]
        u = mm(h, w_ref[3]) + mm(agg_ref[...], w_ref[2])
        su, dsu = silu_parts(u)
        dsu_ref[...] = dsu.astype(bf)
        h1 = (h.astype(f32) + su).astype(bf)
        coarse = pooled_ref.shape[0]
        hot = hot_rows(row_form(pool_ref, 0, pool_ref.shape[0]), coarse)
        count = mm(hot, jnp.ones((nodes, LANES), bf))
        count_ref[...] = count
        pooled = (mm(hot, h1) / jnp.concatenate([count, count], axis=1)).astype(bf)
        pooled_ref[...] = pooled
        sends = hot_rows(row_form(send_ref, 0, send_ref.shape[0]), coarse)
        out_ref[...] = mm_tn(sends, pooled).astype(bf)


def coarse_own_kernel(
    per, pooled_ref, w_ref, b_ref, src_ref, dst_ref, pool_ref, cot_ref, z_ref, ghc_ref, u_ref
):
    pooled = pooled_ref[...]
    coarse = pooled.shape[0]
    proj = mm(pooled, w_ref[0]).astype(bf)
    recv = mm(pooled, w_ref[1]).astype(bf)
    u_ref[...] = mm(pooled, w_ref[3])
    edges = per * LANES
    for t in range(coarse // TILE):
        src = row_form(src_ref, t * per, per)
        dst = row_form(dst_ref, t * per, per)
        z_ref[t * edges : (t + 1) * edges, :] = (
            mm_tn(hot_rows(src, coarse), proj)
            + mm_tn(hot_rows(dst, TILE), recv[t * TILE : (t + 1) * TILE, :])
            + b_ref[1:2, :]
        )
    hot = hot_rows(row_form(pool_ref, 0, pool_ref.shape[0]), coarse)
    ghc_ref[...] = mm(hot, cot_ref[...])


def coarse_kernel(
    per, z_ref, in_ref, ghc_ref, u_ref, w_ref, src_ref, dst_ref,
    own_ref, back_ref, dz_ref, du_ref, agg_ref, deriv,
):
    coarse = ghc_ref.shape[0]
    edges = per * LANES
    tiles = coarse // TILE
    proj = mm(in_ref[...], w_ref[0]).astype(bf)
    for t in range(tiles):
        src = row_form(src_ref, t * per, per) - coarse
        dst = row_form(dst_ref, t * per, per)
        z = z_ref[t * edges : (t + 1) * edges, :] + mm_tn(hot_rows(src, proj.shape[0]), proj)
        m, d = silu_parts(z)
        deriv[t * edges : (t + 1) * edges, :] = d
        agg_ref[t * TILE : (t + 1) * TILE, :] = mm(hot_rows(dst, TILE), m.astype(bf)).astype(bf)
    u = u_ref[...] + mm(agg_ref[...], w_ref[2])
    _, dsu = silu_parts(u)
    du = (ghc_ref[...] * dsu).astype(bf)
    du_ref[...] = du
    dagg = mm_nt(du, w_ref[2]).astype(bf)
    total = None
    for t in range(tiles):
        src = row_form(src_ref, t * per, per)
        dst = row_form(dst_ref, t * per, per)
        gm = mm_tn(hot_rows(dst, TILE), dagg[t * TILE : (t + 1) * TILE, :])
        dz = (gm * deriv[t * edges : (t + 1) * edges, :]).astype(bf)
        dz_ref[t * edges : (t + 1) * edges, :] = dz
        part = mm(hot_rows(src, coarse + proj.shape[0]), dz)
        total = part if total is None else total + part
    own_ref[...] = total[:coarse].astype(bf)
    back_ref[...] = total[coarse:].astype(bf)


def by_core(core_ref, mine_ref, other_ref, half0, half1):
    core = core_ref[0]

    def write(ref, half):
        at = 0
        for piece in half:
            ref[at : at + piece.shape[0], :] = piece
            at += piece.shape[0]

    @pl.when(core == 0)
    def _():
        write(mine_ref, half0)
        write(other_ref, half1)

    @pl.when(core != 0)
    def _():
        write(mine_ref, half1)
        write(other_ref, half0)


def coarse_grad_kernel(
    per, pooled_ref, in_ref, ghc_ref, w_ref, dst_ref, own_ref, back_ref, dz_ref, du_ref, agg_ref,
    gw_ref, gb_ref, part_ref,
):
    pooled = pooled_ref[...]
    coarse, width = pooled.shape
    edges = per * LANES
    dqs = []
    gb = jnp.zeros((1, width), f32)
    for t in range(coarse // TILE):
        dst = row_form(dst_ref, t * per, per)
        dq = mm(hot_rows(dst, TILE), dz_ref[t * edges : (t + 1) * edges, :])
        gb = gb + jnp.sum(dq, axis=0, keepdims=True)
        dqs.append(dq.astype(bf))
    dq = jnp.concatenate(dqs, axis=0)
    du = du_ref[...]
    gb_ref[...] = jnp.broadcast_to(gb, gb_ref.shape)
    gw_ref[0:width, :] = (mm_tn(pooled, own_ref[...]) + mm_tn(in_ref[...], back_ref[...])).astype(bf)
    gw_ref[width : 2 * width, :] = mm_tn(pooled, dq).astype(bf)
    gw_ref[2 * width : 3 * width, :] = mm_tn(agg_ref[...], du).astype(bf)
    gw_ref[3 * width : 4 * width, :] = mm_tn(pooled, du).astype(bf)
    part_ref[...] = ghc_ref[...] + mm_nt(du, w_ref[3]) + mm_nt(dq, w_ref[1])


def node_back_kernel(
    own_ref, ret_ref, send_ref, part_ref, wc_ref, count_ref, pool_ref, cot_ref, dsu_ref, w_ref,
    g_ref, du_ref, dagg_ref,
):
    coarse = own_ref.shape[0]
    sends = hot_rows(row_form(send_ref, 0, send_ref.shape[0]), coarse)
    dp = (own_ref[...].astype(f32) + mm(sends, ret_ref[...])).astype(bf)
    dc = part_ref[...] + mm_nt(dp, wc_ref[0])
    count = count_ref[...]
    dcs = (dc / jnp.concatenate([count, count], axis=1)).astype(bf)
    hot = hot_rows(row_form(pool_ref, 0, pool_ref.shape[0]), coarse)
    g = cot_ref[...].astype(f32) + mm_tn(hot, dcs)
    g_ref[...] = g
    du = (g * dsu_ref[...].astype(f32)).astype(bf)
    du_ref[...] = du
    dagg_ref[...] = mm_nt(du, w_ref[2]).astype(bf)


def edge_back_kernel(
    per, group, core_ref, d_ref, he_ref, dagg_ref, h_ref, dst_ref, gwc_ref, gbc_ref, agg_ref, du_ref,
    dz_ref, dq_ref, mine_ref, other_ref, gb, gw0,
):
    step = pl.program_id(0)
    width = h_ref.shape[1]
    edges = per * LANES

    @pl.when(step == 0)
    def _():
        gb[...] = jnp.zeros_like(gb)
        gw0[...] = jnp.zeros_like(gw0)

    def tile(k, slot):
        t = step * group + k
        hot = hot_rows(row_form(dst_ref, t * per, per), TILE)
        rows = tile_rows(t, TILE)
        here = tile_rows(k, edges)
        gm = mm_tn(hot, dagg_ref[rows, :])
        dz = (gm * d_ref[here, :].astype(f32)).astype(bf)
        dz_ref[here, :] = dz
        dq = mm(hot, dz)
        gb[...] += jnp.sum(dq, axis=0, keepdims=True)
        dq_ref[rows, :] = dq.astype(bf)

    tile_loop(group, EDGE_UNROLL, tile)
    gw0[...] += mm_tn(he_ref[...], dz_ref[...])

    @pl.when(step == pl.num_programs(0) - 1)
    def _():
        gbf = jnp.broadcast_to(gb[0:1, :], (16, width)).astype(bf)
        gbc = jnp.broadcast_to(gbc_ref[0:1, :], (16, width)).astype(bf)
        h = h_ref[...]
        gw1 = mm_tn(h, dq_ref[...]).astype(bf)
        gw2 = mm_tn(agg_ref[...], du_ref[...]).astype(bf)
        gw3 = mm_tn(h, du_ref[...]).astype(bf)
        half0 = [gwc_ref[0 : 2 * width, :], gw0[...].astype(bf), gw1] + [gbf] * 4
        half1 = [gwc_ref[2 * width : 4 * width, :], gw2, gw3] + [gbc] * 4
        by_core(core_ref, mine_ref, other_ref, half0, half1)


def scatter_kernel(per, group, src_ref, dz_ref, own_ref, gl_ref, gr_ref, dzs, *accs):
    step = pl.program_id(0)
    nodes = own_ref.shape[0]
    halo = gl_ref.shape[0]
    edges = per * LANES

    @pl.when(step == 0)
    def _():
        for acc in accs:
            acc[...] = jnp.zeros_like(acc)

    def tile(k, slot):
        t = step * group + k
        to_pairs(dzs, 0, dz_ref[tile_rows(k, edges), :].astype(f32))
        for e in range(edges):
            acc = accs[e % len(accs)]
            at = pair(src_ref[t * edges + e])
            acc[at, :] = acc[at, :] + dzs[2 * e : 2 * e + 2, :]

    tile_loop(group, 1, tile)

    @pl.when(step == pl.num_programs(0) - 1)
    def _():
        def summed(first, n):
            total = from_pairs(accs[0], first, n)
            for acc in accs[1:]:
                total = total + from_pairs(acc, first, n)
            return total.astype(bf)

        own_ref[...] = summed(0, nodes)
        gl_ref[...] = summed(nodes, halo)
        gr_ref[...] = summed(nodes + halo, halo)


def part_kernel(dq_ref, du_ref, g_ref, w_ref, part_ref):
    part_ref[...] = (
        g_ref[...] + mm_nt(du_ref[...], w_ref[3]) + mm_nt(dq_ref[...], w_ref[1])
    )


def input_kernel(own_ref, from_right_ref, from_left_ref, right_ref, left_ref, part_ref, w_ref, o_ref):
    nodes = own_ref.shape[0]
    n = right_ref.shape[0]
    add = mm(hot_rows(row_form(right_ref, 0, n), nodes), from_right_ref[...]) + mm(
        hot_rows(row_form(left_ref, 0, n), nodes), from_left_ref[...]
    )
    dp = (own_ref[...].astype(f32) + add).astype(bf)
    o_ref[...] = part_ref[...] + mm_nt(dp, w_ref[0])


def finish_kernel(scale, core_ref, a_ref, ax_ref, gf_ref, gc_ref, gb_ref):
    two = gf_ref.shape[0] // 2

    def write(half, src):
        rows = slice(half * two, (half + 1) * two)
        gc_ref[rows, :] = src[0:two, :].astype(f32) * scale
        gf_ref[rows, :] = src[two : 2 * two, :].astype(f32) * scale
        gb_ref[half : half + 1, :] = src[2 * two : 2 * two + 16, :].astype(f32)[0:1] * scale

    core = core_ref[0]

    @pl.when(core == 0)
    def _():
        write(0, a_ref)
        write(1, ax_ref)

    @pl.when(core != 0)
    def _():
        write(1, a_ref)
        write(0, ax_ref)


def shifted(block, axis, distance):
    devices = range(lax.axis_size(axis))
    route = [(i - distance, i) for i in devices if i - distance in devices]
    return lax.ppermute(block, axis, route)


def swapped(block, parts, bit):
    return lax.ppermute(block, "dom", [(i, i ^ bit) for i in range(parts)])


def exchange(block, parts):
    rows, width = block.shape
    got = lax.all_to_all(
        block.reshape(parts, rows // parts, width), "dom", split_axis=0, concat_axis=0, tiled=True
    )
    return got


def add(a, b):
    return (a.astype(f32) + b.astype(f32)).astype(bf)


def over_chips(blocks, groups):
    return lax.all_to_all(blocks, "dom", 0, 0, axis_index_groups=groups, tiled=True)


def shards(
    features, cotangent, w_fine, w_coarse, bias, fine_src, fine_dst, send_left, send_right,
    pool_map, coarse_src, coarse_dst, coarse_send,
):
    nodes, width = features.shape
    parts = lax.axis_size("dom")
    coarse = nodes // 4
    tiles = nodes // TILE
    halo = send_left.shape[0]
    per = fine_src.shape[0] // tiles // LANES
    edges = per * LANES
    fsrc, fdst = fine_src.reshape(-1, LANES), fine_dst.reshape(-1, LANES)
    csrc, cdst = coarse_src.reshape(-1, LANES), coarse_dst.reshape(-1, LANES)
    right, left = send_right.reshape(-1, LANES), send_left.reshape(-1, LANES)
    pool = pool_map.reshape(-1, LANES)
    csend = coarse_send.reshape(-1, LANES)
    crows = coarse_send.shape[0] * coarse_send.shape[1]
    part = functools.partial
    core = (lax.axis_index("dom") % 2).astype(jnp.int32).reshape(1)
    same_core = [list(range(c, parts, 2)) for c in range(2)]
    chips = parts // 2
    group = 4
    steps = tiles // group

    to_right, to_left = call(
        halo_kernel, [sds((halo, width), bf)] * 2, [features, right, left]
    )
    h_left = shifted(to_right, "dom", 1)
    h_right = shifted(to_left, "dom", -1)
    edge_tile = pl.BlockSpec((group * edges, width), lambda t: (t, 0))
    smem = pl.BlockSpec(memory_space=pltpu.SMEM)
    ext_pairs = 2 * (nodes + 2 * halo)
    d_edge, he, agg, dsu, pooled, outgoing, count = call(
        part(fine_kernel, per, group),
        [
            sds((tiles * edges, width), bf),
            sds((tiles * edges, width), bf),
            sds((nodes, width), bf),
            sds((nodes, width), bf),
            sds((coarse, width), bf),
            sds((crows, width), bf),
            sds((coarse, LANES), f32),
        ],
        [fine_src, h_left, h_right, features, w_fine, bias, fdst, pool, csend],
        grid=(steps,),
        specs={0: smem},
        out_specs={0: edge_tile, 1: edge_tile},
        scratch=[
            pltpu.VMEM((nodes, width), bf),
            pltpu.VMEM((ext_pairs, LANES), f32),
            pltpu.VMEM((2 * FINE_UNROLL * edges, LANES), f32),
        ],
    )
    incoming = exchange(outgoing, parts).reshape(crows, width)
    cedges = coarse_src.shape[0]
    zc, ghc, uc = call(
        part(coarse_own_kernel, per),
        [sds((cedges, width), f32), sds((coarse, width), f32), sds((coarse, width), f32)],
        [pooled, w_coarse, bias, csrc, cdst, pool, cotangent],
        cost=(4e9, 10e6),
    )
    own_c, back_c, dz_c, du_c, agg_c = call(
        part(coarse_kernel, per),
        [
            sds((coarse, width), bf),
            sds((crows, width), bf),
            sds((cedges, width), bf),
            sds((coarse, width), bf),
            sds((coarse, width), bf),
        ],
        [zc, incoming, ghc, uc, w_coarse, csrc, cdst],
        scratch=[pltpu.VMEM((cedges, width), f32)],
    )
    returned = exchange(back_c, parts).reshape(crows, width)
    gw_c, gb_c, part_c = call(
        part(coarse_grad_kernel, per),
        [sds((4 * width, width), bf), sds((8, width), f32), sds((coarse, width), f32)],
        [pooled, incoming, ghc, w_coarse, cdst, own_c, back_c, dz_c, du_c, agg_c],
        cost=(4e9, 10e6),
    )
    g, du, dagg = call(
        node_back_kernel,
        [sds((nodes, width), f32), sds((nodes, width), bf), sds((nodes, width), bf)],
        [own_c, returned, csend, part_c, w_coarse, count, pool, cotangent, dsu, w_fine],
        cost=(6e9, 10e6),
    )
    half_rows = 4 * width + 64
    dz, dq, mine, other = call(
        part(edge_back_kernel, per, group),
        [
            sds((tiles * edges, width), bf),
            sds((nodes, width), bf),
            sds((half_rows, width), bf),
            sds((half_rows, width), bf),
        ],
        [core, d_edge, he, dagg, features, fdst, gw_c, gb_c, agg, du],
        grid=(steps,),
        specs={0: smem, 1: edge_tile, 2: edge_tile},
        out_specs={0: edge_tile},
        scratch=[pltpu.VMEM((8, width), f32), pltpu.VMEM((width, width), f32)],
        cost=(15e9, 10e6),
    )
    sums = add(mine, swapped(other, parts, 1)).reshape(chips, -1, width)
    sums, dz = lax.optimization_barrier((sums, dz))
    sums = over_chips(sums, same_core)
    own_f, gl, gr = call(
        part(scatter_kernel, per, group),
        [sds((nodes, width), bf), sds((halo, width), bf), sds((halo, width), bf)],
        [fine_src, dz],
        grid=(steps,),
        specs={0: smem, 1: edge_tile},
        scratch=[pltpu.VMEM((2 * edges, LANES), f32)]
        + [pltpu.VMEM((ext_pairs, LANES), f32)] * 6,
        cost=(15e9, 10e6),
    )
    sums, own_f, gl, gr = lax.optimization_barrier((sums, own_f, gl, gr))
    sums = jnp.sum(sums.astype(f32), axis=0).astype(bf)
    sums = over_chips(jnp.broadcast_to(sums[None], (chips,) + sums.shape), same_core)
    from_right = shifted(gl, "dom", -1)
    from_left = shifted(gr, "dom", 1)
    (part_f,) = call(
        part_kernel, [sds((nodes, width), f32)], [dq, du, g, w_fine], cost=(4e9, 10e6)
    )
    (grad_input,) = call(
        input_kernel,
        [sds((nodes, width), f32)],
        [own_f, from_right, from_left, right, left, part_f, w_fine],
        cost=(4e9, 10e6),
    )
    sums, grad_input = lax.optimization_barrier((sums, grad_input))
    sums = sums.reshape(half_rows, width)
    scale = 1.0 / float(nodes * parts // 256)
    grad_fine, grad_coarse, grad_bias = call(
        part(finish_kernel, scale),
        [sds((4 * width, width), f32), sds((4 * width, width), f32), sds((2, width), f32)],
        [core, sums, swapped(sums, parts, 1)],
        specs={0: smem},
    )
    shape = (4, width, width)
    return (grad_input, grad_fine.reshape(shape), grad_coarse.reshape(shape), grad_bias)


def solution(mesh):
    return jax.shard_map(
        shards,
        mesh=mesh,
        in_specs=(
            P(("groups", "dom"), None),
            P(("groups", "dom"), None),
            P(),
            P(),
            P(),
            P("dom"),
            P("dom"),
            P("dom"),
            P("dom"),
            P("dom"),
            P("dom"),
            P("dom"),
            P("dom", None),
        ),
        out_specs=(
            P(("groups", "dom"), None),
            P("groups", None, None),
            P("groups", None, None),
            P("groups", None),
        ),
        check_vma=False,
    )
```

```python
import functools

import jax
import jax.numpy as jnp
from jax import lax
from jax.experimental import pallas as pl
from jax.experimental.pallas import tpu as pltpu
from jax.sharding import PartitionSpec as P

bf = jnp.bfloat16
f32 = jnp.float32
TILE = 128
LANES = 128
FINE_UNROLL = 4
EDGE_UNROLL = 4


def mm(a, b):
    return jnp.dot(a, b, preferred_element_type=f32)


def mm_tn(a, b):
    return lax.dot_general(a, b, (((0,), (0,)), ((), ())), preferred_element_type=f32)


def mm_nt(a, b):
    return lax.dot_general(a, b, (((1,), (1,)), ((), ())), preferred_element_type=f32)


def as_bf(x):
    return x.astype(f32).astype(bf)


def row_form(ref, first, count):
    return jnp.concatenate([ref[pl.ds(first + j, 1), :] for j in range(count)], axis=1)


def hot_rows(row, rows):
    cols = row.shape[1]
    if rows <= 256:
        io = as_bf(lax.broadcasted_iota(jnp.int32, (rows, cols), 0))
        return jnp.where(io == as_bf(row), bf(1), bf(0))
    low = as_bf(row & 255)
    high = as_bf(lax.shift_right_arithmetic(row, 8))
    io = as_bf(lax.broadcasted_iota(jnp.int32, (256, cols), 0))
    base = jnp.where(io == low, bf(1), bf(0))
    return jnp.concatenate(
        [jnp.where(high == bf(k), base, bf(0)) for k in range(rows // 256)], axis=0
    )


def tile_loop(group, unroll, body):
    if group == unroll:
        for k in range(group):
            body(k, k)
    else:

        def step(j, carry):
            for k in range(unroll):
                body(j * unroll + k, k)
            return carry

        lax.fori_loop(0, group // unroll, step, 0)


def tile_rows(index, size):
    return pl.ds(pl.multiple_of(index * size, size), size)


def silu_parts(v):
    sig = 0.5 * jnp.tanh(0.5 * v) + 0.5
    silu = v * sig
    return silu, sig + silu * (1.0 - sig)


def to_pairs(ref, first, rows):
    n = rows.shape[0]
    for j in range(2):
        ref[pl.ds(2 * first + j, n, stride=2), :] = rows[:, j * LANES : (j + 1) * LANES]


def from_pairs(ref, first, n):
    return jnp.concatenate([ref[pl.ds(2 * first + j, n, stride=2), :] for j in range(2)], axis=1)


def pair(index):
    return pl.ds(pl.multiple_of(index * 2, 2), 2)


def call(kernel, outs, args, grid=(), specs=None, out_specs=None, scratch=(), us=1.0, near=(), near_out=()):
    specs = specs or {}
    args = [
        a
        if k in near or getattr(specs.get(k), "memory_space", None) == pltpu.SMEM
        else pltpu.with_memory_space_constraint(a, pltpu.HBM)
        for k, a in enumerate(args)
    ]
    def whole(a):
        return pl.BlockSpec(a.shape, lambda *_: (0,) * len(a.shape))

    in_specs = [whole(a) for a in args]
    o_specs = [whole(o) for o in outs]
    for k, s in specs.items():
        in_specs[k] = s
    for k, s in (out_specs or {}).items():
        o_specs[k] = s
    return pl.pallas_call(
        kernel,
        grid=grid or (1,),
        in_specs=in_specs,
        out_specs=o_specs,
        out_shape=[o if k in near_out else pltpu.HBM(o.shape, o.dtype) for k, o in enumerate(outs)],
        scratch_shapes=list(scratch),
        compiler_params=pltpu.CompilerParams(vmem_limit_bytes=24 << 20),
        cost_estimate=pl.CostEstimate(
            flops=int(us * 1e9), bytes_accessed=1 << 20, transcendentals=0
        ),
    )(*args)


def sds(shape, dtype):
    return jax.ShapeDtypeStruct(shape, dtype)


def halo_kernel(h_ref, right_ref, left_ref, to_right_ref, to_left_ref):
    h = h_ref[...]
    n = right_ref.shape[0]
    to_right_ref[...] = mm_tn(hot_rows(row_form(right_ref, 0, n), h.shape[0]), h).astype(bf)
    to_left_ref[...] = mm_tn(hot_rows(row_form(left_ref, 0, n), h.shape[0]), h).astype(bf)


def fine_kernel(
    per, group, src_ref, left_ref, right_ref, h_ref, w_ref, b_ref, dst_ref, pool_ref, send_ref,
    d_ref, he_ref, agg_ref, dsu_ref, pooled_ref, out_ref, count_ref, recv, table, taken,
):
    step = pl.program_id(0)
    nodes = h_ref.shape[0]
    halo = left_ref.shape[0]
    edges = per * LANES

    @pl.when(step == 0)
    def _():
        recv[...] = mm(h_ref[...], w_ref[1]).astype(bf)
        to_pairs(table, 0, h_ref[...].astype(f32))
        to_pairs(table, nodes, left_ref[...].astype(f32))
        to_pairs(table, nodes + halo, right_ref[...].astype(f32))

    def tile(k, slot):
        t = step * group + k
        for e in range(edges):
            at = 2 * (slot * edges + e)
            taken[at : at + 2, :] = table[pair(src_ref[t * edges + e]), :]
        rows = tile_rows(t, TILE)
        hot = hot_rows(row_form(dst_ref, t * per, per), TILE)
        he = from_pairs(taken, slot * edges, edges).astype(bf)
        he_ref[tile_rows(k, edges), :] = he
        sent = as_bf(mm(he, w_ref[0])).astype(f32)
        z = sent + mm_tn(hot, recv[rows, :]) + b_ref[0:1, :]
        m, d = silu_parts(z)
        d_ref[tile_rows(k, edges), :] = d.astype(bf)
        agg_ref[rows, :] = mm(hot, m.astype(bf)).astype(bf)

    tile_loop(group, FINE_UNROLL, tile)

    @pl.when(step == pl.num_programs(0) - 1)
    def _():
        h = h_ref[...]
        u = mm(h, w_ref[3]) + mm(agg_ref[...], w_ref[2])
        su, dsu = silu_parts(u)
        dsu_ref[...] = dsu.astype(bf)
        h1 = (h.astype(f32) + su).astype(bf)
        coarse = pooled_ref.shape[0]
        hot = hot_rows(row_form(pool_ref, 0, pool_ref.shape[0]), coarse)
        count = mm(hot, jnp.ones((nodes, LANES), bf))
        count_ref[...] = count
        pooled = (mm(hot, h1) / jnp.concatenate([count, count], axis=1)).astype(bf)
        pooled_ref[...] = pooled
        sends = hot_rows(row_form(send_ref, 0, send_ref.shape[0]), coarse)
        out_ref[...] = mm_tn(sends, pooled).astype(bf)


def coarse_own_kernel(
    per, pooled_ref, w_ref, b_ref, src_ref, dst_ref, pool_ref, cot_ref, z_ref, ghc_ref, u_ref
):
    pooled = pooled_ref[...]
    coarse = pooled.shape[0]
    proj = mm(pooled, w_ref[0]).astype(bf)
    recv = mm(pooled, w_ref[1]).astype(bf)
    u_ref[...] = mm(pooled, w_ref[3])
    edges = per * LANES
    for t in range(coarse // TILE):
        src = row_form(src_ref, t * per, per)
        dst = row_form(dst_ref, t * per, per)
        z_ref[t * edges : (t + 1) * edges, :] = (
            mm_tn(hot_rows(src, coarse), proj)
            + mm_tn(hot_rows(dst, TILE), recv[t * TILE : (t + 1) * TILE, :])
            + b_ref[1:2, :]
        )
    hot = hot_rows(row_form(pool_ref, 0, pool_ref.shape[0]), coarse)
    ghc_ref[...] = mm(hot, cot_ref[...])


def coarse_kernel(
    per, z_ref, in_ref, ghc_ref, u_ref, w_ref, src_ref, dst_ref,
    own_ref, back_ref, dz_ref, du_ref, agg_ref, deriv,
):
    coarse = ghc_ref.shape[0]
    edges = per * LANES
    tiles = coarse // TILE
    proj = mm(in_ref[...], w_ref[0]).astype(bf)
    for t in range(tiles):
        src = row_form(src_ref, t * per, per) - coarse
        dst = row_form(dst_ref, t * per, per)
        z = z_ref[t * edges : (t + 1) * edges, :] + mm_tn(hot_rows(src, proj.shape[0]), proj)
        m, d = silu_parts(z)
        deriv[t * edges : (t + 1) * edges, :] = d
        agg_ref[t * TILE : (t + 1) * TILE, :] = mm(hot_rows(dst, TILE), m.astype(bf)).astype(bf)
    u = u_ref[...] + mm(agg_ref[...], w_ref[2])
    _, dsu = silu_parts(u)
    du = (ghc_ref[...] * dsu).astype(bf)
    du_ref[...] = du
    dagg = mm_nt(du, w_ref[2]).astype(bf)
    total = None
    for t in range(tiles):
        src = row_form(src_ref, t * per, per)
        dst = row_form(dst_ref, t * per, per)
        gm = mm_tn(hot_rows(dst, TILE), dagg[t * TILE : (t + 1) * TILE, :])
        dz = (gm * deriv[t * edges : (t + 1) * edges, :]).astype(bf)
        dz_ref[t * edges : (t + 1) * edges, :] = dz
        part = mm(hot_rows(src, coarse + proj.shape[0]), dz)
        total = part if total is None else total + part
    own_ref[...] = total[:coarse].astype(bf)
    back_ref[...] = total[coarse:].astype(bf)


def by_core(core_ref, mine_ref, other_ref, half0, half1):
    core = core_ref[0]

    def write(ref, half):
        at = 0
        for piece in half:
            ref[at : at + piece.shape[0], :] = piece
            at += piece.shape[0]

    @pl.when(core == 0)
    def _():
        write(mine_ref, half0)
        write(other_ref, half1)

    @pl.when(core != 0)
    def _():
        write(mine_ref, half1)
        write(other_ref, half0)


def coarse_grad_kernel(
    per, pooled_ref, in_ref, ghc_ref, w_ref, dst_ref, own_ref, back_ref, dz_ref, du_ref, agg_ref,
    gw_ref, gb_ref, part_ref,
):
    pooled = pooled_ref[...]
    coarse, width = pooled.shape
    edges = per * LANES
    dqs = []
    gb = jnp.zeros((1, width), f32)
    for t in range(coarse // TILE):
        dst = row_form(dst_ref, t * per, per)
        dq = mm(hot_rows(dst, TILE), dz_ref[t * edges : (t + 1) * edges, :])
        gb = gb + jnp.sum(dq, axis=0, keepdims=True)
        dqs.append(dq.astype(bf))
    dq = jnp.concatenate(dqs, axis=0)
    du = du_ref[...]
    gb_ref[...] = jnp.broadcast_to(gb, gb_ref.shape)
    gw_ref[0:width, :] = (mm_tn(pooled, own_ref[...]) + mm_tn(in_ref[...], back_ref[...])).astype(bf)
    gw_ref[width : 2 * width, :] = mm_tn(pooled, dq).astype(bf)
    gw_ref[2 * width : 3 * width, :] = mm_tn(agg_ref[...], du).astype(bf)
    gw_ref[3 * width : 4 * width, :] = mm_tn(pooled, du).astype(bf)
    part_ref[...] = ghc_ref[...] + mm_nt(du, w_ref[3]) + mm_nt(dq, w_ref[1])


def node_back_kernel(
    own_ref, ret_ref, send_ref, part_ref, wc_ref, count_ref, pool_ref, cot_ref, dsu_ref, w_ref,
    g_ref, du_ref, dagg_ref,
):
    coarse = own_ref.shape[0]
    sends = hot_rows(row_form(send_ref, 0, send_ref.shape[0]), coarse)
    dp = (own_ref[...].astype(f32) + mm(sends, ret_ref[...])).astype(bf)
    dc = part_ref[...] + mm_nt(dp, wc_ref[0])
    count = count_ref[...]
    dcs = (dc / jnp.concatenate([count, count], axis=1)).astype(bf)
    hot = hot_rows(row_form(pool_ref, 0, pool_ref.shape[0]), coarse)
    g = cot_ref[...].astype(f32) + mm_tn(hot, dcs)
    g_ref[...] = g
    du = (g * dsu_ref[...].astype(f32)).astype(bf)
    du_ref[...] = du
    dagg_ref[...] = mm_nt(du, w_ref[2]).astype(bf)


def edge_back_kernel(
    per, group, core_ref, d_ref, he_ref, dagg_ref, h_ref, dst_ref, gwc_ref, gbc_ref, agg_ref, du_ref,
    dz_ref, dq_ref, mine_ref, other_ref, gb, gw0,
):
    step = pl.program_id(0)
    width = h_ref.shape[1]
    edges = per * LANES

    @pl.when(step == 0)
    def _():
        gb[...] = jnp.zeros_like(gb)
        gw0[...] = jnp.zeros_like(gw0)

    def tile(k, slot):
        t = step * group + k
        hot = hot_rows(row_form(dst_ref, t * per, per), TILE)
        rows = tile_rows(t, TILE)
        here = tile_rows(k, edges)
        gm = mm_tn(hot, dagg_ref[rows, :])
        dz = (gm * d_ref[here, :].astype(f32)).astype(bf)
        dz_ref[here, :] = dz
        dq = mm(hot, dz)
        gb[...] += jnp.sum(dq, axis=0, keepdims=True)
        dq_ref[rows, :] = dq.astype(bf)

    tile_loop(group, EDGE_UNROLL, tile)
    gw0[...] += mm_tn(he_ref[...], dz_ref[...])

    @pl.when(step == pl.num_programs(0) - 1)
    def _():
        gbf = jnp.broadcast_to(gb[0:1, :], (16, width)).astype(bf)
        gbc = jnp.broadcast_to(gbc_ref[0:1, :], (16, width)).astype(bf)
        h = h_ref[...]
        gw1 = mm_tn(h, dq_ref[...]).astype(bf)
        gw2 = mm_tn(agg_ref[...], du_ref[...]).astype(bf)
        gw3 = mm_tn(h, du_ref[...]).astype(bf)
        half0 = [gwc_ref[0 : 2 * width, :], gw0[...].astype(bf), gw1] + [gbf] * 4
        half1 = [gwc_ref[2 * width : 4 * width, :], gw2, gw3] + [gbc] * 4
        by_core(core_ref, mine_ref, other_ref, half0, half1)


def scatter_kernel(per, group, src_ref, dz_ref, own_ref, gl_ref, gr_ref, dzs, *accs):
    step = pl.program_id(0)
    nodes = own_ref.shape[0]
    halo = gl_ref.shape[0]
    edges = per * LANES

    @pl.when(step == 0)
    def _():
        for acc in accs:
            acc[...] = jnp.zeros_like(acc)

    def tile(k, slot):
        t = step * group + k
        to_pairs(dzs, 0, dz_ref[tile_rows(k, edges), :].astype(f32))
        for e in range(edges):
            acc = accs[e % len(accs)]
            at = pair(src_ref[t * edges + e])
            acc[at, :] = acc[at, :] + dzs[2 * e : 2 * e + 2, :]

    tile_loop(group, 1, tile)

    @pl.when(step == pl.num_programs(0) - 1)
    def _():
        def summed(first, n):
            total = from_pairs(accs[0], first, n)
            for acc in accs[1:]:
                total = total + from_pairs(acc, first, n)
            return total.astype(bf)

        own_ref[...] = summed(0, nodes)
        gl_ref[...] = summed(nodes, halo)
        gr_ref[...] = summed(nodes + halo, halo)


def part_kernel(dq_ref, du_ref, g_ref, w_ref, part_ref):
    part_ref[...] = (
        g_ref[...] + mm_nt(du_ref[...], w_ref[3]) + mm_nt(dq_ref[...], w_ref[1])
    )


def input_kernel(own_ref, from_right_ref, from_left_ref, right_ref, left_ref, part_ref, w_ref, o_ref):
    nodes = own_ref.shape[0]
    n = right_ref.shape[0]
    add = mm(hot_rows(row_form(right_ref, 0, n), nodes), from_right_ref[...]) + mm(
        hot_rows(row_form(left_ref, 0, n), nodes), from_left_ref[...]
    )
    dp = (own_ref[...].astype(f32) + add).astype(bf)
    o_ref[...] = part_ref[...] + mm_nt(dp, w_ref[0])


def finish_kernel(scale, core_ref, a_ref, ax_ref, gf_ref, gc_ref, gb_ref):
    two = gf_ref.shape[0] // 2

    def write(half, src):
        rows = slice(half * two, (half + 1) * two)
        gc_ref[rows, :] = src[0:two, :].astype(f32) * scale
        gf_ref[rows, :] = src[two : 2 * two, :].astype(f32) * scale
        gb_ref[half : half + 1, :] = src[2 * two : 2 * two + 16, :].astype(f32)[0:1] * scale

    core = core_ref[0]

    @pl.when(core == 0)
    def _():
        write(0, a_ref)
        write(1, ax_ref)

    @pl.when(core != 0)
    def _():
        write(1, a_ref)
        write(0, ax_ref)


def shifted(block, axis, distance):
    devices = range(lax.axis_size(axis))
    route = [(i - distance, i) for i in devices if i - distance in devices]
    return lax.ppermute(block, axis, route)


def swapped(block, parts, bit):
    return lax.ppermute(block, "dom", [(i, i ^ bit) for i in range(parts)])


def exchange(block, parts):
    rows, width = block.shape
    got = lax.all_to_all(
        block.reshape(parts, rows // parts, width), "dom", split_axis=0, concat_axis=0, tiled=True
    )
    return got


def add(a, b):
    return (a.astype(f32) + b.astype(f32)).astype(bf)


def over_chips(blocks, groups):
    return lax.all_to_all(blocks, "dom", 0, 0, axis_index_groups=groups, tiled=True)


def shards(
    features, cotangent, w_fine, w_coarse, bias, fine_src, fine_dst, send_left, send_right,
    pool_map, coarse_src, coarse_dst, coarse_send,
):
    nodes, width = features.shape
    parts = lax.axis_size("dom")
    coarse = nodes // 4
    tiles = nodes // TILE
    halo = send_left.shape[0]
    per = fine_src.shape[0] // tiles // LANES
    edges = per * LANES
    fsrc, fdst = fine_src.reshape(-1, LANES), fine_dst.reshape(-1, LANES)
    csrc, cdst = coarse_src.reshape(-1, LANES), coarse_dst.reshape(-1, LANES)
    right, left = send_right.reshape(-1, LANES), send_left.reshape(-1, LANES)
    pool = pool_map.reshape(-1, LANES)
    csend = coarse_send.reshape(-1, LANES)
    crows = coarse_send.shape[0] * coarse_send.shape[1]
    part = functools.partial
    core = (lax.axis_index("dom") % 2).astype(jnp.int32).reshape(1)
    same_core = [list(range(c, parts, 2)) for c in range(2)]
    chips = parts // 2
    group = 4
    steps = tiles // group

    to_right, to_left = call(
        halo_kernel, [sds((halo, width), bf)] * 2, [features, right, left],
        us=0.8, near_out=(0, 1),
    )
    h_left = shifted(to_right, "dom", 1)
    h_right = shifted(to_left, "dom", -1)
    edge_tile = pl.BlockSpec((group * edges, width), lambda t: (t, 0))
    smem = pl.BlockSpec(memory_space=pltpu.SMEM)
    ext_pairs = 2 * (nodes + 2 * halo)
    d_edge, he, agg, dsu, pooled, outgoing, count = call(
        part(fine_kernel, per, group),
        [
            sds((tiles * edges, width), bf),
            sds((tiles * edges, width), bf),
            sds((nodes, width), bf),
            sds((nodes, width), bf),
            sds((coarse, width), bf),
            sds((crows, width), bf),
            sds((coarse, LANES), f32),
        ],
        [fine_src, h_left, h_right, features, w_fine, bias, fdst, pool, csend],
        grid=(steps,),
        specs={0: smem},
        out_specs={0: edge_tile, 1: edge_tile},
        scratch=[
            pltpu.VMEM((nodes, width), bf),
            pltpu.VMEM((ext_pairs, LANES), f32),
            pltpu.VMEM((2 * FINE_UNROLL * edges, LANES), f32),
        ],
        us=18, near=(1, 2), near_out=(5,),
    )
    incoming = exchange(outgoing, parts).reshape(crows, width)
    cedges = coarse_src.shape[0]
    zc, ghc, uc = call(
        part(coarse_own_kernel, per),
        [sds((cedges, width), f32), sds((coarse, width), f32), sds((coarse, width), f32)],
        [pooled, w_coarse, bias, csrc, cdst, pool, cotangent],
        us=2, near_out=(1, 2),
    )
    own_c, back_c, dz_c, du_c, agg_c = call(
        part(coarse_kernel, per),
        [
            sds((coarse, width), bf),
            sds((crows, width), bf),
            sds((cedges, width), bf),
            sds((coarse, width), bf),
            sds((coarse, width), bf),
        ],
        [zc, incoming, ghc, uc, w_coarse, csrc, cdst],
        scratch=[pltpu.VMEM((cedges, width), f32)],
        us=4.7, near=(1, 2, 3), near_out=(1,),
    )
    returned = exchange(back_c, parts).reshape(crows, width)
    gw_c, gb_c, part_c = call(
        part(coarse_grad_kernel, per),
        [sds((4 * width, width), bf), sds((8, width), f32), sds((coarse, width), f32)],
        [pooled, incoming, ghc, w_coarse, cdst, own_c, back_c, dz_c, du_c, agg_c],
        us=1, near=(1, 2), near_out=(1,),
    )
    g, du, dagg = call(
        node_back_kernel,
        [sds((nodes, width), f32), sds((nodes, width), bf), sds((nodes, width), bf)],
        [own_c, returned, csend, part_c, w_coarse, count, pool, cotangent, dsu, w_fine],
        us=1.6, near=(1,), near_out=(2,),
    )
    half_rows = 4 * width + 64
    dz, dq, mine, other = call(
        part(edge_back_kernel, per, group),
        [
            sds((tiles * edges, width), bf),
            sds((nodes, width), bf),
            sds((half_rows, width), bf),
            sds((half_rows, width), bf),
        ],
        [core, d_edge, he, dagg, features, fdst, gw_c, gb_c, agg, du],
        grid=(steps,),
        specs={0: smem, 1: edge_tile, 2: edge_tile},
        out_specs={0: edge_tile},
        scratch=[pltpu.VMEM((8, width), f32), pltpu.VMEM((width, width), f32)],
        us=8, near=(3,), near_out=(2, 3),
    )
    sums = add(mine, swapped(other, parts, 1)).reshape(chips, -1, width)
    sums, dz = lax.optimization_barrier((sums, dz))
    sums = over_chips(sums, same_core)
    own_f, gl, gr = call(
        part(scatter_kernel, per, group),
        [sds((nodes, width), bf), sds((halo, width), bf), sds((halo, width), bf)],
        [fine_src, dz],
        grid=(steps,),
        specs={0: smem, 1: edge_tile},
        scratch=[pltpu.VMEM((2 * edges, LANES), f32)]
        + [pltpu.VMEM((ext_pairs, LANES), f32)] * 6,
        us=12, near_out=(1, 2),
    )
    sums, own_f, gl, gr = lax.optimization_barrier((sums, own_f, gl, gr))
    sums = jnp.sum(sums.astype(f32), axis=0).astype(bf)
    sums = over_chips(jnp.broadcast_to(sums[None], (chips,) + sums.shape), same_core)
    from_right = shifted(gl, "dom", -1)
    from_left = shifted(gr, "dom", 1)
    (part_f,) = call(
        part_kernel, [sds((nodes, width), f32)], [dq, du, g, w_fine],
        us=0.8, near_out=(0,),
    )
    (grad_input,) = call(
        input_kernel,
        [sds((nodes, width), f32)],
        [own_f, from_right, from_left, right, left, part_f, w_fine],
        us=2.4, near=(1, 2, 5), near_out=(0,),
    )
    sums, grad_input = lax.optimization_barrier((sums, grad_input))
    sums = sums.reshape(half_rows, width)
    scale = 1.0 / float(nodes * parts // 256)
    grad_fine, grad_coarse, grad_bias = call(
        part(finish_kernel, scale),
        [sds((4 * width, width), f32), sds((4 * width, width), f32), sds((2, width), f32)],
        [core, sums, swapped(sums, parts, 1)],
        specs={0: smem},
        us=1.5, near=(1, 2), near_out=(0, 1, 2),
    )
    shape = (4, width, width)
    return (grad_input, grad_fine.reshape(shape), grad_coarse.reshape(shape), grad_bias)


def solution(mesh):
    return jax.shard_map(
        shards,
        mesh=mesh,
        in_specs=(
            P(("groups", "dom"), None),
            P(("groups", "dom"), None),
            P(),
            P(),
            P(),
            P("dom"),
            P("dom"),
            P("dom"),
            P("dom"),
            P("dom"),
            P("dom"),
            P("dom"),
            P("dom", None),
        ),
        out_specs=(
            P(("groups", "dom"), None),
            P("groups", None, None),
            P("groups", None, None),
            P("groups", None),
        ),
        check_vma=False,
    )
```

```python
import functools

import jax
import jax.numpy as jnp
from jax import lax
from jax.experimental import pallas as pl
from jax.experimental.pallas import tpu as pltpu
from jax.sharding import PartitionSpec as P

bf = jnp.bfloat16
f32 = jnp.float32
TILE = 128
LANES = 128
FINE_UNROLL = 4
EDGE_UNROLL = 4


def mm(a, b):
    return jnp.dot(a, b, preferred_element_type=f32)


def mm_tn(a, b):
    return lax.dot_general(a, b, (((0,), (0,)), ((), ())), preferred_element_type=f32)


def mm_nt(a, b):
    return lax.dot_general(a, b, (((1,), (1,)), ((), ())), preferred_element_type=f32)


def as_bf(x):
    return x.astype(f32).astype(bf)


def row_form(ref, first, count):
    return jnp.concatenate([ref[pl.ds(first + j, 1), :] for j in range(count)], axis=1)


def hot_rows(row, rows):
    cols = row.shape[1]
    if rows <= 256:
        io = as_bf(lax.broadcasted_iota(jnp.int32, (rows, cols), 0))
        return jnp.where(io == as_bf(row), bf(1), bf(0))
    low = as_bf(row & 255)
    high = as_bf(lax.shift_right_arithmetic(row, 8))
    io = as_bf(lax.broadcasted_iota(jnp.int32, (256, cols), 0))
    base = jnp.where(io == low, bf(1), bf(0))
    return jnp.concatenate(
        [jnp.where(high == bf(k), base, bf(0)) for k in range(rows // 256)], axis=0
    )


def tile_loop(group, unroll, body):
    if group == unroll:
        for k in range(group):
            body(k, k)
    else:

        def step(j, carry):
            for k in range(unroll):
                body(j * unroll + k, k)
            return carry

        lax.fori_loop(0, group // unroll, step, 0)


def tile_rows(index, size):
    return pl.ds(pl.multiple_of(index * size, size), size)


def silu_parts(v):
    sig = 0.5 * jnp.tanh(0.5 * v) + 0.5
    silu = v * sig
    return silu, sig + silu * (1.0 - sig)


def to_pairs(ref, first, rows):
    n = rows.shape[0]
    for j in range(2):
        ref[pl.ds(2 * first + j, n, stride=2), :] = rows[:, j * LANES : (j + 1) * LANES]


def from_pairs(ref, first, n):
    return jnp.concatenate([ref[pl.ds(2 * first + j, n, stride=2), :] for j in range(2)], axis=1)


def pair(index):
    return pl.ds(pl.multiple_of(index * 2, 2), 2)


def call(kernel, outs, args, grid=(), specs=None, out_specs=None, scratch=(), us=1.0, near=(), near_out=()):
    specs = specs or {}
    args = [
        a
        if k in near or getattr(specs.get(k), "memory_space", None) == pltpu.SMEM
        else pltpu.with_memory_space_constraint(a, pltpu.HBM)
        for k, a in enumerate(args)
    ]
    def whole(a):
        return pl.BlockSpec(a.shape, lambda *_: (0,) * len(a.shape))

    in_specs = [whole(a) for a in args]
    o_specs = [whole(o) for o in outs]
    for k, s in specs.items():
        in_specs[k] = s
    for k, s in (out_specs or {}).items():
        o_specs[k] = s
    return pl.pallas_call(
        kernel,
        grid=grid or (1,),
        in_specs=in_specs,
        out_specs=o_specs,
        out_shape=[o if k in near_out else pltpu.HBM(o.shape, o.dtype) for k, o in enumerate(outs)],
        scratch_shapes=list(scratch),
        compiler_params=pltpu.CompilerParams(vmem_limit_bytes=32 << 20),
        cost_estimate=pl.CostEstimate(
            flops=int(us * 1e9), bytes_accessed=1 << 20, transcendentals=0
        ),
    )(*args)


def sds(shape, dtype):
    return jax.ShapeDtypeStruct(shape, dtype)


def halo_kernel(h_ref, right_ref, left_ref, to_right_ref, to_left_ref):
    h = h_ref[...]
    n = right_ref.shape[0]
    to_right_ref[...] = mm_tn(hot_rows(row_form(right_ref, 0, n), h.shape[0]), h).astype(bf)
    to_left_ref[...] = mm_tn(hot_rows(row_form(left_ref, 0, n), h.shape[0]), h).astype(bf)


def fine_kernel(
    per, group, src_ref, left_ref, right_ref, h_ref, w_ref, b_ref, dst_ref, pool_ref, send_ref,
    d_ref, he_ref, agg_ref, dsu_ref, pooled_ref, out_ref, count_ref, recv, table, taken,
):
    step = pl.program_id(0)
    nodes = h_ref.shape[0]
    halo = left_ref.shape[0]
    edges = per * LANES

    @pl.when(step == 0)
    def _():
        recv[...] = mm(h_ref[...], w_ref[1]).astype(bf)
        to_pairs(table, 0, h_ref[...].astype(f32))
        to_pairs(table, nodes, left_ref[...].astype(f32))
        to_pairs(table, nodes + halo, right_ref[...].astype(f32))

    def tile(k, slot):
        t = step * group + k
        for e in range(edges):
            at = 2 * (slot * edges + e)
            taken[at : at + 2, :] = table[pair(src_ref[t * edges + e]), :]
        rows = tile_rows(t, TILE)
        hot = hot_rows(row_form(dst_ref, t * per, per), TILE)
        he = from_pairs(taken, slot * edges, edges).astype(bf)
        he_ref[tile_rows(k, edges), :] = he
        sent = as_bf(mm(he, w_ref[0])).astype(f32)
        z = sent + mm_tn(hot, recv[rows, :]) + b_ref[0:1, :]
        m, d = silu_parts(z)
        d_ref[tile_rows(k, edges), :] = d.astype(bf)
        agg_ref[rows, :] = mm(hot, m.astype(bf)).astype(bf)

    tile_loop(group, FINE_UNROLL, tile)

    @pl.when(step == pl.num_programs(0) - 1)
    def _():
        h = h_ref[...]
        u = mm(h, w_ref[3]) + mm(agg_ref[...], w_ref[2])
        su, dsu = silu_parts(u)
        dsu_ref[...] = dsu.astype(bf)
        h1 = (h.astype(f32) + su).astype(bf)
        coarse = pooled_ref.shape[0]
        hot = hot_rows(row_form(pool_ref, 0, pool_ref.shape[0]), coarse)
        count = mm(hot, jnp.ones((nodes, LANES), bf))
        count_ref[...] = count
        pooled = (mm(hot, h1) / jnp.concatenate([count, count], axis=1)).astype(bf)
        pooled_ref[...] = pooled
        sends = hot_rows(row_form(send_ref, 0, send_ref.shape[0]), coarse)
        out_ref[...] = mm_tn(sends, pooled).astype(bf)


def coarse_own_kernel(
    per, pooled_ref, w_ref, b_ref, src_ref, dst_ref, pool_ref, cot_ref, z_ref, ghc_ref, u_ref
):
    pooled = pooled_ref[...]
    coarse = pooled.shape[0]
    proj = mm(pooled, w_ref[0]).astype(bf)
    recv = mm(pooled, w_ref[1]).astype(bf)
    u_ref[...] = mm(pooled, w_ref[3])
    edges = per * LANES
    for t in range(coarse // TILE):
        src = row_form(src_ref, t * per, per)
        dst = row_form(dst_ref, t * per, per)
        z_ref[t * edges : (t + 1) * edges, :] = (
            mm_tn(hot_rows(src, coarse), proj)
            + mm_tn(hot_rows(dst, TILE), recv[t * TILE : (t + 1) * TILE, :])
            + b_ref[1:2, :]
        )
    hot = hot_rows(row_form(pool_ref, 0, pool_ref.shape[0]), coarse)
    ghc_ref[...] = mm(hot, cot_ref[...])


def coarse_kernel(
    per, z_ref, in_ref, ghc_ref, u_ref, w_ref, src_ref, dst_ref,
    own_ref, back_ref, dz_ref, du_ref, agg_ref, deriv,
):
    coarse = ghc_ref.shape[0]
    edges = per * LANES
    tiles = coarse // TILE
    proj = mm(in_ref[...], w_ref[0]).astype(bf)
    for t in range(tiles):
        src = row_form(src_ref, t * per, per) - coarse
        dst = row_form(dst_ref, t * per, per)
        z = z_ref[t * edges : (t + 1) * edges, :] + mm_tn(hot_rows(src, proj.shape[0]), proj)
        m, d = silu_parts(z)
        deriv[t * edges : (t + 1) * edges, :] = d
        agg_ref[t * TILE : (t + 1) * TILE, :] = mm(hot_rows(dst, TILE), m.astype(bf)).astype(bf)
    u = u_ref[...] + mm(agg_ref[...], w_ref[2])
    _, dsu = silu_parts(u)
    du = (ghc_ref[...] * dsu).astype(bf)
    du_ref[...] = du
    dagg = mm_nt(du, w_ref[2]).astype(bf)
    total = None
    for t in range(tiles):
        src = row_form(src_ref, t * per, per)
        dst = row_form(dst_ref, t * per, per)
        gm = mm_tn(hot_rows(dst, TILE), dagg[t * TILE : (t + 1) * TILE, :])
        dz = (gm * deriv[t * edges : (t + 1) * edges, :]).astype(bf)
        dz_ref[t * edges : (t + 1) * edges, :] = dz
        part = mm(hot_rows(src, coarse + proj.shape[0]), dz)
        total = part if total is None else total + part
    own_ref[...] = total[:coarse].astype(bf)
    back_ref[...] = total[coarse:].astype(bf)


def by_core(core_ref, mine_ref, other_ref, half0, half1):
    core = core_ref[0]

    def write(ref, half):
        at = 0
        for piece in half:
            ref[at : at + piece.shape[0], :] = piece
            at += piece.shape[0]

    @pl.when(core == 0)
    def _():
        write(mine_ref, half0)
        write(other_ref, half1)

    @pl.when(core != 0)
    def _():
        write(mine_ref, half1)
        write(other_ref, half0)


def coarse_grad_kernel(
    per, pooled_ref, in_ref, ghc_ref, w_ref, dst_ref, own_ref, back_ref, dz_ref, du_ref, agg_ref,
    gw_ref, gb_ref, part_ref,
):
    pooled = pooled_ref[...]
    coarse, width = pooled.shape
    edges = per * LANES
    dqs = []
    gb = jnp.zeros((1, width), f32)
    for t in range(coarse // TILE):
        dst = row_form(dst_ref, t * per, per)
        dq = mm(hot_rows(dst, TILE), dz_ref[t * edges : (t + 1) * edges, :])
        gb = gb + jnp.sum(dq, axis=0, keepdims=True)
        dqs.append(dq.astype(bf))
    dq = jnp.concatenate(dqs, axis=0)
    du = du_ref[...]
    gb_ref[...] = jnp.broadcast_to(gb, gb_ref.shape)
    gw_ref[0:width, :] = (mm_tn(pooled, own_ref[...]) + mm_tn(in_ref[...], back_ref[...])).astype(bf)
    gw_ref[width : 2 * width, :] = mm_tn(pooled, dq).astype(bf)
    gw_ref[2 * width : 3 * width, :] = mm_tn(agg_ref[...], du).astype(bf)
    gw_ref[3 * width : 4 * width, :] = mm_tn(pooled, du).astype(bf)
    part_ref[...] = ghc_ref[...] + mm_nt(du, w_ref[3]) + mm_nt(dq, w_ref[1])


def fine_back_kernel(
    per, group, core_ref, own_ref, ret_ref, send_ref, part_ref, wc_ref, count_ref, pool_ref,
    cot_ref, dsu_ref, w_ref, d_ref, he_ref, dst_ref, gwc_ref, gbc_ref, h_hbm, agg_hbm,
    dz_ref, dq_ref, du_ref, dcs_ref, mine_ref, other_ref, gb, gw0, dagg, h_ref, agg_ref, sems,
):
    step = pl.program_id(0)
    width = h_ref.shape[1]
    edges = per * LANES
    copies = [
        pltpu.make_async_copy(h_hbm, h_ref, sems.at[0]),
        pltpu.make_async_copy(agg_hbm, agg_ref, sems.at[1]),
    ]

    @pl.when(step == 0)
    def _():
        for copy in copies:
            copy.start()
        gb[...] = jnp.zeros_like(gb)
        gw0[...] = jnp.zeros_like(gw0)
        coarse = own_ref.shape[0]
        sends = hot_rows(row_form(send_ref, 0, send_ref.shape[0]), coarse)
        dp = (own_ref[...].astype(f32) + mm(sends, ret_ref[...])).astype(bf)
        dc = part_ref[...] + mm_nt(dp, wc_ref[0])
        count = count_ref[...]
        dcs = (dc / jnp.concatenate([count, count], axis=1)).astype(bf)
        dcs_ref[...] = dcs
        hot = hot_rows(row_form(pool_ref, 0, pool_ref.shape[0]), coarse)
        g = cot_ref[...].astype(f32) + mm_tn(hot, dcs)
        du = (g * dsu_ref[...].astype(f32)).astype(bf)
        du_ref[...] = du
        dagg[...] = mm_nt(du, w_ref[0]).astype(bf)

    def tile(k, slot):
        t = step * group + k
        hot = hot_rows(row_form(dst_ref, t * per, per), TILE)
        rows = tile_rows(t, TILE)
        here = tile_rows(k, edges)
        gm = mm_tn(hot, dagg[rows, :])
        dz = (gm * d_ref[here, :].astype(f32)).astype(bf)
        dz_ref[here, :] = dz
        dq = mm(hot, dz)
        gb[...] += jnp.sum(dq, axis=0, keepdims=True)
        dq_ref[rows, :] = dq.astype(bf)

    tile_loop(group, EDGE_UNROLL, tile)
    gw0[...] += mm_tn(he_ref[...], dz_ref[...])

    @pl.when(step == pl.num_programs(0) - 1)
    def _():
        for copy in copies:
            copy.wait()
        gbf = jnp.broadcast_to(gb[0:1, :], (16, width)).astype(bf)
        gbc = jnp.broadcast_to(gbc_ref[0:1, :], (16, width)).astype(bf)
        h = h_ref[...]
        gw1 = mm_tn(h, dq_ref[...]).astype(bf)
        gw2 = mm_tn(agg_ref[...], du_ref[...]).astype(bf)
        gw3 = mm_tn(h, du_ref[...]).astype(bf)
        half0 = [gwc_ref[0 : 2 * width, :], gw0[...].astype(bf), gw1] + [gbf] * 4
        half1 = [gwc_ref[2 * width : 4 * width, :], gw2, gw3] + [gbc] * 4
        by_core(core_ref, mine_ref, other_ref, half0, half1)


def scatter_kernel(per, group, src_ref, dz_ref, own_ref, gl_ref, gr_ref, dzs, *accs):
    step = pl.program_id(0)
    nodes = own_ref.shape[0]
    halo = gl_ref.shape[0]
    edges = per * LANES

    @pl.when(step == 0)
    def _():
        for acc in accs:
            acc[...] = jnp.zeros_like(acc)

    def tile(k, slot):
        t = step * group + k
        to_pairs(dzs, 0, dz_ref[tile_rows(k, edges), :].astype(f32))
        for e in range(edges):
            acc = accs[e % len(accs)]
            at = pair(src_ref[t * edges + e])
            acc[at, :] = acc[at, :] + dzs[2 * e : 2 * e + 2, :]

    tile_loop(group, 1, tile)

    @pl.when(step == pl.num_programs(0) - 1)
    def _():
        def summed(first, n):
            total = from_pairs(accs[0], first, n)
            for acc in accs[1:]:
                total = total + from_pairs(acc, first, n)
            return total.astype(bf)

        own_ref[...] = summed(0, nodes)
        gl_ref[...] = summed(nodes, halo)
        gr_ref[...] = summed(nodes + halo, halo)


def part_kernel(dq_ref, du_ref, cot_ref, dcs_ref, pool_ref, w3_ref, w1_ref, part_ref):
    hot = hot_rows(row_form(pool_ref, 0, pool_ref.shape[0]), dcs_ref.shape[0])
    part_ref[...] = (
        cot_ref[...].astype(f32)
        + mm_tn(hot, dcs_ref[...])
        + mm_nt(du_ref[...], w3_ref[0])
        + mm_nt(dq_ref[...], w1_ref[0])
    )


def input_kernel(own_ref, from_right_ref, from_left_ref, right_ref, left_ref, part_ref, w_ref, o_ref):
    nodes = own_ref.shape[0]
    n = right_ref.shape[0]
    add = mm(hot_rows(row_form(right_ref, 0, n), nodes), from_right_ref[...]) + mm(
        hot_rows(row_form(left_ref, 0, n), nodes), from_left_ref[...]
    )
    dp = (own_ref[...].astype(f32) + add).astype(bf)
    o_ref[...] = part_ref[...] + mm_nt(dp, w_ref[0])


def finish_kernel(scale, core_ref, a_ref, ax_ref, gf_ref, gc_ref, gb_ref):
    two = gf_ref.shape[0] // 2

    def write(half, src):
        rows = slice(half * two, (half + 1) * two)
        gc_ref[rows, :] = src[0:two, :].astype(f32) * scale
        gf_ref[rows, :] = src[two : 2 * two, :].astype(f32) * scale
        gb_ref[half : half + 1, :] = src[2 * two : 2 * two + 16, :].astype(f32)[0:1] * scale

    core = core_ref[0]

    @pl.when(core == 0)
    def _():
        write(0, a_ref)
        write(1, ax_ref)

    @pl.when(core != 0)
    def _():
        write(1, a_ref)
        write(0, ax_ref)


def shifted(block, axis, distance):
    devices = range(lax.axis_size(axis))
    route = [(i - distance, i) for i in devices if i - distance in devices]
    return lax.ppermute(block, axis, route)


def swapped(block, parts, bit):
    return lax.ppermute(block, "dom", [(i, i ^ bit) for i in range(parts)])


def exchange(block, parts):
    rows, width = block.shape
    got = lax.all_to_all(
        block.reshape(parts, rows // parts, width), "dom", split_axis=0, concat_axis=0, tiled=True
    )
    return got


def add(a, b):
    return (a.astype(f32) + b.astype(f32)).astype(bf)


def over_chips(blocks, groups):
    return lax.all_to_all(blocks, "dom", 0, 0, axis_index_groups=groups, tiled=True)


def shards(
    features, cotangent, w_fine, w_coarse, bias, fine_src, fine_dst, send_left, send_right,
    pool_map, coarse_src, coarse_dst, coarse_send,
):
    nodes, width = features.shape
    parts = lax.axis_size("dom")
    coarse = nodes // 4
    tiles = nodes // TILE
    halo = send_left.shape[0]
    per = fine_src.shape[0] // tiles // LANES
    edges = per * LANES
    fsrc, fdst = fine_src.reshape(-1, LANES), fine_dst.reshape(-1, LANES)
    csrc, cdst = coarse_src.reshape(-1, LANES), coarse_dst.reshape(-1, LANES)
    right, left = send_right.reshape(-1, LANES), send_left.reshape(-1, LANES)
    pool = pool_map.reshape(-1, LANES)
    csend = coarse_send.reshape(-1, LANES)
    crows = coarse_send.shape[0] * coarse_send.shape[1]
    part = functools.partial
    core = (lax.axis_index("dom") % 2).astype(jnp.int32).reshape(1)
    same_core = [list(range(c, parts, 2)) for c in range(2)]
    chips = parts // 2
    group = 4
    steps = tiles // group

    to_right, to_left = call(
        halo_kernel, [sds((halo, width), bf)] * 2, [features, right, left],
        us=0.8, near_out=(0, 1),
    )
    h_left = shifted(to_right, "dom", 1)
    h_right = shifted(to_left, "dom", -1)
    edge_tile = pl.BlockSpec((group * edges, width), lambda t: (t, 0))
    smem = pl.BlockSpec(memory_space=pltpu.SMEM)

    def weight(k):
        return pl.BlockSpec((1, width, width), lambda *_: (k, 0, 0))

    ext_pairs = 2 * (nodes + 2 * halo)
    d_edge, he, agg, dsu, pooled, outgoing, count = call(
        part(fine_kernel, per, group),
        [
            sds((tiles * edges, width), bf),
            sds((tiles * edges, width), bf),
            sds((nodes, width), bf),
            sds((nodes, width), bf),
            sds((coarse, width), bf),
            sds((crows, width), bf),
            sds((coarse, LANES), f32),
        ],
        [fine_src, h_left, h_right, features, w_fine, bias, fdst, pool, csend],
        grid=(steps,),
        specs={0: smem},
        out_specs={0: edge_tile, 1: edge_tile},
        scratch=[
            pltpu.VMEM((nodes, width), bf),
            pltpu.VMEM((ext_pairs, LANES), f32),
            pltpu.VMEM((2 * FINE_UNROLL * edges, LANES), f32),
        ],
        us=18, near=(1, 2), near_out=(5,),
    )
    incoming = exchange(outgoing, parts).reshape(crows, width)
    cedges = coarse_src.shape[0]
    zc, ghc, uc = call(
        part(coarse_own_kernel, per),
        [sds((cedges, width), f32), sds((coarse, width), f32), sds((coarse, width), f32)],
        [pooled, w_coarse, bias, csrc, cdst, pool, cotangent],
        us=2, near_out=(1, 2),
    )
    own_c, back_c, dz_c, du_c, agg_c = call(
        part(coarse_kernel, per),
        [
            sds((coarse, width), bf),
            sds((crows, width), bf),
            sds((cedges, width), bf),
            sds((coarse, width), bf),
            sds((coarse, width), bf),
        ],
        [zc, incoming, ghc, uc, w_coarse, csrc, cdst],
        scratch=[pltpu.VMEM((cedges, width), f32)],
        us=4.7, near=(1, 2, 3), near_out=(1,),
    )
    returned = exchange(back_c, parts).reshape(crows, width)
    gw_c, gb_c, part_c = call(
        part(coarse_grad_kernel, per),
        [sds((4 * width, width), bf), sds((8, width), f32), sds((coarse, width), f32)],
        [pooled, incoming, ghc, w_coarse, cdst, own_c, back_c, dz_c, du_c, agg_c],
        us=1, near=(1, 2), near_out=(1,),
    )
    half_rows = 4 * width + 64
    dz, dq, du, dcs, mine, other = call(
        part(fine_back_kernel, per, group),
        [
            sds((tiles * edges, width), bf),
            sds((nodes, width), bf),
            sds((nodes, width), bf),
            sds((coarse, width), bf),
            sds((half_rows, width), bf),
            sds((half_rows, width), bf),
        ],
        [
            core, own_c, returned, csend, part_c, w_coarse, count, pool, cotangent, dsu, w_fine,
            d_edge, he, fdst, gw_c, gb_c, features, agg,
        ],
        grid=(steps,),
        specs={
            0: smem, 5: weight(0), 10: weight(2), 11: edge_tile, 12: edge_tile,
            16: pl.BlockSpec(memory_space=pltpu.HBM), 17: pl.BlockSpec(memory_space=pltpu.HBM),
        },
        out_specs={0: edge_tile},
        scratch=[
            pltpu.VMEM((8, width), f32),
            pltpu.VMEM((width, width), f32),
            pltpu.VMEM((nodes, width), bf),
            pltpu.VMEM((nodes, width), bf),
            pltpu.VMEM((nodes, width), bf),
            pltpu.SemaphoreType.DMA((2,)),
        ],
        us=10, near=(2, 8, 9), near_out=(4, 5),
    )
    sums = add(mine, swapped(other, parts, 1)).reshape(chips, -1, width)
    sums, dz = lax.optimization_barrier((sums, dz))
    sums = over_chips(sums, same_core)
    own_f, gl, gr = call(
        part(scatter_kernel, per, group),
        [sds((nodes, width), bf), sds((halo, width), bf), sds((halo, width), bf)],
        [fine_src, dz],
        grid=(steps,),
        specs={0: smem, 1: edge_tile},
        scratch=[pltpu.VMEM((2 * edges, LANES), f32)]
        + [pltpu.VMEM((ext_pairs, LANES), f32)] * 6,
        us=12, near_out=(1, 2),
    )
    sums, own_f, gl, gr = lax.optimization_barrier((sums, own_f, gl, gr))
    sums = jnp.sum(sums.astype(f32), axis=0).astype(bf)
    sums = over_chips(jnp.broadcast_to(sums[None], (chips,) + sums.shape), same_core)
    from_right = shifted(gl, "dom", -1)
    from_left = shifted(gr, "dom", 1)
    (part_f,) = call(
        part_kernel,
        [sds((nodes, width), f32)],
        [dq, du, cotangent, dcs, pool, w_fine, w_fine],
        specs={5: weight(3), 6: weight(1)},
        us=1.5, near_out=(0,),
    )
    (grad_input,) = call(
        input_kernel,
        [sds((nodes, width), f32)],
        [own_f, from_right, from_left, right, left, part_f, w_fine],
        specs={6: weight(0)},
        us=2.4, near=(1, 2, 5), near_out=(0,),
    )
    sums, grad_input = lax.optimization_barrier((sums, grad_input))
    sums = sums.reshape(half_rows, width)
    scale = 1.0 / float(nodes * parts // 256)
    grad_fine, grad_coarse, grad_bias = call(
        part(finish_kernel, scale),
        [sds((4 * width, width), f32), sds((4 * width, width), f32), sds((2, width), f32)],
        [core, sums, swapped(sums, parts, 1)],
        specs={0: smem},
        us=1.5, near=(1, 2), near_out=(0, 1, 2),
    )
    shape = (4, width, width)
    return (grad_input, grad_fine.reshape(shape), grad_coarse.reshape(shape), grad_bias)


def solution(mesh):
    return jax.shard_map(
        shards,
        mesh=mesh,
        in_specs=(
            P(("groups", "dom"), None),
            P(("groups", "dom"), None),
            P(),
            P(),
            P(),
            P("dom"),
            P("dom"),
            P("dom"),
            P("dom"),
            P("dom"),
            P("dom"),
            P("dom"),
            P("dom", None),
        ),
        out_specs=(
            P(("groups", "dom"), None),
            P("groups", None, None),
            P("groups", None, None),
            P("groups", None),
        ),
        check_vma=False,
    )
```

```python
import functools

import jax
import jax.numpy as jnp
from jax import lax
from jax.experimental import pallas as pl
from jax.experimental.pallas import tpu as pltpu
from jax.sharding import PartitionSpec as P

bf = jnp.bfloat16
f32 = jnp.float32
TILE = 128
LANES = 128
FINE_UNROLL = 4
EDGE_UNROLL = 4


def mm(a, b):
    return jnp.dot(a, b, preferred_element_type=f32)


def mm_tn(a, b):
    return lax.dot_general(a, b, (((0,), (0,)), ((), ())), preferred_element_type=f32)


def mm_nt(a, b):
    return lax.dot_general(a, b, (((1,), (1,)), ((), ())), preferred_element_type=f32)


def as_bf(x):
    return x.astype(f32).astype(bf)


def row_form(ref, first, count):
    return jnp.concatenate([ref[pl.ds(first + j, 1), :] for j in range(count)], axis=1)


def hot_rows(row, rows):
    cols = row.shape[1]
    if rows <= 256:
        io = as_bf(lax.broadcasted_iota(jnp.int32, (rows, cols), 0))
        return jnp.where(io == as_bf(row), bf(1), bf(0))
    low = as_bf(row & 255)
    high = as_bf(lax.shift_right_arithmetic(row, 8))
    io = as_bf(lax.broadcasted_iota(jnp.int32, (256, cols), 0))
    base = jnp.where(io == low, bf(1), bf(0))
    return jnp.concatenate(
        [jnp.where(high == bf(k), base, bf(0)) for k in range(rows // 256)], axis=0
    )


def tile_loop(group, unroll, body):
    if group == unroll:
        for k in range(group):
            body(k, k)
    else:

        def step(j, carry):
            for k in range(unroll):
                body(j * unroll + k, k)
            return carry

        lax.fori_loop(0, group // unroll, step, 0)


def tile_rows(index, size):
    return pl.ds(pl.multiple_of(index * size, size), size)


def silu_parts(v):
    sig = 0.5 * jnp.tanh(0.5 * v) + 0.5
    silu = v * sig
    return silu, sig + silu * (1.0 - sig)


def to_pairs(ref, first, rows):
    n = rows.shape[0]
    for j in range(2):
        ref[pl.ds(2 * first + j, n, stride=2), :] = rows[:, j * LANES : (j + 1) * LANES]


def from_pairs(ref, first, n):
    return jnp.concatenate([ref[pl.ds(2 * first + j, n, stride=2), :] for j in range(2)], axis=1)


def pair(index):
    return pl.ds(pl.multiple_of(index * 2, 2), 2)


def call(kernel, outs, args, grid=(), specs=None, out_specs=None, scratch=(), us=1.0, near=(), near_out=()):
    specs = specs or {}
    args = [
        a
        if k in near or getattr(specs.get(k), "memory_space", None) == pltpu.SMEM
        else pltpu.with_memory_space_constraint(a, pltpu.HBM)
        for k, a in enumerate(args)
    ]
    def whole(a):
        return pl.BlockSpec(a.shape, lambda *_: (0,) * len(a.shape))

    in_specs = [whole(a) for a in args]
    o_specs = [whole(o) for o in outs]
    for k, s in specs.items():
        in_specs[k] = s
    for k, s in (out_specs or {}).items():
        o_specs[k] = s
    return pl.pallas_call(
        kernel,
        grid=grid or (1,),
        in_specs=in_specs,
        out_specs=o_specs,
        out_shape=[o if k in near_out else pltpu.HBM(o.shape, o.dtype) for k, o in enumerate(outs)],
        scratch_shapes=list(scratch),
        compiler_params=pltpu.CompilerParams(vmem_limit_bytes=32 << 20),
        cost_estimate=pl.CostEstimate(
            flops=int(us * 1e9), bytes_accessed=1 << 20, transcendentals=0
        ),
    )(*args)


def sds(shape, dtype):
    return jax.ShapeDtypeStruct(shape, dtype)


def halo_kernel(h_ref, right_ref, left_ref, to_right_ref, to_left_ref):
    h = h_ref[...]
    n = right_ref.shape[0]
    to_right_ref[...] = mm_tn(hot_rows(row_form(right_ref, 0, n), h.shape[0]), h).astype(bf)
    to_left_ref[...] = mm_tn(hot_rows(row_form(left_ref, 0, n), h.shape[0]), h).astype(bf)


def fine_kernel(
    per, group, src_ref, left_ref, right_ref, h_ref, w_ref, b_ref, dst_ref, pool_ref, send_ref,
    d_ref, he_ref, agg_ref, dsu_ref, pooled_ref, out_ref, count_ref, recv, table, taken,
):
    step = pl.program_id(0)
    nodes = h_ref.shape[0]
    halo = left_ref.shape[0]
    edges = per * LANES

    @pl.when(step == 0)
    def _():
        recv[...] = mm(h_ref[...], w_ref[1]).astype(bf)
        to_pairs(table, 0, h_ref[...].astype(f32))
        to_pairs(table, nodes, left_ref[...].astype(f32))
        to_pairs(table, nodes + halo, right_ref[...].astype(f32))

    def tile(k, slot):
        t = step * group + k
        for e in range(edges):
            at = 2 * (slot * edges + e)
            taken[at : at + 2, :] = table[pair(src_ref[t * edges + e]), :]
        rows = tile_rows(t, TILE)
        hot = hot_rows(row_form(dst_ref, t * per, per), TILE)
        he = from_pairs(taken, slot * edges, edges).astype(bf)
        he_ref[tile_rows(k, edges), :] = he
        sent = as_bf(mm(he, w_ref[0])).astype(f32)
        z = sent + mm_tn(hot, recv[rows, :]) + b_ref[0:1, :]
        m, d = silu_parts(z)
        d_ref[tile_rows(k, edges), :] = d.astype(bf)
        agg_ref[rows, :] = mm(hot, m.astype(bf)).astype(bf)

    tile_loop(group, FINE_UNROLL, tile)

    @pl.when(step == pl.num_programs(0) - 1)
    def _():
        h = h_ref[...]
        u = mm(h, w_ref[3]) + mm(agg_ref[...], w_ref[2])
        su, dsu = silu_parts(u)
        dsu_ref[...] = dsu.astype(bf)
        h1 = (h.astype(f32) + su).astype(bf)
        coarse = pooled_ref.shape[0]
        hot = hot_rows(row_form(pool_ref, 0, pool_ref.shape[0]), coarse)
        count = mm(hot, jnp.ones((nodes, LANES), bf))
        count_ref[...] = count
        pooled = (mm(hot, h1) / jnp.concatenate([count, count], axis=1)).astype(bf)
        pooled_ref[...] = pooled
        sends = hot_rows(row_form(send_ref, 0, send_ref.shape[0]), coarse)
        out_ref[...] = mm_tn(sends, pooled).astype(bf)


def coarse_own_kernel(
    per, pooled_ref, w_ref, b_ref, src_ref, dst_ref, pool_ref, cot_ref, z_ref, ghc_ref, u_ref
):
    pooled = pooled_ref[...]
    coarse = pooled.shape[0]
    proj = mm(pooled, w_ref[0]).astype(bf)
    recv = mm(pooled, w_ref[1]).astype(bf)
    u_ref[...] = mm(pooled, w_ref[3])
    edges = per * LANES
    for t in range(coarse // TILE):
        src = row_form(src_ref, t * per, per)
        dst = row_form(dst_ref, t * per, per)
        z_ref[t * edges : (t + 1) * edges, :] = (
            mm_tn(hot_rows(src, coarse), proj)
            + mm_tn(hot_rows(dst, TILE), recv[t * TILE : (t + 1) * TILE, :])
            + b_ref[1:2, :]
        )
    hot = hot_rows(row_form(pool_ref, 0, pool_ref.shape[0]), coarse)
    ghc_ref[...] = mm(hot, cot_ref[...])


def coarse_kernel(
    per, z_ref, in_ref, ghc_ref, u_ref, w_ref, src_ref, dst_ref,
    own_ref, back_ref, dz_ref, du_ref, agg_ref, deriv,
):
    coarse = ghc_ref.shape[0]
    edges = per * LANES
    tiles = coarse // TILE
    proj = mm(in_ref[...], w_ref[0]).astype(bf)
    for t in range(tiles):
        src = row_form(src_ref, t * per, per) - coarse
        dst = row_form(dst_ref, t * per, per)
        z = z_ref[t * edges : (t + 1) * edges, :] + mm_tn(hot_rows(src, proj.shape[0]), proj)
        m, d = silu_parts(z)
        deriv[t * edges : (t + 1) * edges, :] = d
        agg_ref[t * TILE : (t + 1) * TILE, :] = mm(hot_rows(dst, TILE), m.astype(bf)).astype(bf)
    u = u_ref[...] + mm(agg_ref[...], w_ref[2])
    _, dsu = silu_parts(u)
    du = (ghc_ref[...] * dsu).astype(bf)
    du_ref[...] = du
    dagg = mm_nt(du, w_ref[2]).astype(bf)
    total = None
    for t in range(tiles):
        src = row_form(src_ref, t * per, per)
        dst = row_form(dst_ref, t * per, per)
        gm = mm_tn(hot_rows(dst, TILE), dagg[t * TILE : (t + 1) * TILE, :])
        dz = (gm * deriv[t * edges : (t + 1) * edges, :]).astype(bf)
        dz_ref[t * edges : (t + 1) * edges, :] = dz
        part = mm(hot_rows(src, coarse + proj.shape[0]), dz)
        total = part if total is None else total + part
    own_ref[...] = total[:coarse].astype(bf)
    back_ref[...] = total[coarse:].astype(bf)


def by_core(core_ref, mine_ref, other_ref, half0, half1):
    core = core_ref[0]

    def write(ref, half):
        at = 0
        for piece in half:
            ref[at : at + piece.shape[0], :] = piece
            at += piece.shape[0]

    @pl.when(core == 0)
    def _():
        write(mine_ref, half0)
        write(other_ref, half1)

    @pl.when(core != 0)
    def _():
        write(mine_ref, half1)
        write(other_ref, half0)


def coarse_grad_kernel(
    per, pooled_ref, in_ref, ghc_ref, w_ref, dst_ref, own_ref, back_ref, dz_ref, du_ref, agg_ref,
    gw_ref, gb_ref, part_ref,
):
    pooled = pooled_ref[...]
    coarse, width = pooled.shape
    edges = per * LANES
    dqs = []
    gb = jnp.zeros((1, width), f32)
    for t in range(coarse // TILE):
        dst = row_form(dst_ref, t * per, per)
        dq = mm(hot_rows(dst, TILE), dz_ref[t * edges : (t + 1) * edges, :])
        gb = gb + jnp.sum(dq, axis=0, keepdims=True)
        dqs.append(dq.astype(bf))
    dq = jnp.concatenate(dqs, axis=0)
    du = du_ref[...]
    gb_ref[...] = jnp.broadcast_to(gb, gb_ref.shape)
    gw_ref[0:width, :] = (mm_tn(pooled, own_ref[...]) + mm_tn(in_ref[...], back_ref[...])).astype(bf)
    gw_ref[width : 2 * width, :] = mm_tn(pooled, dq).astype(bf)
    gw_ref[2 * width : 3 * width, :] = mm_tn(agg_ref[...], du).astype(bf)
    gw_ref[3 * width : 4 * width, :] = mm_tn(pooled, du).astype(bf)
    part_ref[...] = ghc_ref[...] + mm_nt(du, w_ref[3]) + mm_nt(dq, w_ref[1])


def fine_back_kernel(
    per, group, core_ref, own_ref, ret_ref, send_ref, part_ref, wc_ref, count_ref, pool_ref,
    cot_ref, dsu_ref, w_ref, d_ref, he_ref, dst_ref, gwc_hbm, gbc_ref, h_hbm, agg_hbm,
    dz_ref, dq_ref, du_ref, dcs_ref, mine_ref, other_ref, gb, gw0, dagg, h_ref, agg_ref, gwc_ref, sems,
):
    step = pl.program_id(0)
    width = h_ref.shape[1]
    edges = per * LANES
    copies = [
        pltpu.make_async_copy(h_hbm, h_ref, sems.at[0]),
        pltpu.make_async_copy(agg_hbm, agg_ref, sems.at[1]),
        pltpu.make_async_copy(gwc_hbm, gwc_ref, sems.at[2]),
    ]

    @pl.when(step == 0)
    def _():
        for copy in copies:
            copy.start()
        gb[...] = jnp.zeros_like(gb)
        gw0[...] = jnp.zeros_like(gw0)
        coarse = own_ref.shape[0]
        sends = hot_rows(row_form(send_ref, 0, send_ref.shape[0]), coarse)
        dp = (own_ref[...].astype(f32) + mm(sends, ret_ref[...])).astype(bf)
        dc = part_ref[...] + mm_nt(dp, wc_ref[0])
        count = count_ref[...]
        dcs = (dc / jnp.concatenate([count, count], axis=1)).astype(bf)
        dcs_ref[...] = dcs
        hot = hot_rows(row_form(pool_ref, 0, pool_ref.shape[0]), coarse)
        g = cot_ref[...].astype(f32) + mm_tn(hot, dcs)
        du = (g * dsu_ref[...].astype(f32)).astype(bf)
        du_ref[...] = du
        dagg[...] = mm_nt(du, w_ref[0]).astype(bf)

    def tile(k, slot):
        t = step * group + k
        hot = hot_rows(row_form(dst_ref, t * per, per), TILE)
        rows = tile_rows(t, TILE)
        here = tile_rows(k, edges)
        gm = mm_tn(hot, dagg[rows, :])
        dz = (gm * d_ref[here, :].astype(f32)).astype(bf)
        dz_ref[here, :] = dz
        dq = mm(hot, dz)
        gb[...] += jnp.sum(dq, axis=0, keepdims=True)
        dq_ref[rows, :] = dq.astype(bf)

    tile_loop(group, EDGE_UNROLL, tile)
    gw0[...] += mm_tn(he_ref[...], dz_ref[...])

    @pl.when(step == pl.num_programs(0) - 1)
    def _():
        for copy in copies:
            copy.wait()
        gbf = jnp.broadcast_to(gb[0:1, :], (16, width)).astype(bf)
        gbc = jnp.broadcast_to(gbc_ref[0:1, :], (16, width)).astype(bf)
        h = h_ref[...]
        gw1 = mm_tn(h, dq_ref[...]).astype(bf)
        gw2 = mm_tn(agg_ref[...], du_ref[...]).astype(bf)
        gw3 = mm_tn(h, du_ref[...]).astype(bf)
        half0 = [gwc_ref[0 : 2 * width, :], gw0[...].astype(bf), gw1] + [gbf] * 4
        half1 = [gwc_ref[2 * width : 4 * width, :], gw2, gw3] + [gbc] * 4
        by_core(core_ref, mine_ref, other_ref, half0, half1)


def scatter_kernel(per, group, src_ref, dz_ref, own_ref, gl_ref, gr_ref, dzs, *accs):
    step = pl.program_id(0)
    nodes = own_ref.shape[0]
    halo = gl_ref.shape[0]
    edges = per * LANES

    @pl.when(step == 0)
    def _():
        for acc in accs:
            acc[...] = jnp.zeros_like(acc)

    def tile(k, slot):
        t = step * group + k
        to_pairs(dzs, 0, dz_ref[tile_rows(k, edges), :].astype(f32))
        for e in range(edges):
            acc = accs[e % len(accs)]
            at = pair(src_ref[t * edges + e])
            acc[at, :] = acc[at, :] + dzs[2 * e : 2 * e + 2, :]

    tile_loop(group, 1, tile)

    @pl.when(step == pl.num_programs(0) - 1)
    def _():
        def summed(first, n):
            total = from_pairs(accs[0], first, n)
            for acc in accs[1:]:
                total = total + from_pairs(acc, first, n)
            return total.astype(bf)

        own_ref[...] = summed(0, nodes)
        gl_ref[...] = summed(nodes, halo)
        gr_ref[...] = summed(nodes + halo, halo)


def part_kernel(dq_ref, du_ref, cot_ref, dcs_ref, pool_ref, w3_ref, w1_ref, part_ref):
    hot = hot_rows(row_form(pool_ref, 0, pool_ref.shape[0]), dcs_ref.shape[0])
    part_ref[...] = (
        cot_ref[...].astype(f32)
        + mm_tn(hot, dcs_ref[...])
        + mm_nt(du_ref[...], w3_ref[0])
        + mm_nt(dq_ref[...], w1_ref[0])
    )


def input_kernel(own_ref, from_right_ref, from_left_ref, right_ref, left_ref, part_ref, w_ref, o_ref):
    nodes = own_ref.shape[0]
    n = right_ref.shape[0]
    add = mm(hot_rows(row_form(right_ref, 0, n), nodes), from_right_ref[...]) + mm(
        hot_rows(row_form(left_ref, 0, n), nodes), from_left_ref[...]
    )
    dp = (own_ref[...].astype(f32) + add).astype(bf)
    o_ref[...] = part_ref[...] + mm_nt(dp, w_ref[0])


def finish_kernel(scale, core_ref, a_ref, ax_ref, gf_ref, gc_ref, gb_ref):
    two = gf_ref.shape[0] // 2

    def write(half, src):
        rows = slice(half * two, (half + 1) * two)
        gc_ref[rows, :] = src[0:two, :].astype(f32) * scale
        gf_ref[rows, :] = src[two : 2 * two, :].astype(f32) * scale
        gb_ref[half : half + 1, :] = src[2 * two : 2 * two + 16, :].astype(f32)[0:1] * scale

    core = core_ref[0]

    @pl.when(core == 0)
    def _():
        write(0, a_ref)
        write(1, ax_ref)

    @pl.when(core != 0)
    def _():
        write(1, a_ref)
        write(0, ax_ref)


def shifted(block, axis, distance):
    devices = range(lax.axis_size(axis))
    route = [(i - distance, i) for i in devices if i - distance in devices]
    return lax.ppermute(block, axis, route)


def swapped(block, parts, bit):
    return lax.ppermute(block, "dom", [(i, i ^ bit) for i in range(parts)])


def exchange(block, parts):
    rows, width = block.shape
    got = lax.all_to_all(
        block.reshape(parts, rows // parts, width), "dom", split_axis=0, concat_axis=0, tiled=True
    )
    return got


def add(a, b):
    return (a.astype(f32) + b.astype(f32)).astype(bf)


def over_chips(blocks, groups):
    return lax.all_to_all(blocks, "dom", 0, 0, axis_index_groups=groups, tiled=True)


def shards(
    features, cotangent, w_fine, w_coarse, bias, fine_src, fine_dst, send_left, send_right,
    pool_map, coarse_src, coarse_dst, coarse_send,
):
    nodes, width = features.shape
    parts = lax.axis_size("dom")
    coarse = nodes // 4
    tiles = nodes // TILE
    halo = send_left.shape[0]
    per = fine_src.shape[0] // tiles // LANES
    edges = per * LANES
    fsrc, fdst = fine_src.reshape(-1, LANES), fine_dst.reshape(-1, LANES)
    csrc, cdst = coarse_src.reshape(-1, LANES), coarse_dst.reshape(-1, LANES)
    right, left = send_right.reshape(-1, LANES), send_left.reshape(-1, LANES)
    pool = pool_map.reshape(-1, LANES)
    csend = coarse_send.reshape(-1, LANES)
    crows = coarse_send.shape[0] * coarse_send.shape[1]
    part = functools.partial
    core = (lax.axis_index("dom") % 2).astype(jnp.int32).reshape(1)
    same_core = [list(range(c, parts, 2)) for c in range(2)]
    chips = parts // 2
    group = 4
    steps = tiles // group

    to_right, to_left = call(
        halo_kernel, [sds((halo, width), bf)] * 2, [features, right, left],
        us=0.8, near_out=(0, 1),
    )
    h_left = shifted(to_right, "dom", 1)
    h_right = shifted(to_left, "dom", -1)
    edge_tile = pl.BlockSpec((group * edges, width), lambda t: (t, 0))
    smem = pl.BlockSpec(memory_space=pltpu.SMEM)

    def weight(k):
        return pl.BlockSpec((1, width, width), lambda *_: (k, 0, 0))

    ext_pairs = 2 * (nodes + 2 * halo)
    d_edge, he, agg, dsu, pooled, outgoing, count = call(
        part(fine_kernel, per, group),
        [
            sds((tiles * edges, width), bf),
            sds((tiles * edges, width), bf),
            sds((nodes, width), bf),
            sds((nodes, width), bf),
            sds((coarse, width), bf),
            sds((crows, width), bf),
            sds((coarse, LANES), f32),
        ],
        [fine_src, h_left, h_right, features, w_fine, bias, fdst, pool, csend],
        grid=(steps,),
        specs={0: smem},
        out_specs={0: edge_tile, 1: edge_tile},
        scratch=[
            pltpu.VMEM((nodes, width), bf),
            pltpu.VMEM((ext_pairs, LANES), f32),
            pltpu.VMEM((2 * FINE_UNROLL * edges, LANES), f32),
        ],
        us=18, near=(1, 2), near_out=(5,),
    )
    incoming = exchange(outgoing, parts).reshape(crows, width)
    cedges = coarse_src.shape[0]
    zc, ghc, uc = call(
        part(coarse_own_kernel, per),
        [sds((cedges, width), f32), sds((coarse, width), f32), sds((coarse, width), f32)],
        [pooled, w_coarse, bias, csrc, cdst, pool, cotangent],
        us=2, near_out=(1, 2),
    )
    own_c, back_c, dz_c, du_c, agg_c = call(
        part(coarse_kernel, per),
        [
            sds((coarse, width), bf),
            sds((crows, width), bf),
            sds((cedges, width), bf),
            sds((coarse, width), bf),
            sds((coarse, width), bf),
        ],
        [zc, incoming, ghc, uc, w_coarse, csrc, cdst],
        scratch=[pltpu.VMEM((cedges, width), f32)],
        us=4.7, near=(1, 2, 3), near_out=(1,),
    )
    returned = exchange(back_c, parts).reshape(crows, width)
    gw_c, gb_c, part_c = call(
        part(coarse_grad_kernel, per),
        [sds((4 * width, width), bf), sds((8, width), f32), sds((coarse, width), f32)],
        [pooled, incoming, ghc, w_coarse, cdst, own_c, back_c, dz_c, du_c, agg_c],
        us=1, near=(1, 2), near_out=(1,),
    )
    half_rows = 4 * width + 64
    dz, dq, du, dcs, mine, other = call(
        part(fine_back_kernel, per, group),
        [
            sds((tiles * edges, width), bf),
            sds((nodes, width), bf),
            sds((nodes, width), bf),
            sds((coarse, width), bf),
            sds((half_rows, width), bf),
            sds((half_rows, width), bf),
        ],
        [
            core, own_c, returned, csend, part_c, w_coarse, count, pool, cotangent, dsu, w_fine,
            d_edge, he, fdst, gw_c, gb_c, features, agg,
        ],
        grid=(steps,),
        specs={
            0: smem, 5: weight(0), 10: weight(2), 11: edge_tile, 12: edge_tile,
            14: pl.BlockSpec(memory_space=pltpu.HBM),
            16: pl.BlockSpec(memory_space=pltpu.HBM), 17: pl.BlockSpec(memory_space=pltpu.HBM),
        },
        out_specs={0: edge_tile},
        scratch=[
            pltpu.VMEM((8, width), f32),
            pltpu.VMEM((width, width), f32),
            pltpu.VMEM((nodes, width), bf),
            pltpu.VMEM((nodes, width), bf),
            pltpu.VMEM((nodes, width), bf),
            pltpu.VMEM((4 * width, width), bf),
            pltpu.SemaphoreType.DMA((3,)),
        ],
        us=10, near=(2, 8, 9), near_out=(4, 5),
    )
    sums = add(mine, swapped(other, parts, 1)).reshape(chips, -1, width)
    sums, dz = lax.optimization_barrier((sums, dz))
    sums = over_chips(sums, same_core)
    own_f, gl, gr = call(
        part(scatter_kernel, per, group),
        [sds((nodes, width), bf), sds((halo, width), bf), sds((halo, width), bf)],
        [fine_src, dz],
        grid=(steps,),
        specs={0: smem, 1: edge_tile},
        scratch=[pltpu.VMEM((2 * edges, LANES), f32)]
        + [pltpu.VMEM((ext_pairs, LANES), f32)] * 6,
        us=12, near_out=(1, 2),
    )
    sums, own_f, gl, gr = lax.optimization_barrier((sums, own_f, gl, gr))
    sums = jnp.sum(sums.astype(f32), axis=0).astype(bf)
    sums = over_chips(jnp.broadcast_to(sums[None], (chips,) + sums.shape), same_core)
    from_right = shifted(gl, "dom", -1)
    from_left = shifted(gr, "dom", 1)
    (part_f,) = call(
        part_kernel,
        [sds((nodes, width), f32)],
        [dq, du, cotangent, dcs, pool, w_fine, w_fine],
        specs={5: weight(3), 6: weight(1)},
        us=1.5, near_out=(0,),
    )
    (grad_input,) = call(
        input_kernel,
        [sds((nodes, width), f32)],
        [own_f, from_right, from_left, right, left, part_f, w_fine],
        specs={6: weight(0)},
        us=2.4, near=(1, 2, 5), near_out=(0,),
    )
    sums, grad_input = lax.optimization_barrier((sums, grad_input))
    sums = sums.reshape(half_rows, width)
    scale = 1.0 / float(nodes * parts // 256)
    grad_fine, grad_coarse, grad_bias = call(
        part(finish_kernel, scale),
        [sds((4 * width, width), f32), sds((4 * width, width), f32), sds((2, width), f32)],
        [core, sums, swapped(sums, parts, 1)],
        specs={0: smem},
        us=1.5, near=(1, 2), near_out=(0, 1, 2),
    )
    shape = (4, width, width)
    return (grad_input, grad_fine.reshape(shape), grad_coarse.reshape(shape), grad_bias)


def solution(mesh):
    return jax.shard_map(
        shards,
        mesh=mesh,
        in_specs=(
            P(("groups", "dom"), None),
            P(("groups", "dom"), None),
            P(),
            P(),
            P(),
            P("dom"),
            P("dom"),
            P("dom"),
            P("dom"),
            P("dom"),
            P("dom"),
            P("dom"),
            P("dom", None),
        ),
        out_specs=(
            P(("groups", "dom"), None),
            P("groups", None, None),
            P("groups", None, None),
            P("groups", None),
        ),
        check_vma=False,
    )
```
